32 devices in a mesh: grp: 2 (over y), ccd: 4 (over z), row: 2 (over x), amp: 2 (over core).
Axes of the slice: x: 2, y: 2, z: 4, core: 2. Of those that a mesh axis runs over, the one named last changes fastest.
Arguments:
- science: float32 [8, 512, 1024], P(('grp', 'ccd'), 'row', 'amp'), parts along dimension 0, may hold values from -6 to 6
- template: bfloat16 [8, 2, 2, 8, 32, 512], P(('grp', 'ccd'), 'row', 'amp'), parts along dimension 0, may hold values from -6 to 6
- owners: int32 [8, 2, 2, 8, 1], P(('grp', 'ccd'), 'row', 'amp'), parts along dimension 0, may hold values from 0 to 3; in each aligned block of 8 rows (0 to 7, 8 to 15, ..., all dimensions but the last counted through in order) at most 2 rows name the same one
- patch_strip: int32 [8, 2, 2, 8], P(('grp', 'ccd'), 'row', 'amp'), parts along dimension 0, may hold values from 0 to 7
- shifts: int32 [8, 2, 2, 2, 8], P(('grp', 'ccd'), 'row', 'amp'), parts along dimension 0, may hold values from -3 to 3
- fractions: float32 [8, 2, 2, 2, 8], P(('grp', 'ccd'), 'row', 'amp'), parts along dimension 0, may hold values from 0.05 to 0.95
- coefs: float32 [8, 3, 9], P(('grp', 'ccd')), parts along dimension 0, may hold values from -3 to 3
Outputs:
- difference: float32 [8, 512, 1024], P(('grp', 'ccd'), 'row', 'amp'), parts along dimension 0
- stack: float32 [8, 2, 2, 8, 32, 512], P(('grp', 'ccd'), 'row', 'amp'), parts along dimension 0
The draws below stay inside these ranges and needn't reach their ends.
There are 2 independent parts, one for each index of `grp`. The reference program is written for one: setup_inputs(seed, part) draws one part's arguments, and reference() takes and returns one part's arrays. A program takes and returns all parts, laid end to end along the dimension named above; each array names one. Nothing has to cross between parts.
Inputs may be any that keep to these rules, and one draw needn't show every extreme that they name: Among the 8 strips of one device's block no owner is named more than 2 times, and some block names one owner exactly 2 times in every draw; owners lie in the same row band and column half as the block.
All inputs are finite; a program needn't handle non-finite values.
Results may differ from the reference program's by a relative error of at most 0.0057.
Values may be sent and summed in bfloat16 or wider, within the bound.
No kernel may reach another device: no remote copies, remote signals or barrier semaphores. Data moves between devices by JAX's collectives and lax.ppermute only.
A program may use at most 64 MiB of HBM per device.

```python
import math
import jax
import jax.numpy as jnp
import numpy as np
from jax import lax

BAND = 256
HALF = 512
STRIP_ROWS = 32
RADIUS = 9
CCDS = 4
BANDS = 2
HALVES = 2
STRIPS = 8
CAP = 2
IMG_ROWS = 512
IMG_COLS = 1024


def with_ends(array, key, smallest, largest):
    index_at = [jax.random.randint(jax.random.fold_in(key, axis), (), 0, length) for axis, length in enumerate(array.shape)]
    widest = array.shape.index(max(array.shape))
    neighbour = index_at[:widest] + [(index_at[widest] + 1) % array.shape[widest]] + index_at[widest + 1:]
    return array.at[tuple(index_at)].set(smallest).at[tuple(neighbour)].set(largest)


def levels(key, dims, shards, smallest, largest):
    gain = 1.0
    for axis_at, shards_of in shards:
        steps = jax.random.uniform(jax.random.fold_in(jax.random.fold_in(key, 6), axis_at), (shards_of,), jnp.float32, smallest / len(shards), largest / len(shards))
        gain = gain * jnp.repeat(jnp.exp(steps), dims[axis_at] // shards_of).reshape((-1,) + (1,) * (len(dims) - 1 - axis_at))
    return gain


def shared_out(own_key, own, number, rows, number_of, top, limit, lean):
    ranking = jax.random.permutation(own_key, number_of)
    packed, common = portions_of(number_of, rows * top, limit, lean, True), portions_of(number_of, rows * top, limit, lean, False)
    places = jnp.arange(number_of)

    def named(sizes, turn):
        used = int((sizes > 0).sum())
        fixed = max(1, used // 4)
        passed = fixed + (places - fixed + turn * (used - fixed)) % max(1, number_of - fixed)
        return jnp.zeros((number_of,), jnp.int32).at[ranking[jnp.where(places < fixed, places, passed)]].set(jnp.asarray(sizes, jnp.int32))

    sizes = jnp.where(number % 4 == 0, named(packed, number // 4), named(common, number - number // 4 - 1))
    mixed = jax.random.permutation(jax.random.fold_in(own, 3), number_of)
    donor, receiver = mixed[0:number_of // 2 * 2:2], mixed[1:number_of // 2 * 2:2]
    room = jnp.minimum(sizes[donor] - 1, limit - sizes[receiver]) // 2
    room = jnp.where((donor == ranking[0]) | (receiver == ranking[0]) | (sizes[receiver] == 0), 0, jnp.maximum(room, 0))
    passed = jax.random.randint(jax.random.fold_in(own, 4), (number_of // 2,), 0, 1 << 20) % (room + 1)
    sizes = sizes.at[donor].add(-passed).at[receiver].add(passed)
    members = jnp.searchsorted(jnp.cumsum(sizes), jnp.arange(rows * top), side="right").astype(jnp.int32)
    listing = members.reshape(top, rows).T
    listing = listing[jax.random.permutation(jax.random.fold_in(own, 1), rows)]
    turn = jax.random.randint(jax.random.fold_in(own, 2), (rows, 1), 0, top)
    return jnp.take_along_axis(listing, (jnp.arange(top)[None, :] + turn) % top, axis=1)


def portions_of(count, total, reach, skew, full):
    weights = [(1 << 20) // math.isqrt(rank ** skew) + 1 for rank in range(1, count + 1)]
    largest = reach if full else min(reach, max(-(-total // count), total * weights[0] // sum(weights)))
    least = 1 if total - largest >= count - 1 else 0
    given, spare = [largest] + [least] * (count - 1), total - largest - least * (count - 1)
    while spare > 0:
        movable = [i for i in range(1, count) if given[i] < largest] or [i for i in range(1, count) if given[i] < reach]
        pool, left = sum([weights[i] for i in movable]), spare
        for i in movable:
            addition = min(reach - given[i], max(1, left * weights[i] // pool), spare)
            given[i] = given[i] + addition
            spare = spare - addition
    return np.array(given)


def centred(own_key, extent, scale, bound, split=(), held_as=jnp.bfloat16):
    entries = scale * jax.random.normal(own_key, extent, jnp.float32)
    if split:
        entries = entries * levels(own_key, extent, split, -0.22, 0.18)
    return jnp.clip(entries, -bound, bound).astype(held_as)


def setup_inputs(seed: int = 0, part: int = 0) -> dict:
    keys = jax.random.split(jax.random.key(seed), 8)
    own_keys = jax.random.split(jax.random.fold_in(keys[7], part), 8)
    science = centred(own_keys[0], (CCDS, IMG_ROWS, IMG_COLS), 1.0, 6.0, ((0, 4), (1, 2), (2, 2)), jnp.float32)
    template = centred(own_keys[1], (CCDS, BANDS, HALVES, STRIPS, STRIP_ROWS, HALF), 1.0, 6.0, ((0, 4), (1, 2), (2, 2)))
    owners_keys = jax.random.split(jax.random.fold_in(own_keys[2], 1), CCDS * BANDS * HALVES * STRIPS // STRIPS)
    owners_turns = jax.random.permutation(jax.random.fold_in(own_keys[2], 3), CCDS * BANDS * HALVES * STRIPS // STRIPS)
    owners = jax.vmap(lambda own, number: shared_out(jax.random.fold_in(own_keys[2], 2), own, number, STRIPS, CCDS, 1, CAP, 2))(owners_keys, owners_turns).reshape((CCDS, BANDS, HALVES, STRIPS, 1))
    patch_strip = with_ends(jax.random.randint(own_keys[3], (CCDS, BANDS, HALVES, STRIPS), 0, STRIPS), jax.random.fold_in(own_keys[3], 1), 0, STRIPS - 1).astype(jnp.int32)
    shifts = with_ends(jax.random.randint(own_keys[4], (CCDS, BANDS, HALVES, 2, STRIPS), -3, 4), jax.random.fold_in(own_keys[4], 1), -3, 3).astype(jnp.int32)
    fractions = jnp.clip(0.05 + 0.9 * jax.random.uniform(own_keys[5], (CCDS, BANDS, HALVES, 2, STRIPS), jnp.float32) ** levels(own_keys[5], (CCDS, BANDS, HALVES, 2, STRIPS), ((0, 4), (1, 2), (2, 2)), -0.2, 0.2), 0.05, 0.95)
    coefs = centred(own_keys[6], (CCDS, 3, 9), 0.5, 3.0, ((0, 4),), jnp.float32)
    return {"science": science, "template": template, "owners": owners, "patch_strip": patch_strip, "shifts": shifts, "fractions": fractions, "coefs": coefs}


tap_margin = 6


def lanczos_taps(fraction):
    offsets = jnp.arange(-2, 4).astype(jnp.float32)
    spread = offsets[None, :] - fraction[:, None]
    return (jnp.sinc(spread) * jnp.sinc(spread / 3.0)).astype(jnp.bfloat16)


def kernel_table():
    support = jnp.arange(-RADIUS, RADIUS + 1).astype(jnp.float32)
    narrow = jnp.exp(-support * support / 4.5)
    slope = support * jnp.exp(-support * support / 12.5)
    broad = jnp.exp(-support * support / 40.5)
    return jnp.stack([narrow / jnp.sum(narrow), slope / jnp.sum(jnp.abs(slope)), broad / jnp.sum(broad)]).astype(jnp.bfloat16)


def strip_operator(taps, shift, strip_rows):
    out_rows = jnp.arange(strip_rows).astype(jnp.int32)[None, :, None]
    src_rows = jnp.arange(strip_rows).astype(jnp.int32)[None, None, :]
    offset = src_rows - out_rows - shift.astype(jnp.int32)[:, None, None]
    table = jnp.zeros(offset.shape, jnp.bfloat16)
    for which in range(6):
        table = jnp.where(offset == which - 2, taps[:, which][:, None, None], table)
    return table


def shift_columns(values, taps, starts, width):
    def one_strip(block, tap_row, start_row):
        total = jnp.zeros((block.shape[0], width), jnp.float32)
        for which in range(6):
            moved = lax.dynamic_slice_in_dim(block, start_row[which], width, 1)
            total = total + tap_row[which].astype(jnp.float32) * moved.astype(jnp.float32)
        return total
    return jax.vmap(one_strip)(values, taps, starts)


def tap_steps():
    return (jnp.arange(6) - 2).astype(jnp.int32)


def forward_warp(block, shift_pair, fraction_pair):
    strip_rows = block.shape[1]
    width = block.shape[2]
    row_taps = lanczos_taps(fraction_pair[0])
    col_taps = lanczos_taps(fraction_pair[1])
    operator = strip_operator(row_taps, shift_pair[0], strip_rows)
    rows_done = jnp.einsum("qik,qkz->qiz", operator.astype(jnp.float32), block.astype(jnp.float32)).astype(jnp.bfloat16)
    starts = (tap_margin + shift_pair[1].astype(jnp.int32)[:, None] + tap_steps()[None, :]).astype(jnp.int32)
    padded = jnp.pad(rows_done, ((0, 0), (0, 0), (tap_margin, tap_margin)))
    return shift_columns(padded, col_taps, starts, width).astype(jnp.bfloat16)


def backward_warp(block, shift_pair, fraction_pair):
    strip_rows = block.shape[1]
    width = block.shape[2]
    row_taps = lanczos_taps(fraction_pair[0])
    col_taps = lanczos_taps(fraction_pair[1])
    operator = strip_operator(row_taps, shift_pair[0], strip_rows)
    starts = (tap_margin - shift_pair[1].astype(jnp.int32)[:, None] - tap_steps()[None, :]).astype(jnp.int32)
    padded = jnp.pad(block, ((0, 0), (0, 0), (tap_margin, tap_margin)))
    columns_back = shift_columns(padded, col_taps, starts, width).astype(jnp.bfloat16)
    return jnp.einsum("qik,qiz->qkz", operator.astype(jnp.float32), columns_back.astype(jnp.float32))


def reference(science, template, owners, patch_strip, shifts, fractions, coefs):
    kernels = kernel_table()
    owner_all = owners[..., 0]
    band_index = jnp.arange(BANDS).astype(jnp.int32)[None, :, None, None]
    half_index = jnp.arange(HALVES).astype(jnp.int32)[None, None, :, None]
    chosen_all = template[owner_all, band_index, half_index, patch_strip]
    row_place = (jnp.arange(IMG_ROWS) + 0.5) / IMG_ROWS * 2.0 - 1.0
    col_place = (jnp.arange(IMG_COLS) + 0.5) / IMG_COLS * 2.0 - 1.0
    blocks = BANDS * HALVES
    width = 2 * RADIUS + 1

    def one_ccd(inputs):
        chosen, image_science, shift_ccd, fraction_ccd, coef_ccd = inputs
        chosen_flat = chosen.reshape(blocks, STRIPS, STRIP_ROWS, HALF)
        shift_flat = shift_ccd.reshape(blocks, 2, STRIPS)
        fraction_flat = fraction_ccd.reshape(blocks, 2, STRIPS)
        warped = jax.vmap(forward_warp)(chosen_flat, shift_flat, fraction_flat)
        image = warped.reshape(BANDS, HALVES, BAND, HALF).transpose(0, 2, 1, 3).reshape(IMG_ROWS, IMG_COLS)
        padded = jnp.pad(image, RADIUS)
        model = jnp.zeros((IMG_ROWS, IMG_COLS), jnp.float32)
        for first in range(3):
            across = jnp.zeros((IMG_ROWS, IMG_COLS + 2 * RADIUS), jnp.float32)
            for offset in range(width):
                across = across + kernels[first, offset].astype(jnp.float32) * padded[offset:offset + IMG_ROWS, :].astype(jnp.float32)
            across = across.astype(jnp.bfloat16)
            for second in range(3):
                term = jnp.zeros((IMG_ROWS, IMG_COLS), jnp.float32)
                for offset in range(width):
                    term = term + kernels[second, offset].astype(jnp.float32) * across[:, offset:offset + IMG_COLS].astype(jnp.float32)
                basis = first * 3 + second
                weight = coef_ccd[0, basis] + coef_ccd[1, basis] * col_place[None, :] + coef_ccd[2, basis] * row_place[:, None]
                model = model + weight * term
        difference = image_science - model
        lowered = difference.astype(jnp.bfloat16).reshape(BANDS, BAND, HALVES, HALF).transpose(0, 2, 1, 3)
        lowered = lowered.reshape(blocks, STRIPS, STRIP_ROWS, HALF)
        contribution = jax.vmap(backward_warp)(lowered, shift_flat, fraction_flat)
        return difference, contribution.reshape(BANDS, HALVES, STRIPS, STRIP_ROWS, HALF)

    differences, contributions = lax.map(one_ccd, (chosen_all, science, shifts, fractions, coefs))
    stack = jnp.zeros(template.shape, jnp.float32).at[owner_all, band_index, half_index, patch_strip].add(contributions)
    return differences, stack
```

```python
import functools

import jax
import jax.numpy as jnp
import ml_dtypes
import numpy as np
from jax import lax
from jax.experimental import pallas as pl
from jax.experimental.pallas import tpu as pltpu
from jax.sharding import PartitionSpec as P

RADIUS = 9
LANES = 128
HALF_TILE = 64
MARGIN = 16
TAPS = 6
KINDS = 3

F32 = jnp.float32
BF16 = jnp.bfloat16
SMEM = pl.BlockSpec(memory_space=pltpu.SMEM)
VMEM = pl.BlockSpec(memory_space=pltpu.VMEM)


def kernel_table():
    support = np.arange(-RADIUS, RADIUS + 1).astype(np.float32)
    narrow = np.exp(-support * support / np.float32(4.5))
    slope = support * np.exp(-support * support / np.float32(12.5))
    broad = np.exp(-support * support / np.float32(40.5))
    table = np.stack([narrow / narrow.sum(), slope / np.abs(slope).sum(), broad / broad.sum()])
    return table.astype(ml_dtypes.bfloat16)


def column_bands():
    table = kernel_table()
    source = np.arange(2 * LANES)[:, None]
    target = np.arange(LANES)[None, :]
    place = source - HALF_TILE - target + RADIUS
    inside = (place >= 0) & (place <= 2 * RADIUS)
    return np.stack(
        [np.where(inside, row[np.clip(place, 0, 2 * RADIUS)], 0) for row in table]
    ).astype(ml_dtypes.bfloat16)


def row_bands(count):
    table = kernel_table()
    source = np.arange(count + 2 * MARGIN)[None, :]
    target = np.arange(count)[:, None]
    place = source - MARGIN - target + RADIUS
    inside = (place >= 0) & (place <= 2 * RADIUS)
    return np.concatenate(
        [np.where(inside, row[np.clip(place, 0, 2 * RADIUS)], 0) for row in table]
    ).astype(ml_dtypes.bfloat16)


def lanczos_taps(fraction):
    offsets = jnp.arange(-2, 4).astype(F32)
    spread = offsets[None, :] - fraction[:, None]
    return (jnp.sinc(spread) * jnp.sinc(spread / 3.0)).astype(BF16)


def lane_index(rows):
    return lax.broadcasted_iota(jnp.int32, (rows, LANES), 1)


def partner_of(me, group, xor):
    return me ^ group if xor else group


def matches(code_ref, group, me, strips, capacity):
    found, count = [jnp.int32(0)] * capacity, jnp.int32(0)
    for q in range(strips):
        code = code_ref[group * strips + q] if group is not None else code_ref[q]
        hit = lax.div(code, jnp.int32(strips)) == me
        strip = lax.rem(code, jnp.int32(strips))
        found = [jnp.where(hit & (count == j), strip, f) for j, f in enumerate(found)]
        count = count + hit.astype(jnp.int32)
    return found, count


def slots_of(code_ref, me, strips, capacity, xor):
    owners = [lax.div(code_ref[q], jnp.int32(strips)) for q in range(strips)]
    slots = []
    for q in range(strips):
        rank = jnp.int32(0)
        for p in range(q):
            rank = rank + (owners[p] == owners[q]).astype(jnp.int32)
        slots.append(partner_of(me, owners[q], xor) * capacity + rank)
    return slots


def pick_kernel(n, capacity, strips, xor, *refs):
    codes, template, outs = refs[:-2] if xor else refs[:1], None, None
    if xor:
        codes, template, outs = refs[:n], refs[n], refs[n + 1 :]
    else:
        codes, template, outs = [refs[0]] * n, refs[1], refs[2:]
    me = lax.axis_index("ccd")
    for g in range(n):
        found, _ = matches(codes[g], None if xor else g, me, strips, capacity)
        for j in range(capacity):
            if xor:
                outs[g][j] = template[found[j]]
            else:
                outs[0][g * capacity + j] = template[found[j]]


def prepare_kernel(strips, strip_rows, tiles, amp_count, coefs, taps, shifts, bands, de, forward, mid, edge):
    amp = lax.axis_index("amp")
    width = tiles * LANES
    for first in range(KINDS):
        for tile in range(tiles):
            column = lane_index(1) + (amp * width + tile * LANES)
            px = (column.astype(F32) + 0.5) / (width * amp_count) * 2.0 - 1.0
            for half in range(2):
                rows = pl.ds(half * LANES, LANES)
                d = jnp.zeros((LANES, LANES), F32)
                e = jnp.zeros((LANES, LANES), F32)
                for second in range(KINDS):
                    basis = first * KINDS + second
                    band = bands[second, rows, :].astype(F32)
                    d = d + band * (coefs[basis] + coefs[9 + basis] * px)
                    e = e + band * coefs[18 + basis]
                at = pl.ds(half * KINDS * LANES + first * LANES, LANES)
                de[tile, at, 0:LANES] = d.astype(BF16)
                de[tile, at, LANES : 2 * LANES] = e.astype(BF16)

    def operator(out, chosen, transposed):
        size = out.shape[1]
        lane = lax.broadcasted_iota(jnp.int32, (strip_rows, size), 1)
        row = lax.broadcasted_iota(jnp.int32, (strip_rows, size), 0)
        for place, q in enumerate(chosen):
            low = place * strip_rows
            within = (lane >= low) & (lane < low + strip_rows)
            step = lane - low - row
            offset = (-step if transposed else step) - shifts[q]
            offset = jnp.where(within, offset, jnp.int32(1 << 20))
            value = jnp.zeros((strip_rows, size), F32)
            for t in range(TAPS):
                value = jnp.where(offset == t - 2, taps[q * TAPS + t], value)
            out[pl.ds(low, strip_rows), :] = value.astype(BF16)

    operator(forward, range(strips), False)
    operator(mid, range(1, strips - 1), True)
    operator(edge, (0, strips - 1), True)


def warp_kernel(n, capacity, strips, strip_rows, tiles, xor, paired, *refs):
    code, shifts, taps, forward = refs[:4]
    if xor:
        received, rest = refs[4 : 4 + n], refs[4 + n :]
    else:
        received, rest = refs[4:5], refs[5:]
    if paired:
        image, send_row, send_amp, send_diag, pool, fetched, rows_done = rest
    else:
        image, pool, fetched, rows_done = rest
    me = lax.axis_index("ccd")
    if xor:
        for g in range(n):
            pool[pl.ds(g * capacity, capacity)] = received[g][...]
    else:
        pool[...] = received[0][...]
    for q, slot in enumerate(slots_of(code, me, strips, capacity, xor)):
        fetched[pl.ds(q * strip_rows, strip_rows), :] = pool[slot]
    rows_done[...] = jnp.dot(forward[...], fetched[...], preferred_element_type=F32).astype(BF16).astype(F32)
    lane = lane_index(strip_rows)
    for q in range(strips):
        rows = pl.ds(q * strip_rows, strip_rows)
        source = [rows_done[rows, pl.ds(b * LANES, LANES)] for b in range(tiles)]
        total = [jnp.zeros((strip_rows, LANES), F32)] * (tiles + 1)
        for t in range(TAPS):
            amount = HALF_TILE - (shifts[strips + q] + (t - 2))
            tap = taps[(strips + q) * TAPS + t]
            spill = lane < amount
            before = None
            for b in range(tiles + 1):
                here = pltpu.roll(source[b], amount, 1) * tap if b < tiles else None
                if before is None:
                    value = jnp.where(spill, 0.0, here)
                elif here is None:
                    value = jnp.where(spill, before, 0.0)
                else:
                    value = jnp.where(spill, before, here)
                total[b] = total[b] + value
                before = here
        total[0] = jnp.where(lane < HALF_TILE, 0.0, total[0])
        total[tiles] = jnp.where(lane < HALF_TILE, total[tiles], 0.0)
        for b in range(tiles + 1):
            image[rows, pl.ds(b * LANES, LANES)] = total[b].astype(BF16)
    if paired:
        band = strips * strip_rows
        row_first = lax.axis_index("row") == 0
        amp_first = lax.axis_index("amp") == 0
        edge_rows = jnp.where(row_first, image[band - MARGIN : band, :], image[0:MARGIN, :])
        send_row[...] = edge_rows
        send_amp[...] = jnp.where(amp_first, image[:, tiles * LANES :], image[:, 0:LANES])
        send_diag[...] = jnp.where(amp_first, edge_rows[:, tiles * LANES :], edge_rows[:, 0:LANES])


def joined(ref, rows, left, right, tiles, amp_count):
    amp = lax.axis_index("amp")
    zero = jnp.zeros((), BF16)
    first = ref[rows, 0:LANES] + jnp.where(amp > 0, left, zero)
    last = ref[rows, tiles * LANES :] + jnp.where(amp < amp_count - 1, right, zero)
    return [first] + [ref[rows, b * LANES : (b + 1) * LANES] for b in range(1, tiles)] + [last]


def row_convolved(bands, parts, across, at, count):
    for low in range(0, len(parts), 2):
        window = jnp.concatenate(parts[low : low + 2], axis=1)
        result = jnp.dot(bands, window, preferred_element_type=F32)
        for b in range(low, min(low + 2, len(parts))):
            for kind in range(KINDS):
                piece = result[kind * count : (kind + 1) * count, (b - low) * LANES : (b - low + 1) * LANES]
                across[at : at + count, (b * KINDS + kind) * LANES : (b * KINDS + kind + 1) * LANES] = piece.astype(BF16)


def columns_returned(lowered, columns, at, strips, q, strip_rows, tiles, shifts, taps):
    lane = lane_index(strip_rows)
    rows = slice(at, at + strip_rows)
    source = [lowered[rows, b * LANES : (b + 1) * LANES] for b in range(tiles)]
    total = [jnp.zeros((strip_rows, LANES), F32)] * tiles
    for t in range(TAPS):
        amount = shifts[strips + q] + (t - 2)
        tap = taps[(strips + q) * TAPS + t]
        turn = jnp.where(amount < 0, amount + LANES, amount)
        low, high = lane < amount, lane >= LANES + amount
        moved = [pltpu.roll(s, turn, 1) * tap for s in source]
        for b in range(tiles):
            value = jnp.where(low, moved[b - 1] if b > 0 else 0.0, moved[b])
            value = jnp.where(high, moved[b + 1] if b < tiles - 1 else 0.0, value)
            total[b] = total[b] + value
    for b in range(tiles):
        columns[rows, b * LANES : (b + 1) * LANES] = total[b].astype(BF16)


def subtracted(science, across, de, store, count, tiles, place):
    for b in range(tiles):
        acc = jnp.dot(
            across[:, b * KINDS * LANES : (b + 2) * KINDS * LANES], de[b], preferred_element_type=F32
        )
        store(b, science(b) - (acc[:, 0:LANES] + place * acc[:, LANES:]))


def row_place(first, count, band, row_count):
    row = lax.broadcasted_iota(jnp.int32, (count, LANES), 0) + (lax.axis_index("row") * band + first)
    return (row.astype(F32) + 0.5) / (band * row_count) * 2.0 - 1.0


def mid_kernel(strips, strip_rows, tiles, row_count, amp_count, image, left, right, science, de, bands, operator,
               shifts, taps, diff, contribution, across, lowered, columns):
    band = strips * strip_rows
    count = band - 2 * strip_rows
    rows = slice(strip_rows - MARGIN, band - strip_rows + MARGIN)
    parts = joined(image, rows, left[rows, :], right[rows, :], tiles, amp_count)
    row_convolved(bands[...], parts, across, 0, count)

    def store(b, value):
        diff[:, b * LANES : (b + 1) * LANES] = value
        lowered[:, b * LANES : (b + 1) * LANES] = value.astype(BF16).astype(F32)

    subtracted(
        lambda b: science[strip_rows : strip_rows + count, b * LANES : (b + 1) * LANES],
        across, de, store, count, tiles, row_place(strip_rows, count, band, row_count),
    )
    for q in range(1, strips - 1):
        columns_returned(lowered, columns, (q - 1) * strip_rows, strips, q, strip_rows, tiles, shifts, taps)
    contribution[...] = jnp.dot(operator[...], columns[...], preferred_element_type=F32).astype(BF16)


def edge_kernel(n, capacity, strips, strip_rows, tiles, row_count, amp_count, xor, image, left, right, top, bottom,
                top_left, top_right, bottom_left, bottom_right, science, de, bands, operator, shifts, taps, code,
                diff_mid, contribution_mid, diff, *rest):
    outs = rest[: n if xor else 1]
    across, lowered, columns, pool = rest[len(outs) :]
    band = strips * strip_rows
    inner = strip_rows + MARGIN
    row = lax.axis_index("row")
    zero = jnp.zeros((), BF16)
    everything = slice(0, MARGIN)
    above = [jnp.where(row > 0, part, zero)
             for part in joined(top, everything, top_left[...], top_right[...], tiles, amp_count)]
    below = [jnp.where(row < row_count - 1, part, zero)
             for part in joined(bottom, everything, bottom_left[...], bottom_right[...], tiles, amp_count)]
    first, last = slice(0, inner), slice(band - inner, band)
    upper = joined(image, first, left[first, :], right[first, :], tiles, amp_count)
    lower = joined(image, last, left[last, :], right[last, :], tiles, amp_count)
    row_convolved(bands[...], [jnp.concatenate(p, axis=0) for p in zip(above, upper)], across, 0, strip_rows)
    row_convolved(bands[...], [jnp.concatenate(p, axis=0) for p in zip(lower, below)], across, strip_rows, strip_rows)

    def store(b, value):
        at = slice(b * LANES, (b + 1) * LANES)
        diff[0:strip_rows, at] = value[0:strip_rows]
        diff[band - strip_rows : band, at] = value[strip_rows:]
        lowered[:, at] = value.astype(BF16).astype(F32)

    def edge_science(b):
        at = slice(b * LANES, (b + 1) * LANES)
        return jnp.concatenate([science[0:strip_rows, at], science[band - strip_rows : band, at]], axis=0)

    place = jnp.concatenate([row_place(0, strip_rows, band, row_count),
                             row_place(band - strip_rows, strip_rows, band, row_count)], axis=0)
    subtracted(edge_science, across, de, store, 2 * strip_rows, tiles, place)
    diff[strip_rows : band - strip_rows, :] = diff_mid[...]
    columns_returned(lowered, columns, 0, strips, 0, strip_rows, tiles, shifts, taps)
    columns_returned(lowered, columns, strip_rows, strips, strips - 1, strip_rows, tiles, shifts, taps)
    ends = jnp.dot(operator[...], columns[...], preferred_element_type=F32).astype(BF16)
    me = lax.axis_index("ccd")
    target = pool if xor else outs[0]
    if n * capacity != strips:
        target[...] = jnp.zeros(target.shape, BF16)
    for q, slot in enumerate(slots_of(code, me, strips, capacity, xor)):
        if q == 0:
            target[slot] = ends[0:strip_rows]
        elif q == strips - 1:
            target[slot] = ends[strip_rows:]
        else:
            target[slot] = contribution_mid[(q - 1) * strip_rows : q * strip_rows, :]
    if xor:
        for g in range(n):
            outs[g][...] = pool[pl.ds(g * capacity, capacity)]


def sum_kernel(n, capacity, strips, xor, *refs):
    if xor:
        codes, returned, stack = refs[:n], refs[n : 2 * n], refs[2 * n]
    else:
        codes, returned, stack = [refs[0]] * n, [refs[1]] * n, refs[2]
    me = lax.axis_index("ccd")
    stack[...] = jnp.zeros(stack.shape, F32)
    for g in range(n):
        found, count = matches(codes[g], None if xor else g, me, strips, capacity)
        for j in range(capacity):

            @pl.when(count > j)
            def _(g=g, j=j, strip=found[j]):
                at = j if xor else g * capacity + j
                stack[strip] += returned[g][at].astype(F32)


def body(science, template, owners, patch_strip, shifts, fractions, coefs):
    n = lax.axis_size("ccd")
    row_count = lax.axis_size("row")
    amp_count = lax.axis_size("amp")
    band, width = science.shape[1:]
    strips, strip_rows = template.shape[3:5]
    capacity = max(2, strips // n)
    tiles = width // LANES
    padded = width + LANES
    xor = n in (2, 4)
    paired = row_count == 2 and amp_count == 2
    swap = [(0, 1), (1, 0)]
    strip_shape = (capacity, strip_rows, width)

    def call(kernel, out_shape, operands, spaces, scratch=(), megabytes=8, flops=0):
        return pl.pallas_call(
            kernel,
            out_shape=[jax.ShapeDtypeStruct(s, d) for s, d in out_shape],
            in_specs=list(spaces),
            out_specs=[VMEM] * len(out_shape),
            scratch_shapes=[pltpu.VMEM(s, d) for s, d in scratch],
            compiler_params=pltpu.CompilerParams(vmem_limit_bytes=megabytes << 20),
            cost_estimate=pl.CostEstimate(flops=flops, bytes_accessed=1 << 20, transcendentals=0),
        )(*operands)

    def exchange(parts):
        if not xor:
            return [lax.all_to_all(parts[0], "ccd", split_axis=0, concat_axis=0, tiled=True)]
        return [parts[0]] + [
            lax.ppermute(parts[g], "ccd", [(i, i ^ g) for i in range(n)]) for g in range(1, n)
        ]

    code = owners.reshape(strips) * strips + patch_strip.reshape(strips)
    if xor:
        codes = [code] + [lax.ppermute(code, "ccd", [(i, i ^ g) for i in range(n)]) for g in range(1, n)]
        picked_shapes = [(strip_shape, BF16)] * n
    else:
        codes = [lax.all_gather(code, "ccd", axis=0, tiled=True)]
        picked_shapes = [((n * capacity, strip_rows, width), BF16)]
    shift_list = shifts.reshape(2 * strips)
    taps = lanczos_taps(fractions.reshape(2 * strips)).astype(F32).reshape(2 * strips * TAPS)
    science = science.reshape(band, width)
    template_strips = template.reshape(strips, strip_rows, width)

    picked = call(
        functools.partial(pick_kernel, n, capacity, strips, xor),
        picked_shapes,
        [*codes, template_strips],
        [SMEM] * len(codes) + [VMEM],
    )
    mid_rows = band - 2 * strip_rows
    de, forward, mid_operator, edge_operator = call(
        functools.partial(prepare_kernel, strips, strip_rows, tiles, amp_count),
        [
            ((tiles, 2 * KINDS * LANES, 2 * LANES), BF16),
            ((band, band), BF16),
            ((mid_rows, mid_rows), BF16),
            ((2 * strip_rows, 2 * strip_rows), BF16),
        ],
        [coefs.reshape(27), taps, shift_list, jnp.asarray(column_bands())],
        [SMEM, SMEM, SMEM, VMEM],
    )
    received = exchange(picked)
    image_shape = ((band, padded), BF16)
    halo_shapes = [((MARGIN, padded), BF16), ((band, LANES), BF16), ((MARGIN, LANES), BF16)]
    warped = call(
        functools.partial(warp_kernel, n, capacity, strips, strip_rows, tiles, xor, paired),
        [image_shape] + (halo_shapes if paired else []),
        [code, shift_list, taps, forward, *received],
        [SMEM, SMEM, SMEM, VMEM] + [VMEM] * len(received),
        [((n * capacity, strip_rows, width), BF16), ((band, width), BF16), ((band, width), F32)],
    )
    image = warped[0]
    if paired:
        side = lax.ppermute(warped[2], "amp", swap)
        ends = lax.ppermute(warped[1], "row", swap)
        corner = lax.ppermute(warped[3], ("row", "amp"), [(0, 3), (3, 0), (1, 2), (2, 1)])
        left = right = side
        top = bottom = ends
        top_left = top_right = bottom_left = bottom_right = corner
    else:
        first, last = image[:MARGIN], image[band - MARGIN :]

        def moved(value, down, along):
            pairs = []
            for r in range(row_count):
                for a in range(amp_count):
                    if 0 <= r + down < row_count and 0 <= a + along < amp_count:
                        pairs.append((r * amp_count + a, (r + down) * amp_count + a + along))
            return lax.ppermute(value, ("row", "amp"), pairs)

        left = moved(image[:, padded - LANES :], 0, 1)
        right = moved(image[:, :LANES], 0, -1)
        top, bottom = moved(last, 1, 0), moved(first, -1, 0)
        top_left = moved(last[:, padded - LANES :], 1, 1)
        top_right = moved(last[:, :LANES], 1, -1)
        bottom_left = moved(first[:, padded - LANES :], -1, 1)
        bottom_right = moved(first[:, :LANES], -1, -1)

    diff_mid, contribution_mid = call(
        functools.partial(mid_kernel, strips, strip_rows, tiles, row_count, amp_count),
        [((mid_rows, width), F32), ((mid_rows, width), BF16)],
        [image, left, right, science, de, jnp.asarray(row_bands(mid_rows)), mid_operator, shift_list, taps],
        [VMEM] * 7 + [SMEM] * 2,
        [((mid_rows, (tiles + 1) * KINDS * LANES), BF16), ((mid_rows, width), F32), ((mid_rows, width), BF16)],
        megabytes=12,
    )
    outgoing_shapes = picked_shapes
    difference, *outgoing = call(
        functools.partial(edge_kernel, n, capacity, strips, strip_rows, tiles, row_count, amp_count, xor),
        [((band, width), F32)] + outgoing_shapes,
        [image, left, right, top, bottom, top_left, top_right, bottom_left, bottom_right, science, de,
         jnp.asarray(row_bands(strip_rows)), edge_operator, shift_list, taps, code, diff_mid, contribution_mid],
        [VMEM] * 13 + [SMEM] * 3 + [VMEM] * 2,
        [((2 * strip_rows, (tiles + 1) * KINDS * LANES), BF16), ((2 * strip_rows, width), F32),
         ((2 * strip_rows, width), BF16), ((n * capacity, strip_rows, width), BF16)],
        megabytes=12,
    )
    returned = exchange(outgoing)
    (stack,) = call(
        functools.partial(sum_kernel, n, capacity, strips, xor),
        [((strips, strip_rows, width), F32)],
        [*codes, *returned],
        [SMEM] * len(codes) + [VMEM] * len(returned),
    )
    return difference[None], stack.reshape(template.shape)


def solution(mesh):
    return jax.shard_map(
        body,
        mesh=mesh,
        in_specs=(
            P(("grp", "ccd"), "row", "amp"),
            P(("grp", "ccd"), "row", "amp", None, None, None),
            P(("grp", "ccd"), "row", "amp", None, None),
            P(("grp", "ccd"), "row", "amp", None),
            P(("grp", "ccd"), "row", "amp", None, None),
            P(("grp", "ccd"), "row", "amp", None, None),
            P(("grp", "ccd"), None, None),
        ),
        out_specs=(
            P(("grp", "ccd"), "row", "amp"),
            P(("grp", "ccd"), "row", "amp", None, None, None),
        ),
        check_vma=False,
    )
```

```python
import functools

import jax
import jax.numpy as jnp
import ml_dtypes
import numpy as np
from jax import lax
from jax.experimental import pallas as pl
from jax.experimental.pallas import tpu as pltpu
from jax.sharding import PartitionSpec as P

RADIUS = 9
LANES = 128
HALF_TILE = 64
MARGIN = 16
TAPS = 6
KINDS = 3

F32 = jnp.float32
BF16 = jnp.bfloat16
SMEM = pl.BlockSpec(memory_space=pltpu.SMEM)
VMEM = pl.BlockSpec(memory_space=pltpu.VMEM)
HBM = pl.BlockSpec(memory_space=pltpu.HBM)


def kernel_table():
    support = np.arange(-RADIUS, RADIUS + 1).astype(np.float32)
    narrow = np.exp(-support * support / np.float32(4.5))
    slope = support * np.exp(-support * support / np.float32(12.5))
    broad = np.exp(-support * support / np.float32(40.5))
    table = np.stack([narrow / narrow.sum(), slope / np.abs(slope).sum(), broad / broad.sum()])
    return table.astype(ml_dtypes.bfloat16)


def column_bands():
    table = kernel_table()
    source = np.arange(2 * LANES)[:, None]
    target = np.arange(LANES)[None, :]
    place = source - HALF_TILE - target + RADIUS
    inside = (place >= 0) & (place <= 2 * RADIUS)
    return np.stack(
        [np.where(inside, row[np.clip(place, 0, 2 * RADIUS)], 0) for row in table]
    ).astype(ml_dtypes.bfloat16)


def row_bands(count):
    table = kernel_table()
    source = np.arange(count + 2 * MARGIN)[None, :]
    target = np.arange(count)[:, None]
    place = source - MARGIN - target + RADIUS
    inside = (place >= 0) & (place <= 2 * RADIUS)
    return np.concatenate(
        [np.where(inside, row[np.clip(place, 0, 2 * RADIUS)], 0) for row in table]
    ).astype(ml_dtypes.bfloat16)


def sinc(value):
    turn = jnp.pi * value
    return jnp.where(value == 0.0, 1.0, jnp.sin(turn) / jnp.where(value == 0.0, 1.0, turn))


def lanczos_taps(fraction):
    place = lax.broadcasted_iota(jnp.int32, (8, fraction.shape[1]), 0) - 2
    spread = place.astype(F32) - fraction
    return (sinc(spread) * sinc(spread / 3.0)).astype(BF16).astype(F32)


def in_hbm(value):
    return pltpu.with_memory_space_constraint(value, pltpu.HBM)


def lane_index(rows):
    return lax.broadcasted_iota(jnp.int32, (rows, LANES), 1)


def partner_of(me, group, xor):
    return me ^ group if xor else group


def matches(code_ref, group, me, strips, capacity):
    found, count = [jnp.int32(0)] * capacity, jnp.int32(0)
    for q in range(strips):
        code = code_ref[group * strips + q] if group is not None else code_ref[q]
        hit = lax.div(code, jnp.int32(strips)) == me
        strip = lax.rem(code, jnp.int32(strips))
        found = [jnp.where(hit & (count == j), strip, f) for j, f in enumerate(found)]
        count = count + hit.astype(jnp.int32)
    return found, count


def slots_of(code_ref, me, strips, capacity, xor):
    owners = [lax.div(code_ref[q], jnp.int32(strips)) for q in range(strips)]
    slots = []
    for q in range(strips):
        rank = jnp.int32(0)
        for p in range(q):
            rank = rank + (owners[p] == owners[q]).astype(jnp.int32)
        slots.append(partner_of(me, owners[q], xor) * capacity + rank)
    return slots


def pick_kernel(n, capacity, strips, xor, *refs):
    codes, template, outs = refs[:-2] if xor else refs[:1], None, None
    if xor:
        codes, template, outs = refs[:n], refs[n], refs[n + 1 :]
    else:
        codes, template, outs = [refs[0]] * n, refs[1], refs[2:]
    me = lax.axis_index("ccd")
    for g in range(n):
        found, _ = matches(codes[g], None if xor else g, me, strips, capacity)
        for j in range(capacity):
            if xor:
                outs[g][j] = template[found[j]]
            else:
                outs[0][g * capacity + j] = template[found[j]]


def load_kernel(source, target, sem):
    copy = pltpu.make_async_copy(source, target, sem)
    copy.start()
    copy.wait()


def prepare_kernel(strips, strip_rows, tiles, amp_count, coefs_in, shifts_in, fractions_in, bands_in, science_in,
                   row_band_in, after, de, forward, mid, edge, spread, gather, science, row_band,
                   coefs, shifts, fractions, bands, sems):
    del after
    pairs = [(fractions_in, fractions), (shifts_in, shifts), (coefs_in, coefs),
             (bands_in, bands), (row_band_in, row_band), (science_in, science)]
    copies = [pltpu.make_async_copy(source, target, sems.at[i]) for i, (source, target) in enumerate(pairs)]
    for copy in copies:
        copy.start()
    for copy in copies[:2]:
        copy.wait()
    taps = [lanczos_taps(fractions[d : d + 1, :]) for d in range(2)]

    def operator(out, chosen, transposed):
        size = out.shape[1]
        lane = lax.broadcasted_iota(jnp.int32, (strip_rows, size), 1)
        row = lax.broadcasted_iota(jnp.int32, (strip_rows, size), 0)
        for place, q in enumerate(chosen):
            low = place * strip_rows
            within = (lane >= low) & (lane < low + strip_rows)
            step = lane - low - row
            offset = (-step if transposed else step) - shifts[0, q]
            offset = jnp.where(within, offset, jnp.int32(1 << 20))
            value = jnp.zeros((strip_rows, size), F32)
            for t in range(TAPS):
                tap = jnp.broadcast_to(taps[0][t : t + 1, q : q + 1], (strip_rows, size))
                value = jnp.where(offset == t - 2, tap, value)
            out[pl.ds(low, strip_rows), :] = value.astype(BF16)

    operator(forward, range(strips), False)
    operator(mid, range(1, strips - 1), True)
    operator(edge, (0, strips - 1), True)

    rows = 160
    away = lane_index(rows) - lax.broadcasted_iota(jnp.int32, (rows, LANES), 0)
    for out, low, centre, sign in ((spread, 48, HALF_TILE, 1), (gather, 112, LANES, -1)):
        size = out.shape[1]
        for q in range(strips):
            step = -sign * (away + (centre - low)) - shifts[1, q]
            value = jnp.zeros((rows, LANES), F32)
            for t in range(TAPS):
                tap = jnp.broadcast_to(taps[1][t : t + 1, q : q + 1], (rows, LANES))
                value = jnp.where(step == t - 2, tap, value)
            out[q, 0:low, :] = jnp.zeros((low, LANES), BF16)
            out[q, low : low + rows, :] = value.astype(BF16)
            out[q, low + rows : size, :] = jnp.zeros((size - low - rows, LANES), BF16)
    for copy in copies[2:4]:
        copy.wait()
    amp = lax.axis_index("amp")
    width = tiles * LANES
    for first in range(KINDS):
        for half in range(2):
            rows = pl.ds(half * LANES, LANES)
            at = pl.ds((half * KINDS + first) * LANES, LANES)
            band = [bands[second, rows, :].astype(F32) for second in range(KINDS)]
            e = sum(band[b] * coefs[2, 0, first * KINDS + b] for b in range(KINDS)).astype(BF16)
            for tile in range(tiles):
                column = lane_index(1) + (amp * width + tile * LANES)
                px = (column.astype(F32) + 0.5) / (width * amp_count) * 2.0 - 1.0
                weight = [coefs[0, 0, first * KINDS + b] + coefs[1, 0, first * KINDS + b] * px for b in range(KINDS)]
                de[tile, at, 0:LANES] = sum(band[b] * weight[b] for b in range(KINDS)).astype(BF16)
                de[tile, at, LANES : 2 * LANES] = e
    for copy in copies[4:]:
        copy.wait()


def clear_ends(ref, tiles):
    zero = jnp.zeros((ref.shape[0], LANES), BF16)
    ref[:, 0:LANES] = zero
    ref[:, (tiles + 1) * LANES : (tiles + 2) * LANES] = zero


def warp_kernel(n, capacity, strips, strip_rows, tiles, xor, paired, *refs):
    code, forward, spread = refs[:3]
    if xor:
        received, rest = refs[3 : 3 + n], refs[3 + n :]
    else:
        received, rest = refs[3:4], refs[4:]
    if paired:
        image, send_row, send_amp, send_diag, pool, fetched, rows_done = rest
    else:
        image, pool, fetched, rows_done = rest
    me = lax.axis_index("ccd")
    if xor:
        for g in range(n):
            pool[pl.ds(g * capacity, capacity)] = received[g][...]
    else:
        pool[...] = received[0][...]
    for q, slot in enumerate(slots_of(code, me, strips, capacity, xor)):
        fetched[pl.ds(q * strip_rows, strip_rows), :] = pool[slot]
    width = tiles * LANES
    clear_ends(rows_done, tiles)
    rows_done[:, LANES : LANES + width] = jnp.dot(
        forward[...], fetched[...], preferred_element_type=F32
    ).astype(BF16)
    lane = lane_index(strip_rows)
    for q in range(strips):
        rows = slice(q * strip_rows, (q + 1) * strip_rows)
        windows = [rows_done[rows, b * LANES : (b + 2) * LANES] for b in range(tiles + 1)]
        result = jnp.dot(jnp.concatenate(windows, axis=0), spread[q], preferred_element_type=F32)
        for b in range(tiles + 1):
            value = result[b * strip_rows : (b + 1) * strip_rows]
            if b == 0:
                value = jnp.where(lane < HALF_TILE, 0.0, value)
            if b == tiles:
                value = jnp.where(lane < HALF_TILE, value, 0.0)
            image[rows, b * LANES : (b + 1) * LANES] = value.astype(BF16)
    if paired:
        band = strips * strip_rows
        row_first = lax.axis_index("row") == 0
        amp_first = lax.axis_index("amp") == 0
        edge_rows = jnp.where(row_first, image[band - MARGIN : band, :], image[0:MARGIN, :])
        send_row[...] = edge_rows
        send_amp[...] = jnp.where(amp_first, image[:, tiles * LANES :], image[:, 0:LANES])
        send_diag[...] = jnp.where(amp_first, edge_rows[:, tiles * LANES :], edge_rows[:, 0:LANES])


def joined(ref, rows, left, right, tiles, amp_count):
    amp = lax.axis_index("amp")
    zero = jnp.zeros((), BF16)
    first = ref[rows, 0:LANES] + jnp.where(amp > 0, left, zero)
    last = ref[rows, tiles * LANES :] + jnp.where(amp < amp_count - 1, right, zero)
    return [first] + [ref[rows, b * LANES : (b + 1) * LANES] for b in range(1, tiles)] + [last]


def row_convolved(bands, parts, across, at, count):
    for low in range(0, len(parts), 2):
        window = jnp.concatenate(parts[low : low + 2], axis=1)
        result = jnp.dot(bands, window, preferred_element_type=F32)
        for b in range(low, min(low + 2, len(parts))):
            for kind in range(KINDS):
                piece = result[kind * count : (kind + 1) * count, (b - low) * LANES : (b - low + 1) * LANES]
                across[at : at + count, (b * KINDS + kind) * LANES : (b * KINDS + kind + 1) * LANES] = piece.astype(BF16)


def columns_returned(lowered, columns, at, gather, strip_rows, tiles):
    rows = slice(at, at + strip_rows)
    windows = [lowered[rows, b * LANES : (b + 3) * LANES] for b in range(tiles)]
    result = jnp.dot(jnp.concatenate(windows, axis=0), gather, preferred_element_type=F32)
    for b in range(tiles):
        columns[rows, b * LANES : (b + 1) * LANES] = result[b * strip_rows : (b + 1) * strip_rows].astype(BF16)


def subtracted(science, across, de, store, count, tiles, place):
    for b in range(tiles):
        acc = jnp.dot(
            across[:, b * KINDS * LANES : (b + 2) * KINDS * LANES], de[b], preferred_element_type=F32
        )
        store(b, science(b) - (acc[:, 0:LANES] + place * acc[:, LANES:]))


def row_place(first, count, band, row_count):
    row = lax.broadcasted_iota(jnp.int32, (count, LANES), 0) + (lax.axis_index("row") * band + first)
    return (row.astype(F32) + 0.5) / (band * row_count) * 2.0 - 1.0


def mid_kernel(strips, strip_rows, tiles, row_count, amp_count, image, left, right, science, de, bands, operator,
               gather, diff, contribution, across, lowered, columns):
    band = strips * strip_rows
    count = band - 2 * strip_rows
    rows = slice(strip_rows - MARGIN, band - strip_rows + MARGIN)
    parts = joined(image, rows, left[rows, :], right[rows, :], tiles, amp_count)
    row_convolved(bands[...], parts, across, 0, count)
    clear_ends(lowered, tiles)

    def store(b, value):
        diff[:, b * LANES : (b + 1) * LANES] = value
        lowered[:, (b + 1) * LANES : (b + 2) * LANES] = value.astype(BF16)

    subtracted(
        lambda b: science[strip_rows : strip_rows + count, b * LANES : (b + 1) * LANES],
        across, de, store, count, tiles, row_place(strip_rows, count, band, row_count),
    )
    for q in range(1, strips - 1):
        columns_returned(lowered, columns, (q - 1) * strip_rows, gather[q], strip_rows, tiles)
    contribution[...] = jnp.dot(operator[...], columns[...], preferred_element_type=F32).astype(BF16)


def edge_kernel(n, capacity, strips, strip_rows, tiles, row_count, amp_count, xor, image, left, right, top, bottom,
                top_left, top_right, bottom_left, bottom_right, science, de, bands, operator, gather, code,
                contribution_mid, diff, *rest):
    outs = rest[: n if xor else 1]
    across, lowered, columns, pool = rest[len(outs) :]
    band = strips * strip_rows
    inner = strip_rows + MARGIN
    row = lax.axis_index("row")
    zero = jnp.zeros((), BF16)
    everything = slice(0, MARGIN)
    above = [jnp.where(row > 0, part, zero)
             for part in joined(top, everything, top_left[...], top_right[...], tiles, amp_count)]
    below = [jnp.where(row < row_count - 1, part, zero)
             for part in joined(bottom, everything, bottom_left[...], bottom_right[...], tiles, amp_count)]
    first, last = slice(0, inner), slice(band - inner, band)
    upper = joined(image, first, left[first, :], right[first, :], tiles, amp_count)
    lower = joined(image, last, left[last, :], right[last, :], tiles, amp_count)
    row_convolved(bands[...], [jnp.concatenate(p, axis=0) for p in zip(above, upper)], across, 0, strip_rows)
    row_convolved(bands[...], [jnp.concatenate(p, axis=0) for p in zip(lower, below)], across, strip_rows, strip_rows)

    def store(b, value):
        at = slice(b * LANES, (b + 1) * LANES)
        diff[:, at] = value
        lowered[:, (b + 1) * LANES : (b + 2) * LANES] = value.astype(BF16)

    clear_ends(lowered, tiles)

    def edge_science(b):
        at = slice(b * LANES, (b + 1) * LANES)
        return jnp.concatenate([science[0:strip_rows, at], science[band - strip_rows : band, at]], axis=0)

    place = jnp.concatenate([row_place(0, strip_rows, band, row_count),
                             row_place(band - strip_rows, strip_rows, band, row_count)], axis=0)
    subtracted(edge_science, across, de, store, 2 * strip_rows, tiles, place)
    columns_returned(lowered, columns, 0, gather[0], strip_rows, tiles)
    columns_returned(lowered, columns, strip_rows, gather[strips - 1], strip_rows, tiles)
    ends = jnp.dot(operator[...], columns[...], preferred_element_type=F32).astype(BF16)
    me = lax.axis_index("ccd")
    target = pool if xor else outs[0]
    if n * capacity != strips:
        target[...] = jnp.zeros(target.shape, BF16)
    for q, slot in enumerate(slots_of(code, me, strips, capacity, xor)):
        if q == 0:
            target[slot] = ends[0:strip_rows]
        elif q == strips - 1:
            target[slot] = ends[strip_rows:]
        else:
            target[slot] = contribution_mid[(q - 1) * strip_rows : q * strip_rows, :]
    if xor:
        for g in range(n):
            outs[g][...] = pool[pl.ds(g * capacity, capacity)]


def sum_kernel(n, capacity, strips, xor, *refs):
    if xor:
        codes, returned, stack = refs[:n], refs[n : 2 * n], refs[2 * n]
    else:
        codes, returned, stack = [refs[0]] * n, [refs[1]] * n, refs[2]
    me = lax.axis_index("ccd")
    stack[...] = jnp.zeros(stack.shape, F32)
    for g in range(n):
        found, count = matches(codes[g], None if xor else g, me, strips, capacity)
        for j in range(capacity):

            @pl.when(count > j)
            def _(g=g, j=j, strip=found[j]):
                at = j if xor else g * capacity + j
                stack[strip] += returned[g][at].astype(F32)


def body(science, template, owners, patch_strip, shifts, fractions, coefs):
    n = lax.axis_size("ccd")
    row_count = lax.axis_size("row")
    amp_count = lax.axis_size("amp")
    band, width = science.shape[1:]
    strips, strip_rows = template.shape[3:5]
    capacity = max(2, strips // n)
    tiles = width // LANES
    padded = width + LANES
    xor = n in (2, 4)
    paired = row_count == 2 and amp_count == 2
    swap = [(0, 1), (1, 0)]
    strip_shape = (capacity, strip_rows, width)

    def call(kernel, out_shape, operands, spaces, scratch=(), megabytes=8, flops=0):
        return pl.pallas_call(
            kernel,
            out_shape=[jax.ShapeDtypeStruct(s, d) for s, d in out_shape],
            in_specs=list(spaces),
            out_specs=[VMEM] * len(out_shape),
            scratch_shapes=[pltpu.VMEM(*s) if isinstance(s, tuple) else s for s in scratch],
            compiler_params=pltpu.CompilerParams(vmem_limit_bytes=megabytes << 20),
            cost_estimate=pl.CostEstimate(flops=flops, bytes_accessed=1 << 20, transcendentals=0),
        )(*operands)

    def exchange(parts):
        if not xor:
            return [lax.all_to_all(parts[0], "ccd", split_axis=0, concat_axis=0, tiled=True)]
        return [parts[0]] + [
            lax.ppermute(parts[g], "ccd", [(i, i ^ g) for i in range(n)]) for g in range(1, n)
        ]

    code = owners.reshape(strips) * strips + patch_strip.reshape(strips)
    if xor:
        codes = [code] + [lax.ppermute(code, "ccd", [(i, i ^ g) for i in range(n)]) for g in range(1, n)]
        picked_shapes = [(strip_shape, BF16)] * n
    else:
        codes = [lax.all_gather(code, "ccd", axis=0, tiled=True)]
        picked_shapes = [((n * capacity, strip_rows, width), BF16)]
    (template_strips,) = call(
        load_kernel,
        [((strips, strip_rows, width), BF16)],
        [in_hbm(template.reshape(strips, strip_rows, width))],
        [HBM],
        [pltpu.SemaphoreType.DMA],
    )
    picked = call(
        functools.partial(pick_kernel, n, capacity, strips, xor),
        picked_shapes,
        [*codes, template_strips],
        [SMEM] * len(codes) + [VMEM],
    )
    mid_rows = band - 2 * strip_rows
    mid_bands = jnp.asarray(row_bands(mid_rows))
    de, forward, mid_operator, edge_operator, spread, gather, science, mid_bands = call(
        functools.partial(prepare_kernel, strips, strip_rows, tiles, amp_count),
        [
            ((tiles, 2 * KINDS * LANES, 2 * LANES), BF16),
            ((band, band), BF16),
            ((mid_rows, mid_rows), BF16),
            ((2 * strip_rows, 2 * strip_rows), BF16),
            ((strips, 2 * LANES, LANES), BF16),
            ((strips, 3 * LANES, LANES), BF16),
            ((band, width), F32),
            (mid_bands.shape, BF16),
        ],
        [in_hbm(value) for value in (
            coefs.transpose(1, 0, 2), shifts.reshape(2, strips), fractions.reshape(2, strips),
            jnp.asarray(column_bands()), science.reshape(band, width), mid_bands)] + [picked[0]],
        [HBM] * 6 + [VMEM],
        [pltpu.SMEM((3, 1, 9), F32), pltpu.SMEM((2, strips), jnp.int32),
         ((2, strips), F32), ((KINDS, 2 * LANES, LANES), BF16), pltpu.SemaphoreType.DMA((6,))],
    )
    received = exchange(picked)
    image_shape = ((band, padded), BF16)
    halo_shapes = [((MARGIN, padded), BF16), ((band, LANES), BF16), ((MARGIN, LANES), BF16)]
    warped = call(
        functools.partial(warp_kernel, n, capacity, strips, strip_rows, tiles, xor, paired),
        [image_shape] + (halo_shapes if paired else []),
        [code, forward, spread, *received],
        [SMEM, VMEM, VMEM] + [VMEM] * len(received),
        [((n * capacity, strip_rows, width), BF16), ((band, width), BF16),
         ((band, padded + LANES), BF16)],
    )
    image = warped[0]
    if paired:
        side = lax.ppermute(warped[2], "amp", swap)
        ends = lax.ppermute(warped[1], "row", swap)
        corner = lax.ppermute(warped[3], ("row", "amp"), [(0, 3), (3, 0), (1, 2), (2, 1)])
        left = right = side
        top = bottom = ends
        top_left = top_right = bottom_left = bottom_right = corner
    else:
        first, last = image[:MARGIN], image[band - MARGIN :]

        def moved(value, down, along):
            pairs = []
            for r in range(row_count):
                for a in range(amp_count):
                    if 0 <= r + down < row_count and 0 <= a + along < amp_count:
                        pairs.append((r * amp_count + a, (r + down) * amp_count + a + along))
            return lax.ppermute(value, ("row", "amp"), pairs)

        left = moved(image[:, padded - LANES :], 0, 1)
        right = moved(image[:, :LANES], 0, -1)
        top, bottom = moved(last, 1, 0), moved(first, -1, 0)
        top_left = moved(last[:, padded - LANES :], 1, 1)
        top_right = moved(last[:, :LANES], 1, -1)
        bottom_left = moved(first[:, padded - LANES :], -1, 1)
        bottom_right = moved(first[:, :LANES], -1, -1)

    diff_mid, contribution_mid = call(
        functools.partial(mid_kernel, strips, strip_rows, tiles, row_count, amp_count),
        [((mid_rows, width), F32), ((mid_rows, width), BF16)],
        [image, left, right, science, de, mid_bands, mid_operator, gather],
        [VMEM] * 8,
        [((mid_rows, (tiles + 1) * KINDS * LANES), BF16), ((mid_rows, padded + LANES), BF16),
         ((mid_rows, width), BF16)],
        megabytes=12,
    )
    outgoing_shapes = picked_shapes
    diff_edge, *outgoing = call(
        functools.partial(edge_kernel, n, capacity, strips, strip_rows, tiles, row_count, amp_count, xor),
        [((2 * strip_rows, width), F32)] + outgoing_shapes,
        [image, left, right, top, bottom, top_left, top_right, bottom_left, bottom_right, science, de,
         jnp.asarray(row_bands(strip_rows)), edge_operator, gather, code, contribution_mid],
        [VMEM] * 14 + [SMEM, VMEM],
        [((2 * strip_rows, (tiles + 1) * KINDS * LANES), BF16), ((2 * strip_rows, padded + LANES), BF16),
         ((2 * strip_rows, width), BF16), ((n * capacity, strip_rows, width), BF16)],
        megabytes=12,
    )
    returned = exchange(outgoing)
    (stack,) = call(
        functools.partial(sum_kernel, n, capacity, strips, xor),
        [((strips, strip_rows, width), F32)],
        [*codes, *returned],
        [SMEM] * len(codes) + [VMEM] * len(returned),
    )
    difference = jnp.concatenate([diff_edge[:strip_rows], diff_mid, diff_edge[strip_rows:]])
    return difference[None], stack.reshape(template.shape)


def solution(mesh):
    return jax.shard_map(
        body,
        mesh=mesh,
        in_specs=(
            P(("grp", "ccd"), "row", "amp"),
            P(("grp", "ccd"), "row", "amp", None, None, None),
            P(("grp", "ccd"), "row", "amp", None, None),
            P(("grp", "ccd"), "row", "amp", None),
            P(("grp", "ccd"), "row", "amp", None, None),
            P(("grp", "ccd"), "row", "amp", None, None),
            P(("grp", "ccd"), None, None),
        ),
        out_specs=(
            P(("grp", "ccd"), "row", "amp"),
            P(("grp", "ccd"), "row", "amp", None, None, None),
        ),
        check_vma=False,
    )
```

```python
import functools

import jax
import jax.numpy as jnp
import ml_dtypes
import numpy as np
from jax import lax
from jax.experimental import pallas as pl
from jax.experimental.pallas import tpu as pltpu
from jax.sharding import PartitionSpec as P

RADIUS = 9
LANES = 128
HALF_TILE = 64
MARGIN = 16
TAPS = 6
KINDS = 3

F32 = jnp.float32
BF16 = jnp.bfloat16
SMEM = pl.BlockSpec(memory_space=pltpu.SMEM)
VMEM = pl.BlockSpec(memory_space=pltpu.VMEM)
HBM = pl.BlockSpec(memory_space=pltpu.HBM)


def kernel_table():
    support = np.arange(-RADIUS, RADIUS + 1).astype(np.float32)
    narrow = np.exp(-support * support / np.float32(4.5))
    slope = support * np.exp(-support * support / np.float32(12.5))
    broad = np.exp(-support * support / np.float32(40.5))
    table = np.stack([narrow / narrow.sum(), slope / np.abs(slope).sum(), broad / broad.sum()])
    return table.astype(ml_dtypes.bfloat16)


def column_bands():
    table = kernel_table()
    source = np.arange(2 * LANES)[:, None]
    target = np.arange(LANES)[None, :]
    place = source - HALF_TILE - target + RADIUS
    inside = (place >= 0) & (place <= 2 * RADIUS)
    return np.stack(
        [np.where(inside, row[np.clip(place, 0, 2 * RADIUS)], 0) for row in table]
    ).astype(ml_dtypes.bfloat16)


def row_bands(count):
    table = kernel_table()
    source = np.arange(count + 2 * MARGIN)[None, :]
    target = np.arange(count)[:, None]
    place = source - MARGIN - target + RADIUS
    inside = (place >= 0) & (place <= 2 * RADIUS)
    return np.concatenate(
        [np.where(inside, row[np.clip(place, 0, 2 * RADIUS)], 0) for row in table]
    ).astype(ml_dtypes.bfloat16)


def sinc(value):
    turn = jnp.pi * value
    return jnp.where(value == 0.0, 1.0, jnp.sin(turn) / jnp.where(value == 0.0, 1.0, turn))


def lanczos_taps(fraction):
    place = lax.broadcasted_iota(jnp.int32, (8, fraction.shape[1]), 0) - 2
    spread = place.astype(F32) - fraction
    return (sinc(spread) * sinc(spread / 3.0)).astype(BF16).astype(F32)


def in_hbm(value):
    return pltpu.with_memory_space_constraint(value, pltpu.HBM)


def lane_index(rows):
    return lax.broadcasted_iota(jnp.int32, (rows, LANES), 1)


def partner_of(me, group, xor):
    return me ^ group if xor else group


def matches(code_ref, group, me, strips, capacity):
    found, count = [jnp.int32(0)] * capacity, jnp.int32(0)
    for q in range(strips):
        code = code_ref[group * strips + q] if group is not None else code_ref[q]
        hit = lax.div(code, jnp.int32(strips)) == me
        strip = lax.rem(code, jnp.int32(strips))
        found = [jnp.where(hit & (count == j), strip, f) for j, f in enumerate(found)]
        count = count + hit.astype(jnp.int32)
    return found, count


def slots_of(code_ref, me, strips, capacity, xor):
    owners = [lax.div(code_ref[0, q], jnp.int32(strips)) for q in range(strips)]
    slots = []
    for q in range(strips):
        rank = jnp.int32(0)
        for p in range(q):
            rank = rank + (owners[p] == owners[q]).astype(jnp.int32)
        slots.append(partner_of(me, owners[q], xor) * capacity + rank)
    return slots


def pick_kernel(n, capacity, strips, xor, *refs):
    if xor:
        codes, template, outs = refs[:n], refs[n], refs[n + 1 :]
    else:
        codes, template, outs = [refs[0]] * n, refs[1], refs[2:]
    me = lax.axis_index("ccd")
    for g in range(n):
        found, _ = matches(codes[g], None if xor else g, me, strips, capacity)
        for j in range(capacity):
            if xor:
                outs[g][j] = template[strip_rows_at(found[j], template.shape[0] // strips), :]
            else:
                outs[0][g * capacity + j] = template[strip_rows_at(found[j], template.shape[0] // strips), :]


def two_of(value, owner, strips):
    lane = lax.broadcasted_iota(jnp.int32, value.shape, 1).astype(F32)
    low = (owner * strips).astype(F32)
    hit = (value >= low) & (value < low + strips)
    key = lane * strips + (value - low)
    first = jnp.min(jnp.where(hit, key, 1024.0)).astype(jnp.int32)
    last = jnp.max(jnp.where(hit, key, 0.0)).astype(jnp.int32)
    return lax.rem(first, jnp.int32(strips)), lax.rem(last, jnp.int32(strips))


def strip_rows_at(strip, strip_rows):
    return pl.ds(pl.multiple_of(strip * strip_rows, strip_rows), strip_rows)


def pick_two_kernel(strips, strip_rows, *refs):
    count = len(refs) // 2
    template = refs[count]
    for code, out in zip(refs[:count], refs[count + 1 :]):
        for j, strip in enumerate(two_of(code[...].astype(F32), lax.axis_index("ccd"), strips)):
            out[j] = template[strip_rows_at(strip, strip_rows), :]


def load_kernel(source, target, sem):
    copy = pltpu.make_async_copy(source, target, sem)
    copy.start()
    copy.wait()


def turned(base, first, rows):
    return pltpu.roll(jnp.broadcast_to(base, (rows, base.shape[1])), first, 1, stride=1, stride_axis=0)


def base_row(taps, q, start, sign, size):
    lane = lax.broadcasted_iota(jnp.int32, (1, size), 1)
    value = jnp.zeros((1, size), F32)
    for t in range(TAPS):
        at = lax.rem(start + sign * (t - 2) + size, jnp.int32(size))
        value = jnp.where(lane == at, jnp.broadcast_to(taps[t : t + 1, q : q + 1], (1, size)), value)
    return value


def prepare_kernel(n, capacity, strips, strip_rows, tiles, amp_count, xor, two, coefs_in, shifts_in, fractions_in,
                   bands_in, science_in, row_band_in, after, code, *refs):
    del after
    if two:
        own_code, template, own = refs[:3]
        refs = refs[3:]
    de, forward, backward, spread, gather, science, row_band, coefs, shifts, fractions, bands, sems = refs
    pairs = [(fractions_in, fractions), (shifts_in, shifts), (coefs_in, coefs),
             (bands_in, bands), (row_band_in, row_band), (science_in, science)]
    copies = [pltpu.make_async_copy(source, target, sems.at[i]) for i, (source, target) in enumerate(pairs)]
    for copy in copies:
        copy.start()
    for copy in copies[:2]:
        copy.wait()
    taps = [lanczos_taps(fractions[d : d + 1, :]) for d in range(2)]
    me = lax.axis_index("ccd")
    band, slots = strips * strip_rows, n * capacity
    size = slots * strip_rows
    if slots != strips:
        backward[...] = jnp.zeros(backward.shape, BF16)
    forward_lane = lax.broadcasted_iota(jnp.int32, (strip_rows, size), 1)
    backward_lane = lax.broadcasted_iota(jnp.int32, (strip_rows, band), 1)
    for q, slot in enumerate(slots_of(code, me, strips, capacity, xor)):
        low, high = slot * strip_rows, q * strip_rows
        value = turned(base_row(taps[0], q, low + shifts[0, q], 1, size), 0, strip_rows)
        value = jnp.where((forward_lane >= low) & (forward_lane < low + strip_rows), value, 0.0)
        forward[high : high + strip_rows, :] = value.astype(BF16)
        value = turned(base_row(taps[0], q, high - shifts[0, q], -1, band), 0, strip_rows)
        value = jnp.where((backward_lane >= high) & (backward_lane < high + strip_rows), value, 0.0)
        backward[strip_rows_at(slot, strip_rows), :] = value.astype(BF16)

    if two:
        for j, strip in enumerate(two_of(own_code[...].astype(F32), me, strips)):
            own[j] = template[strip_rows_at(strip, strip_rows), :]

    rows = 160
    away = lax.broadcasted_iota(jnp.int32, (rows, LANES), 0) - lane_index(rows)
    for out, low, centre, sign in ((spread, 48, HALF_TILE, -1), (gather, 112, LANES, 1)):
        within = (away >= centre - low - 8) & (away <= centre - low + 8)
        end = out.shape[1]
        for q in range(strips):
            start = (low - centre) + sign * shifts[1, q] + LANES
            value = turned(base_row(taps[1], q, start, sign, LANES), 0, rows)
            out[q, 0:low, :] = jnp.zeros((low, LANES), BF16)
            out[q, low : low + rows, :] = jnp.where(within, value, 0.0).astype(BF16)
            out[q, low + rows : end, :] = jnp.zeros((end - low - rows, LANES), BF16)
    for copy in copies[2:4]:
        copy.wait()
    amp = lax.axis_index("amp")
    width = tiles * LANES
    rows = 80
    for half in range(2):
        low = half * LANES + (0 if half else LANES - rows)
        for first in range(KINDS):
            at = (half * KINDS + first) * LANES
            band_rows = [bands[second, low : low + rows, :].astype(F32) for second in range(KINDS)]
            e = sum(band_rows[b] * coefs[2, 0, first * KINDS + b] for b in range(KINDS)).astype(BF16)
            empty = jnp.zeros((LANES - rows, 2 * LANES), BF16)
            begin = at + (0 if half else LANES - rows)
            for tile in range(tiles):
                column = lane_index(1) + (amp * width + tile * LANES)
                px = (column.astype(F32) + 0.5) / (width * amp_count) * 2.0 - 1.0
                weight = [coefs[0, 0, first * KINDS + b] + coefs[1, 0, first * KINDS + b] * px for b in range(KINDS)]
                d = sum(band_rows[b] * weight[b] for b in range(KINDS)).astype(BF16)
                de[tile, begin : begin + rows, 0:LANES] = d
                de[tile, begin : begin + rows, LANES : 2 * LANES] = e
                hollow = at + (rows if half else 0)
                de[tile, hollow : hollow + LANES - rows, :] = empty
    for copy in copies[4:]:
        copy.wait()


def collect_kernel(n, capacity, strips, strip_rows, xor, two, after, *refs):
    del after
    out = refs[-1]
    me = lax.axis_index("ccd")
    size = n * capacity * strip_rows
    lane = lax.broadcasted_iota(jnp.int32, (1, size), 1)
    named = jnp.full(lane.shape, -1, jnp.int32)
    for g in range(n):
        if two:
            found = two_of(refs[g][...].astype(F32), me, strips)
        else:
            found, total = matches(refs[g if xor else 0], None if xor else g, me, strips, capacity)
            found = [jnp.where(total > j, strip, -1) for j, strip in enumerate(found)]
        for j in range(capacity):
            low = (g * capacity + j) * strip_rows
            named = jnp.where((lane >= low) & (lane < low + strip_rows), found[j], named)
    lane = lax.broadcasted_iota(jnp.int32, (strip_rows, size), 1)
    row = lax.broadcasted_iota(jnp.int32, lane.shape, 0)
    same_row = lax.rem(lane, jnp.int32(strip_rows)) == row
    for p in range(strips):
        value = jnp.where(same_row & (named == p), 1.0, 0.0)
        out[p * strip_rows : (p + 1) * strip_rows, :] = value.astype(BF16)


def clear_ends(ref, tiles):
    zero = jnp.zeros((ref.shape[0], LANES), BF16)
    ref[:, 0:LANES] = zero
    ref[:, (tiles + 1) * LANES : (tiles + 2) * LANES] = zero


def stacked(refs):
    parts = [ref[...].reshape(-1, ref.shape[-1]) for ref in refs]
    return jnp.concatenate(parts, axis=0) if len(parts) > 1 else parts[0]


def warp_kernel(n, strips, strip_rows, tiles, xor, paired, *refs):
    forward, spread = refs[:2]
    count = n if xor else 1
    received, rest = refs[2 : 2 + count][::-1], refs[2 + count :]
    if paired:
        image, send_row, send_amp, send_diag, rows_done = rest
    else:
        image, rows_done = rest
    width = tiles * LANES
    clear_ends(rows_done, tiles)
    rows_done[:, LANES : LANES + width] = jnp.dot(
        forward[...], stacked(received), preferred_element_type=F32
    ).astype(BF16)
    lane = lane_index(strip_rows)
    for q in range(strips):
        rows = slice(q * strip_rows, (q + 1) * strip_rows)
        windows = [rows_done[rows, b * LANES : (b + 2) * LANES] for b in range(tiles + 1)]
        result = jnp.dot(jnp.concatenate(windows, axis=0), spread[q], preferred_element_type=F32)
        for b in range(tiles + 1):
            value = result[b * strip_rows : (b + 1) * strip_rows]
            if b == 0:
                value = jnp.where(lane < HALF_TILE, 0.0, value)
            if b == tiles:
                value = jnp.where(lane < HALF_TILE, value, 0.0)
            image[rows, b * LANES : (b + 1) * LANES] = value.astype(BF16)
    if paired:
        band = strips * strip_rows
        row_first = lax.axis_index("row") == 0
        amp_first = lax.axis_index("amp") == 0
        edge_rows = jnp.where(row_first, image[band - MARGIN : band, :], image[0:MARGIN, :])
        send_row[...] = edge_rows
        send_amp[...] = jnp.where(amp_first, image[:, tiles * LANES :], image[:, 0:LANES])
        send_diag[...] = jnp.where(amp_first, edge_rows[:, tiles * LANES :], edge_rows[:, 0:LANES])


def joined(ref, rows, left, right, tiles, amp_count):
    amp = lax.axis_index("amp")
    zero = jnp.zeros((), BF16)
    first = ref[rows, 0:LANES] + jnp.where(amp > 0, left, zero)
    last = ref[rows, tiles * LANES :] + jnp.where(amp < amp_count - 1, right, zero)
    return [first] + [ref[rows, b * LANES : (b + 1) * LANES] for b in range(1, tiles)] + [last]


def row_convolved(bands, parts, across, at, count):
    for low in range(0, len(parts), 2):
        window = jnp.concatenate(parts[low : low + 2], axis=1)
        result = jnp.dot(bands, window, preferred_element_type=F32)
        for b in range(low, min(low + 2, len(parts))):
            for kind in range(KINDS):
                piece = result[kind * count : (kind + 1) * count, (b - low) * LANES : (b - low + 1) * LANES]
                across[at : at + count, (b * KINDS + kind) * LANES : (b * KINDS + kind + 1) * LANES] = piece.astype(BF16)


def columns_returned(lowered, columns, at, gather, strip_rows, tiles):
    rows = slice(at, at + strip_rows)
    windows = [lowered[rows, b * LANES : (b + 3) * LANES] for b in range(tiles)]
    result = jnp.dot(jnp.concatenate(windows, axis=0), gather, preferred_element_type=F32)
    for b in range(tiles):
        columns[rows, b * LANES : (b + 1) * LANES] = result[b * strip_rows : (b + 1) * strip_rows].astype(BF16)


def subtracted(science, across, de, store, count, tiles, place):
    for b in range(tiles):
        acc = jnp.dot(
            across[:, b * KINDS * LANES : (b + 2) * KINDS * LANES], de[b], preferred_element_type=F32
        )
        store(b, science(b) - (acc[:, 0:LANES] + place * acc[:, LANES:]))


def row_place(first, count, band, row_count):
    row = lax.broadcasted_iota(jnp.int32, (count, LANES), 0) + (lax.axis_index("row") * band + first)
    return (row.astype(F32) + 0.5) / (band * row_count) * 2.0 - 1.0


def mid_kernel(strips, strip_rows, tiles, row_count, amp_count, image, left, right, science, de, bands, gather,
               diff, columns, across, lowered):
    band = strips * strip_rows
    count = band - 2 * strip_rows
    rows = slice(strip_rows - MARGIN, band - strip_rows + MARGIN)
    parts = joined(image, rows, left[rows, :], right[rows, :], tiles, amp_count)
    row_convolved(bands[...], parts, across, 0, count)
    clear_ends(lowered, tiles)

    def store(b, value):
        diff[:, b * LANES : (b + 1) * LANES] = value
        lowered[:, (b + 1) * LANES : (b + 2) * LANES] = value.astype(BF16)

    subtracted(
        lambda b: science[strip_rows : strip_rows + count, b * LANES : (b + 1) * LANES],
        across, de, store, count, tiles, row_place(strip_rows, count, band, row_count),
    )
    for q in range(1, strips - 1):
        columns_returned(lowered, columns, (q - 1) * strip_rows, gather[q], strip_rows, tiles)


def edge_kernel(n, capacity, strips, strip_rows, tiles, row_count, amp_count, xor, image, left, right, top, bottom,
                top_left, top_right, bottom_left, bottom_right, science, de, bands, backward, gather,
                columns_mid, diff, *rest):
    outs = rest[: n if xor else 1]
    across, lowered, columns = rest[len(outs) :]
    band = strips * strip_rows
    inner = strip_rows + MARGIN
    row = lax.axis_index("row")
    zero = jnp.zeros((), BF16)
    everything = slice(0, MARGIN)
    above = [jnp.where(row > 0, part, zero)
             for part in joined(top, everything, top_left[...], top_right[...], tiles, amp_count)]
    below = [jnp.where(row < row_count - 1, part, zero)
             for part in joined(bottom, everything, bottom_left[...], bottom_right[...], tiles, amp_count)]
    first, last = slice(0, inner), slice(band - inner, band)
    upper = joined(image, first, left[first, :], right[first, :], tiles, amp_count)
    lower = joined(image, last, left[last, :], right[last, :], tiles, amp_count)
    row_convolved(bands[...], [jnp.concatenate(p, axis=0) for p in zip(above, upper)], across, 0, strip_rows)
    row_convolved(bands[...], [jnp.concatenate(p, axis=0) for p in zip(lower, below)], across, strip_rows, strip_rows)

    def store(b, value):
        at = slice(b * LANES, (b + 1) * LANES)
        diff[:, at] = value
        lowered[:, (b + 1) * LANES : (b + 2) * LANES] = value.astype(BF16)

    clear_ends(lowered, tiles)

    def edge_science(b):
        at = slice(b * LANES, (b + 1) * LANES)
        return jnp.concatenate([science[0:strip_rows, at], science[band - strip_rows : band, at]], axis=0)

    place = jnp.concatenate([row_place(0, strip_rows, band, row_count),
                             row_place(band - strip_rows, strip_rows, band, row_count)], axis=0)
    subtracted(edge_science, across, de, store, 2 * strip_rows, tiles, place)
    columns_returned(lowered, columns, 0, gather[0], strip_rows, tiles)
    columns_returned(lowered, columns, strip_rows, gather[strips - 1], strip_rows, tiles)
    whole = jnp.concatenate([columns[:strip_rows, :], columns_mid[...], columns[strip_rows:, :]], axis=0)
    result = jnp.dot(backward[...], whole, preferred_element_type=F32).astype(BF16)
    size = capacity * strip_rows * (1 if xor else n)
    for g, out in enumerate(outs):
        out[...] = result[g * size : (g + 1) * size].reshape(out.shape)


def sum_kernel(collect, *refs):
    *returned, stack, total, sems = refs
    values = stacked(returned[::-1])
    copies = []
    half = total.shape[0] // 2
    for i in range(2):
        rows = pl.ds(i * half, half)
        total[rows, :] = jnp.dot(collect[rows, :], values, preferred_element_type=F32)
        copy = pltpu.make_async_copy(total.at[rows], stack.at[rows], sems.at[i])
        copy.start()
        copies.append(copy)
    for copy in copies:
        copy.wait()


def body(science, template, owners, patch_strip, shifts, fractions, coefs):
    n = lax.axis_size("ccd")
    row_count = lax.axis_size("row")
    amp_count = lax.axis_size("amp")
    band, width = science.shape[1:]
    strips, strip_rows = template.shape[3:5]
    capacity = max(2, strips // n)
    tiles = width // LANES
    padded = width + LANES
    xor = n in (2, 4)
    two = xor and capacity == 2 and strips == 2 * n
    paired = row_count == 2 and amp_count == 2
    swap = [(0, 1), (1, 0)]
    strip_shape = (capacity, strip_rows, width)

    def call(kernel, out_shape, operands, spaces, scratch=(), megabytes=8):
        shapes = [jax.ShapeDtypeStruct(*s) if isinstance(s, tuple) else s for s in out_shape]
        return pl.pallas_call(
            kernel,
            out_shape=shapes,
            in_specs=list(spaces),
            out_specs=[VMEM if isinstance(s, tuple) else HBM for s in out_shape],
            scratch_shapes=[pltpu.VMEM(*s) if isinstance(s, tuple) else s for s in scratch],
            compiler_params=pltpu.CompilerParams(vmem_limit_bytes=megabytes << 20),
            cost_estimate=pl.CostEstimate(flops=0, bytes_accessed=1 << 20, transcendentals=0),
        )(*operands)

    def exchange(parts):
        if not xor:
            return [lax.all_to_all(parts[0], "ccd", split_axis=0, concat_axis=0, tiled=True)]
        return [parts[0]] + [
            lax.ppermute(parts[g], "ccd", [(i, i ^ g) for i in range(n)]) for g in range(1, n)
        ]

    code = owners.reshape(1, strips) * strips + patch_strip.reshape(1, strips)
    (template_rows,) = call(
        load_kernel,
        [((band, width), BF16)],
        [in_hbm(template.reshape(band, width))],
        [HBM],
        [pltpu.SemaphoreType.DMA],
    )

    def exchanged(value, g):
        return lax.ppermute(value, "ccd", [(i, i ^ g) for i in range(n)])

    if two:
        codes = [code] + [exchanged(code, g) for g in range(1, n)]
        picked = call(
            functools.partial(pick_two_kernel, strips, strip_rows),
            [(strip_shape, BF16)] * (n - 1),
            [*codes[1:], template_rows],
            [VMEM] * n,
        )
    elif xor:
        codes = [code.reshape(strips)] + [exchanged(code.reshape(strips), g) for g in range(1, n)]
        picked_shapes = [(strip_shape, BF16)] * n
    else:
        codes = [lax.all_gather(code.reshape(strips), "ccd", axis=0, tiled=True)]
        picked_shapes = [((n * capacity, strip_rows, width), BF16)]
    if not two:
        picked = call(
            functools.partial(pick_kernel, n, capacity, strips, xor),
            picked_shapes,
            [*codes, template_rows],
            [SMEM] * len(codes) + [VMEM],
        )
    mid_rows = band - 2 * strip_rows
    mid_bands = jnp.asarray(row_bands(mid_rows))
    slot_rows = n * capacity * strip_rows
    *own, de, forward, backward, spread, gather, science, mid_bands = call(
        functools.partial(prepare_kernel, n, capacity, strips, strip_rows, tiles, amp_count, xor, two),
        ([(strip_shape, BF16)] if two else []) + [
            ((tiles, 2 * KINDS * LANES, 2 * LANES), BF16),
            ((band, slot_rows), BF16),
            ((slot_rows, band), BF16),
            ((strips, 2 * LANES, LANES), BF16),
            ((strips, 3 * LANES, LANES), BF16),
            ((band, width), F32),
            (mid_bands.shape, BF16),
        ],
        [in_hbm(value) for value in (
            coefs.transpose(1, 0, 2), shifts.reshape(2, strips), fractions.reshape(2, strips),
            jnp.asarray(column_bands()), science.reshape(band, width), mid_bands)]
        + [picked[-1], code] + ([code, template_rows] if two else []),
        [HBM] * 6 + [VMEM, SMEM] + [VMEM] * (2 if two else 0),
        [pltpu.SMEM((3, 1, 9), F32), pltpu.SMEM((2, strips), jnp.int32),
         ((2, strips), F32), ((KINDS, 2 * LANES, LANES), BF16), pltpu.SemaphoreType.DMA((6,))],
        megabytes=10,
    )
    if two:
        received = exchange([*own, *picked])[::-1]
    else:
        received = exchange(picked)[::-1]
    image_shape = ((band, padded), BF16)
    halo_shapes = [((MARGIN, padded), BF16), ((band, LANES), BF16), ((MARGIN, LANES), BF16)]
    warped = call(
        functools.partial(warp_kernel, n, strips, strip_rows, tiles, xor, paired),
        [image_shape] + (halo_shapes if paired else []),
        [forward, spread, *received],
        [VMEM] * (2 + len(received)),
        [((band, padded + LANES), BF16)],
    )
    image = warped[0]
    if paired:
        side = lax.ppermute(warped[2], "amp", swap)
        ends = lax.ppermute(warped[1], "row", swap)
        corner = lax.ppermute(warped[3], ("row", "amp"), [(0, 3), (3, 0), (1, 2), (2, 1)])
        left = right = side
        top = bottom = ends
        top_left = top_right = bottom_left = bottom_right = corner
    else:
        first, last = image[:MARGIN], image[band - MARGIN :]

        def moved(value, down, along):
            pairs = []
            for r in range(row_count):
                for a in range(amp_count):
                    if 0 <= r + down < row_count and 0 <= a + along < amp_count:
                        pairs.append((r * amp_count + a, (r + down) * amp_count + a + along))
            return lax.ppermute(value, ("row", "amp"), pairs)

        left = moved(image[:, padded - LANES :], 0, 1)
        right = moved(image[:, :LANES], 0, -1)
        top, bottom = moved(last, 1, 0), moved(first, -1, 0)
        top_left = moved(last[:, padded - LANES :], 1, 1)
        top_right = moved(last[:, :LANES], 1, -1)
        bottom_left = moved(first[:, padded - LANES :], -1, 1)
        bottom_right = moved(first[:, :LANES], -1, -1)

    diff_mid, columns_mid = call(
        functools.partial(mid_kernel, strips, strip_rows, tiles, row_count, amp_count),
        [((mid_rows, width), F32), ((mid_rows, width), BF16)],
        [image, left, right, science, de, mid_bands, gather],
        [VMEM] * 7,
        [((mid_rows, (tiles + 1) * KINDS * LANES), BF16), ((mid_rows, padded + LANES), BF16)],
    )
    outgoing_shapes = [(strip_shape, BF16)] * n if xor else [((n * capacity, strip_rows, width), BF16)]
    diff_edge, *outgoing = call(
        functools.partial(edge_kernel, n, capacity, strips, strip_rows, tiles, row_count, amp_count, xor),
        [((2 * strip_rows, width), F32)] + outgoing_shapes,
        [image, left, right, top, bottom, top_left, top_right, bottom_left, bottom_right, science, de,
         jnp.asarray(row_bands(strip_rows)), backward, gather, columns_mid],
        [VMEM] * 15,
        [((2 * strip_rows, (tiles + 1) * KINDS * LANES), BF16), ((2 * strip_rows, padded + LANES), BF16),
         ((2 * strip_rows, width), BF16)],
    )
    returned = exchange(outgoing)[::-1]
    (collect,) = call(
        functools.partial(collect_kernel, n, capacity, strips, strip_rows, xor, two),
        [((band, slot_rows), BF16)],
        [outgoing[0], *codes],
        [VMEM] + [VMEM if two else SMEM] * len(codes),
    )
    (stack,) = call(
        sum_kernel,
        [pltpu.HBM((band, width), F32)],
        [collect, *returned],
        [VMEM] * (1 + len(returned)),
        [((band, width), F32), pltpu.SemaphoreType.DMA((2,))],
    )
    difference = jnp.concatenate([diff_edge[:strip_rows], diff_mid, diff_edge[strip_rows:]])
    return difference[None], stack.reshape(template.shape)


def solution(mesh):
    return jax.shard_map(
        body,
        mesh=mesh,
        in_specs=(
            P(("grp", "ccd"), "row", "amp"),
            P(("grp", "ccd"), "row", "amp", None, None, None),
            P(("grp", "ccd"), "row", "amp", None, None),
            P(("grp", "ccd"), "row", "amp", None),
            P(("grp", "ccd"), "row", "amp", None, None),
            P(("grp", "ccd"), "row", "amp", None, None),
            P(("grp", "ccd"), None, None),
        ),
        out_specs=(
            P(("grp", "ccd"), "row", "amp"),
            P(("grp", "ccd"), "row", "amp", None, None, None),
        ),
        check_vma=False,
    )
```

```python
import functools

import jax
import jax.numpy as jnp
import ml_dtypes
import numpy as np
from jax import lax
from jax.experimental import pallas as pl
from jax.experimental.pallas import tpu as pltpu
from jax.sharding import PartitionSpec as P

RADIUS = 9
LANES = 128
HALF_TILE = 64
MARGIN = 16
TAPS = 6
KINDS = 3

F32 = jnp.float32
BF16 = jnp.bfloat16
SMEM = pl.BlockSpec(memory_space=pltpu.SMEM)
VMEM = pl.BlockSpec(memory_space=pltpu.VMEM)
HBM = pl.BlockSpec(memory_space=pltpu.HBM)


def kernel_table():
    support = np.arange(-RADIUS, RADIUS + 1).astype(np.float32)
    narrow = np.exp(-support * support / np.float32(4.5))
    slope = support * np.exp(-support * support / np.float32(12.5))
    broad = np.exp(-support * support / np.float32(40.5))
    table = np.stack([narrow / narrow.sum(), slope / np.abs(slope).sum(), broad / broad.sum()])
    return table.astype(ml_dtypes.bfloat16)


def column_bands():
    table = kernel_table()
    source = np.arange(2 * LANES)[:, None]
    target = np.arange(LANES)[None, :]
    place = source - HALF_TILE - target + RADIUS
    inside = (place >= 0) & (place <= 2 * RADIUS)
    return np.stack(
        [np.where(inside, row[np.clip(place, 0, 2 * RADIUS)], 0) for row in table]
    ).astype(ml_dtypes.bfloat16)


def row_bands(count):
    table = kernel_table()
    source = np.arange(count + 2 * MARGIN)[None, :]
    target = np.arange(count)[:, None]
    place = source - MARGIN - target + RADIUS
    inside = (place >= 0) & (place <= 2 * RADIUS)
    return np.concatenate(
        [np.where(inside, row[np.clip(place, 0, 2 * RADIUS)], 0) for row in table]
    ).astype(ml_dtypes.bfloat16)


def sinc(value):
    turn = jnp.pi * value
    return jnp.where(value == 0.0, 1.0, jnp.sin(turn) / jnp.where(value == 0.0, 1.0, turn))


def lanczos_taps(fraction):
    place = lax.broadcasted_iota(jnp.int32, (8, fraction.shape[1]), 0) - 2
    spread = place.astype(F32) - fraction
    return (sinc(spread) * sinc(spread / 3.0)).astype(BF16).astype(F32)


def in_hbm(value):
    return pltpu.with_memory_space_constraint(value, pltpu.HBM)


def lane_index(rows):
    return lax.broadcasted_iota(jnp.int32, (rows, LANES), 1)


def order_of(n):
    return (2, 3, 1, 0) if n == 4 else (*range(1, n), 0)


def in_order(values):
    return [values[g] for g in order_of(len(values))]


def from_order(values):
    order = order_of(len(values))
    return [values[order.index(g)] for g in range(len(values))]


def matches(code_ref, group, me, strips, capacity):
    found, count = [jnp.int32(0)] * capacity, jnp.int32(0)
    for q in range(strips):
        code = code_ref[group * strips + q] if group is not None else code_ref[q]
        hit = lax.div(code, jnp.int32(strips)) == me
        strip = lax.rem(code, jnp.int32(strips))
        found = [jnp.where(hit & (count == j), strip, f) for j, f in enumerate(found)]
        count = count + hit.astype(jnp.int32)
    return found, count


def slots_of(code_ref, me, strips, capacity, n, ring):
    owners = [lax.div(code_ref[0, q], jnp.int32(strips)) for q in range(strips)]
    slots = []
    for q in range(strips):
        rank = jnp.int32(0)
        for p in range(q):
            rank = rank + (owners[p] == owners[q]).astype(jnp.int32)
        group = lax.rem(owners[q] - me + n, jnp.int32(n)) if ring else owners[q]
        slots.append(group * capacity + rank)
    return slots


def pick_kernel(n, capacity, strips, ring, *refs):
    if ring:
        codes, template, outs = refs[:n], refs[n], refs[n + 1 :]
    else:
        codes, template, outs = [refs[0]] * n, refs[1], refs[2:]
    me = lax.axis_index("ccd")
    for g in range(n):
        found, _ = matches(codes[g], None if ring else g, me, strips, capacity)
        for j in range(capacity):
            if ring:
                outs[g][j] = template[strip_rows_at(found[j], template.shape[0] // strips), :]
            else:
                outs[0][g * capacity + j] = template[strip_rows_at(found[j], template.shape[0] // strips), :]


def two_of(value, owner, strips):
    lane = lax.broadcasted_iota(jnp.int32, value.shape, 1).astype(F32)
    low = (owner * strips).astype(F32)
    hit = (value >= low) & (value < low + strips)
    key = lane * strips + (value - low)
    first = jnp.min(jnp.where(hit, key, 1024.0)).astype(jnp.int32)
    last = jnp.max(jnp.where(hit, key, 0.0)).astype(jnp.int32)
    return lax.rem(first, jnp.int32(strips)), lax.rem(last, jnp.int32(strips))


def strip_rows_at(strip, strip_rows):
    return pl.ds(pl.multiple_of(strip * strip_rows, strip_rows), strip_rows)


def pick_two_kernel(strips, strip_rows, *refs):
    count = len(refs) // 2
    template = refs[count]
    for code, out in zip(from_order([*refs[:count], None])[1:], refs[count + 1 :]):
        for j, strip in enumerate(two_of(code[...].astype(F32), lax.axis_index("ccd"), strips)):
            out[j] = template[strip_rows_at(strip, strip_rows), :]


def load_kernel(source, target, sem):
    copy = pltpu.make_async_copy(source, target, sem)
    copy.start()
    copy.wait()


def turned(base, first, rows):
    return pltpu.roll(jnp.broadcast_to(base, (rows, base.shape[1])), first, 1, stride=1, stride_axis=0)


def base_row(taps, q, start, sign, size):
    lane = lax.broadcasted_iota(jnp.int32, (1, size), 1)
    value = jnp.zeros((1, size), F32)
    for t in range(TAPS):
        at = lax.rem(start + sign * (t - 2) + size, jnp.int32(size))
        value = jnp.where(lane == at, jnp.broadcast_to(taps[t : t + 1, q : q + 1], (1, size)), value)
    return value


def prepare_kernel(n, capacity, strips, strip_rows, tiles, amp_count, ring, two, coefs_in, shifts_in, fractions_in,
                   bands_in, science_in, row_band_in, after, code, *refs):
    del after
    if two:
        own_code, template, own = refs[:3]
        refs = refs[3:]
    de, forward, backward, spread, gather, science, row_band, coefs, shifts, fractions, bands, sems = refs
    pairs = [(fractions_in, fractions), (shifts_in, shifts), (coefs_in, coefs),
             (bands_in, bands), (row_band_in, row_band), (science_in, science)]
    copies = [pltpu.make_async_copy(source, target, sems.at[i]) for i, (source, target) in enumerate(pairs)]
    for copy in copies:
        copy.start()
    for copy in copies[:2]:
        copy.wait()
    taps = [lanczos_taps(fractions[d : d + 1, :]) for d in range(2)]
    me = lax.axis_index("ccd")
    band, slots = strips * strip_rows, n * capacity
    size = slots * strip_rows
    if slots != strips:
        backward[...] = jnp.zeros(backward.shape, BF16)
    forward_lane = lax.broadcasted_iota(jnp.int32, (strip_rows, size), 1)
    backward_lane = lax.broadcasted_iota(jnp.int32, (strip_rows, band), 1)
    for q, slot in enumerate(slots_of(code, me, strips, capacity, n, ring)):
        low, high = slot * strip_rows, q * strip_rows
        value = turned(base_row(taps[0], q, low + shifts[0, q], 1, size), 0, strip_rows)
        value = jnp.where((forward_lane >= low) & (forward_lane < low + strip_rows), value, 0.0)
        forward[high : high + strip_rows, :] = value.astype(BF16)
        value = turned(base_row(taps[0], q, high - shifts[0, q], -1, band), 0, strip_rows)
        value = jnp.where((backward_lane >= high) & (backward_lane < high + strip_rows), value, 0.0)
        backward[strip_rows_at(slot, strip_rows), :] = value.astype(BF16)

    if two:
        for j, strip in enumerate(two_of(own_code[...].astype(F32), me, strips)):
            own[j] = template[strip_rows_at(strip, strip_rows), :]

    rows = 160
    away = lax.broadcasted_iota(jnp.int32, (rows, LANES), 0) - lane_index(rows)
    for out, low, centre, sign in ((spread, 48, HALF_TILE, -1), (gather, 112, LANES, 1)):
        within = (away >= centre - low - 8) & (away <= centre - low + 8)
        end = out.shape[1]
        for q in range(strips):
            start = (low - centre) + sign * shifts[1, q] + LANES
            value = turned(base_row(taps[1], q, start, sign, LANES), 0, rows)
            out[q, 0:low, :] = jnp.zeros((low, LANES), BF16)
            out[q, low : low + rows, :] = jnp.where(within, value, 0.0).astype(BF16)
            out[q, low + rows : end, :] = jnp.zeros((end - low - rows, LANES), BF16)
    for copy in copies[2:4]:
        copy.wait()
    amp = lax.axis_index("amp")
    width = tiles * LANES
    rows = 80
    for half in range(2):
        low = half * LANES + (0 if half else LANES - rows)
        for first in range(KINDS):
            at = (half * KINDS + first) * LANES
            band_rows = [bands[second, low : low + rows, :].astype(F32) for second in range(KINDS)]
            e = sum(band_rows[b] * coefs[2, 0, first * KINDS + b] for b in range(KINDS)).astype(BF16)
            empty = jnp.zeros((LANES - rows, 2 * LANES), BF16)
            begin = at + (0 if half else LANES - rows)
            for tile in range(tiles):
                column = lane_index(1) + (amp * width + tile * LANES)
                px = (column.astype(F32) + 0.5) / (width * amp_count) * 2.0 - 1.0
                weight = [coefs[0, 0, first * KINDS + b] + coefs[1, 0, first * KINDS + b] * px for b in range(KINDS)]
                d = sum(band_rows[b] * weight[b] for b in range(KINDS)).astype(BF16)
                de[tile, begin : begin + rows, 0:LANES] = d
                de[tile, begin : begin + rows, LANES : 2 * LANES] = e
                hollow = at + (rows if half else 0)
                de[tile, hollow : hollow + LANES - rows, :] = empty
    for copy in copies[4:]:
        copy.wait()


def collect_kernel(n, capacity, strips, strip_rows, ring, two, after, *refs):
    del after
    out = refs[-1]
    me = lax.axis_index("ccd")
    size = n * capacity * strip_rows
    lane = lax.broadcasted_iota(jnp.int32, (1, size), 1)
    named = jnp.full(lane.shape, -1, jnp.int32)
    for g in range(n):
        if two:
            found = two_of(refs[g][...].astype(F32), me, strips)
        else:
            found, total = matches(refs[g if ring else 0], None if ring else g, me, strips, capacity)
            found = [jnp.where(total > j, strip, -1) for j, strip in enumerate(found)]
        for j in range(capacity):
            low = (g * capacity + j) * strip_rows
            named = jnp.where((lane >= low) & (lane < low + strip_rows), found[j], named)
    lane = lax.broadcasted_iota(jnp.int32, (strip_rows, size), 1)
    row = lax.broadcasted_iota(jnp.int32, lane.shape, 0)
    same_row = lax.rem(lane, jnp.int32(strip_rows)) == row
    for p in range(strips):
        value = jnp.where(same_row & (named == p), 1.0, 0.0)
        out[p * strip_rows : (p + 1) * strip_rows, :] = value.astype(BF16)


def clear_ends(ref, tiles):
    zero = jnp.zeros((ref.shape[0], LANES), BF16)
    ref[:, 0:LANES] = zero
    ref[:, (tiles + 1) * LANES : (tiles + 2) * LANES] = zero


def stacked(refs):
    parts = [ref[...].reshape(-1, ref.shape[-1]) for ref in refs]
    return jnp.concatenate(parts, axis=0) if len(parts) > 1 else parts[0]


def warp_kernel(n, strips, strip_rows, tiles, ring, paired, *refs):
    forward, spread = refs[:2]
    count = n if ring else 1
    received, rest = from_order(refs[2 : 2 + count]), refs[2 + count :]
    if paired:
        image, send_row, send_amp, send_diag, rows_done = rest
    else:
        image, rows_done = rest
    width = tiles * LANES
    clear_ends(rows_done, tiles)
    rows_done[:, LANES : LANES + width] = jnp.dot(
        forward[...], stacked(received), preferred_element_type=F32
    ).astype(BF16)
    lane = lane_index(strip_rows)
    for q in range(strips):
        rows = slice(q * strip_rows, (q + 1) * strip_rows)
        windows = [rows_done[rows, b * LANES : (b + 2) * LANES] for b in range(tiles + 1)]
        result = jnp.dot(jnp.concatenate(windows, axis=0), spread[q], preferred_element_type=F32)
        for b in range(tiles + 1):
            value = result[b * strip_rows : (b + 1) * strip_rows]
            if b == 0:
                value = jnp.where(lane < HALF_TILE, 0.0, value)
            if b == tiles:
                value = jnp.where(lane < HALF_TILE, value, 0.0)
            image[rows, b * LANES : (b + 1) * LANES] = value.astype(BF16)
    if paired:
        band = strips * strip_rows
        row_first = lax.axis_index("row") == 0
        amp_first = lax.axis_index("amp") == 0
        edge_rows = jnp.where(row_first, image[band - MARGIN : band, :], image[0:MARGIN, :])
        send_row[...] = edge_rows
        send_amp[...] = jnp.where(amp_first, image[:, tiles * LANES :], image[:, 0:LANES])
        send_diag[...] = jnp.where(amp_first, edge_rows[:, tiles * LANES :], edge_rows[:, 0:LANES])


def joined(ref, rows, left, right, tiles, amp_count):
    amp = lax.axis_index("amp")
    zero = jnp.zeros((), BF16)
    first = ref[rows, 0:LANES] + jnp.where(amp > 0, left, zero)
    last = ref[rows, tiles * LANES :] + jnp.where(amp < amp_count - 1, right, zero)
    return [first] + [ref[rows, b * LANES : (b + 1) * LANES] for b in range(1, tiles)] + [last]


def row_convolved(bands, parts, across, at, count):
    for low in range(0, len(parts), 2):
        window = jnp.concatenate(parts[low : low + 2], axis=1)
        result = jnp.dot(bands, window, preferred_element_type=F32)
        for b in range(low, min(low + 2, len(parts))):
            for kind in range(KINDS):
                piece = result[kind * count : (kind + 1) * count, (b - low) * LANES : (b - low + 1) * LANES]
                across[at : at + count, (b * KINDS + kind) * LANES : (b * KINDS + kind + 1) * LANES] = piece.astype(BF16)


def columns_returned(lowered, columns, at, gather, strip_rows, tiles):
    rows = slice(at, at + strip_rows)
    windows = [lowered[rows, b * LANES : (b + 3) * LANES] for b in range(tiles)]
    result = jnp.dot(jnp.concatenate(windows, axis=0), gather, preferred_element_type=F32)
    for b in range(tiles):
        columns[rows, b * LANES : (b + 1) * LANES] = result[b * strip_rows : (b + 1) * strip_rows].astype(BF16)


def subtracted(science, across, de, store, count, tiles, place):
    for b in range(tiles):
        acc = jnp.dot(
            across[:, b * KINDS * LANES : (b + 2) * KINDS * LANES], de[b], preferred_element_type=F32
        )
        store(b, science(b) - (acc[:, 0:LANES] + place * acc[:, LANES:]))


def row_place(first, count, band, row_count):
    row = lax.broadcasted_iota(jnp.int32, (count, LANES), 0) + (lax.axis_index("row") * band + first)
    return (row.astype(F32) + 0.5) / (band * row_count) * 2.0 - 1.0


def mid_kernel(strips, strip_rows, tiles, row_count, amp_count, image, left, right, science, de, bands, gather,
               diff, columns, across, lowered):
    band = strips * strip_rows
    count = band - 2 * strip_rows
    rows = slice(strip_rows - MARGIN, band - strip_rows + MARGIN)
    parts = joined(image, rows, left[rows, :], right[rows, :], tiles, amp_count)
    row_convolved(bands[...], parts, across, 0, count)
    clear_ends(lowered, tiles)

    def store(b, value):
        diff[:, b * LANES : (b + 1) * LANES] = value
        lowered[:, (b + 1) * LANES : (b + 2) * LANES] = value.astype(BF16)

    subtracted(
        lambda b: science[strip_rows : strip_rows + count, b * LANES : (b + 1) * LANES],
        across, de, store, count, tiles, row_place(strip_rows, count, band, row_count),
    )
    for q in range(1, strips - 1):
        columns_returned(lowered, columns, (q - 1) * strip_rows, gather[q], strip_rows, tiles)


def edge_kernel(n, capacity, strips, strip_rows, tiles, row_count, amp_count, ring, image, left, right, top, bottom,
                top_left, top_right, bottom_left, bottom_right, science, de, bands, backward, gather,
                columns_mid, diff, *rest):
    outs = rest[: n if ring else 1]
    across, lowered, columns = rest[len(outs) :]
    band = strips * strip_rows
    inner = strip_rows + MARGIN
    row = lax.axis_index("row")
    zero = jnp.zeros((), BF16)
    everything = slice(0, MARGIN)
    above = [jnp.where(row > 0, part, zero)
             for part in joined(top, everything, top_left[...], top_right[...], tiles, amp_count)]
    below = [jnp.where(row < row_count - 1, part, zero)
             for part in joined(bottom, everything, bottom_left[...], bottom_right[...], tiles, amp_count)]
    first, last = slice(0, inner), slice(band - inner, band)
    upper = joined(image, first, left[first, :], right[first, :], tiles, amp_count)
    lower = joined(image, last, left[last, :], right[last, :], tiles, amp_count)
    row_convolved(bands[...], [jnp.concatenate(p, axis=0) for p in zip(above, upper)], across, 0, strip_rows)
    row_convolved(bands[...], [jnp.concatenate(p, axis=0) for p in zip(lower, below)], across, strip_rows, strip_rows)

    def store(b, value):
        at = slice(b * LANES, (b + 1) * LANES)
        diff[:, at] = value
        lowered[:, (b + 1) * LANES : (b + 2) * LANES] = value.astype(BF16)

    clear_ends(lowered, tiles)

    def edge_science(b):
        at = slice(b * LANES, (b + 1) * LANES)
        return jnp.concatenate([science[0:strip_rows, at], science[band - strip_rows : band, at]], axis=0)

    place = jnp.concatenate([row_place(0, strip_rows, band, row_count),
                             row_place(band - strip_rows, strip_rows, band, row_count)], axis=0)
    subtracted(edge_science, across, de, store, 2 * strip_rows, tiles, place)
    columns_returned(lowered, columns, 0, gather[0], strip_rows, tiles)
    columns_returned(lowered, columns, strip_rows, gather[strips - 1], strip_rows, tiles)
    whole = jnp.concatenate([columns[:strip_rows, :], columns_mid[...], columns[strip_rows:, :]], axis=0)
    result = jnp.dot(backward[...], whole, preferred_element_type=F32).astype(BF16)
    size = capacity * strip_rows * (1 if ring else n)
    for g, out in enumerate(outs):
        out[...] = result[g * size : (g + 1) * size].reshape(out.shape)


def sum_kernel(collect, *refs):
    *returned, stack, total, sems = refs
    values = stacked(from_order(returned))
    copies = []
    half = total.shape[0] // 2
    for i in range(2):
        rows = pl.ds(i * half, half)
        total[rows, :] = jnp.dot(collect[rows, :], values, preferred_element_type=F32)
        copy = pltpu.make_async_copy(total.at[rows], stack.at[rows], sems.at[i])
        copy.start()
        copies.append(copy)
    for copy in copies:
        copy.wait()


def body(science, template, owners, patch_strip, shifts, fractions, coefs):
    n = lax.axis_size("ccd")
    row_count = lax.axis_size("row")
    amp_count = lax.axis_size("amp")
    band, width = science.shape[1:]
    strips, strip_rows = template.shape[3:5]
    capacity = max(2, strips // n)
    tiles = width // LANES
    padded = width + LANES
    ring = n <= 4
    two = ring and capacity == 2 and strips == 2 * n
    paired = row_count == 2 and amp_count == 2
    swap = [(0, 1), (1, 0)]
    strip_shape = (capacity, strip_rows, width)

    def call(kernel, out_shape, operands, spaces, scratch=(), megabytes=8):
        shapes = [jax.ShapeDtypeStruct(*s) if isinstance(s, tuple) else s for s in out_shape]
        return pl.pallas_call(
            kernel,
            out_shape=shapes,
            in_specs=list(spaces),
            out_specs=[VMEM if isinstance(s, tuple) else HBM for s in out_shape],
            scratch_shapes=[pltpu.VMEM(*s) if isinstance(s, tuple) else s for s in scratch],
            compiler_params=pltpu.CompilerParams(vmem_limit_bytes=megabytes << 20),
            cost_estimate=pl.CostEstimate(flops=0, bytes_accessed=1 << 20, transcendentals=0),
        )(*operands)

    def turn(value, g):
        return lax.ppermute(value, "ccd", [(i, (i + g) % n) for i in range(n)])

    def exchange(parts, sign):
        if not ring:
            return [lax.all_to_all(parts[0], "ccd", split_axis=0, concat_axis=0, tiled=True)]
        return [parts[0]] + [turn(parts[g], sign * g) for g in range(1, n)]

    code = owners.reshape(1, strips) * strips + patch_strip.reshape(1, strips)
    (template_rows,) = call(
        load_kernel,
        [((band, width), BF16)],
        [in_hbm(template.reshape(band, width))],
        [HBM],
        [pltpu.SemaphoreType.DMA],
    )

    if two:
        codes = exchange([code] * n, 1)
        picked = call(
            functools.partial(pick_two_kernel, strips, strip_rows),
            [(strip_shape, BF16)] * (n - 1),
            [*in_order(codes)[:-1], template_rows],
            [VMEM] * n,
        )
    elif ring:
        codes = exchange([code.reshape(strips)] * n, 1)
        picked_shapes = [(strip_shape, BF16)] * n
    else:
        codes = [lax.all_gather(code.reshape(strips), "ccd", axis=0, tiled=True)]
        picked_shapes = [((n * capacity, strip_rows, width), BF16)]
    if not two:
        picked = call(
            functools.partial(pick_kernel, n, capacity, strips, ring),
            picked_shapes,
            [*codes, template_rows],
            [SMEM] * len(codes) + [VMEM],
        )
    mid_rows = band - 2 * strip_rows
    mid_bands = jnp.asarray(row_bands(mid_rows))
    slot_rows = n * capacity * strip_rows
    *own, de, forward, backward, spread, gather, science, mid_bands = call(
        functools.partial(prepare_kernel, n, capacity, strips, strip_rows, tiles, amp_count, ring, two),
        ([(strip_shape, BF16)] if two else []) + [
            ((tiles, 2 * KINDS * LANES, 2 * LANES), BF16),
            ((band, slot_rows), BF16),
            ((slot_rows, band), BF16),
            ((strips, 2 * LANES, LANES), BF16),
            ((strips, 3 * LANES, LANES), BF16),
            ((band, width), F32),
            (mid_bands.shape, BF16),
        ],
        [in_hbm(value) for value in (
            coefs.transpose(1, 0, 2), shifts.reshape(2, strips), fractions.reshape(2, strips),
            jnp.asarray(column_bands()), science.reshape(band, width), mid_bands)]
        + [picked[-1], code] + ([code, template_rows] if two else []),
        [HBM] * 6 + [VMEM, SMEM] + [VMEM] * (2 if two else 0),
        [pltpu.SMEM((3, 1, 9), F32), pltpu.SMEM((2, strips), jnp.int32),
         ((2, strips), F32), ((KINDS, 2 * LANES, LANES), BF16), pltpu.SemaphoreType.DMA((6,))],
        megabytes=10,
    )
    if two:
        received = in_order(exchange([*own, *picked], -1))
    else:
        received = in_order(exchange(picked, -1))
    image_shape = ((band, padded), BF16)
    halo_shapes = [((MARGIN, padded), BF16), ((band, LANES), BF16), ((MARGIN, LANES), BF16)]
    warped = call(
        functools.partial(warp_kernel, n, strips, strip_rows, tiles, ring, paired),
        [image_shape] + (halo_shapes if paired else []),
        [forward, spread, *received],
        [VMEM] * (2 + len(received)),
        [((band, padded + LANES), BF16)],
    )
    image = warped[0]
    if paired:
        side = lax.ppermute(warped[2], "amp", swap)
        ends = lax.ppermute(warped[1], "row", swap)
        corner = lax.ppermute(warped[3], ("row", "amp"), [(0, 3), (3, 0), (1, 2), (2, 1)])
        left = right = side
        top = bottom = ends
        top_left = top_right = bottom_left = bottom_right = corner
    else:
        first, last = image[:MARGIN], image[band - MARGIN :]

        def moved(value, down, along):
            pairs = []
            for r in range(row_count):
                for a in range(amp_count):
                    if 0 <= r + down < row_count and 0 <= a + along < amp_count:
                        pairs.append((r * amp_count + a, (r + down) * amp_count + a + along))
            return lax.ppermute(value, ("row", "amp"), pairs)

        left = moved(image[:, padded - LANES :], 0, 1)
        right = moved(image[:, :LANES], 0, -1)
        top, bottom = moved(last, 1, 0), moved(first, -1, 0)
        top_left = moved(last[:, padded - LANES :], 1, 1)
        top_right = moved(last[:, :LANES], 1, -1)
        bottom_left = moved(first[:, padded - LANES :], -1, 1)
        bottom_right = moved(first[:, :LANES], -1, -1)

    diff_mid, columns_mid = call(
        functools.partial(mid_kernel, strips, strip_rows, tiles, row_count, amp_count),
        [((mid_rows, width), F32), ((mid_rows, width), BF16)],
        [image, left, right, science, de, mid_bands, gather],
        [VMEM] * 7,
        [((mid_rows, (tiles + 1) * KINDS * LANES), BF16), ((mid_rows, padded + LANES), BF16)],
    )
    outgoing_shapes = [(strip_shape, BF16)] * n if ring else [((n * capacity, strip_rows, width), BF16)]
    diff_edge, *outgoing = call(
        functools.partial(edge_kernel, n, capacity, strips, strip_rows, tiles, row_count, amp_count, ring),
        [((2 * strip_rows, width), F32)] + outgoing_shapes,
        [image, left, right, top, bottom, top_left, top_right, bottom_left, bottom_right, science, de,
         jnp.asarray(row_bands(strip_rows)), backward, gather, columns_mid],
        [VMEM] * 15,
        [((2 * strip_rows, (tiles + 1) * KINDS * LANES), BF16), ((2 * strip_rows, padded + LANES), BF16),
         ((2 * strip_rows, width), BF16)],
    )
    returned = in_order(exchange(outgoing, 1))
    (collect,) = call(
        functools.partial(collect_kernel, n, capacity, strips, strip_rows, ring, two),
        [((band, slot_rows), BF16)],
        [outgoing[0], *codes],
        [VMEM] + [VMEM if two else SMEM] * len(codes),
    )
    (stack,) = call(
        sum_kernel,
        [pltpu.HBM((band, width), F32)],
        [collect, *returned],
        [VMEM] * (1 + len(returned)),
        [((band, width), F32), pltpu.SemaphoreType.DMA((2,))],
    )
    difference = jnp.concatenate([diff_edge[:strip_rows], diff_mid, diff_edge[strip_rows:]])
    return difference[None], stack.reshape(template.shape)


def solution(mesh):
    return jax.shard_map(
        body,
        mesh=mesh,
        in_specs=(
            P(("grp", "ccd"), "row", "amp"),
            P(("grp", "ccd"), "row", "amp", None, None, None),
            P(("grp", "ccd"), "row", "amp", None, None),
            P(("grp", "ccd"), "row", "amp", None),
            P(("grp", "ccd"), "row", "amp", None, None),
            P(("grp", "ccd"), "row", "amp", None, None),
            P(("grp", "ccd"), None, None),
        ),
        out_specs=(
            P(("grp", "ccd"), "row", "amp"),
            P(("grp", "ccd"), "row", "amp", None, None, None),
        ),
        check_vma=False,
    )
```

```python
import functools

import jax
import jax.numpy as jnp
import ml_dtypes
import numpy as np
from jax import lax
from jax.experimental import pallas as pl
from jax.experimental.pallas import tpu as pltpu
from jax.sharding import PartitionSpec as P

RADIUS = 9
LANES = 128
HALF_TILE = 64
MARGIN = 16
TAPS = 6
KINDS = 3

F32 = jnp.float32
BF16 = jnp.bfloat16
SMEM = pl.BlockSpec(memory_space=pltpu.SMEM)
VMEM = pl.BlockSpec(memory_space=pltpu.VMEM)
HBM = pl.BlockSpec(memory_space=pltpu.HBM)


def kernel_table():
    support = np.arange(-RADIUS, RADIUS + 1).astype(np.float32)
    narrow = np.exp(-support * support / np.float32(4.5))
    slope = support * np.exp(-support * support / np.float32(12.5))
    broad = np.exp(-support * support / np.float32(40.5))
    table = np.stack([narrow / narrow.sum(), slope / np.abs(slope).sum(), broad / broad.sum()])
    return table.astype(ml_dtypes.bfloat16)


def column_bands():
    table = kernel_table()
    source = np.arange(2 * LANES)[:, None]
    target = np.arange(LANES)[None, :]
    place = source - HALF_TILE - target + RADIUS
    inside = (place >= 0) & (place <= 2 * RADIUS)
    return np.stack(
        [np.where(inside, row[np.clip(place, 0, 2 * RADIUS)], 0) for row in table]
    ).astype(ml_dtypes.bfloat16)


def row_bands(count):
    table = kernel_table()
    source = np.arange(count + 2 * MARGIN)[None, :]
    target = np.arange(count)[:, None]
    place = source - MARGIN - target + RADIUS
    inside = (place >= 0) & (place <= 2 * RADIUS)
    return np.concatenate(
        [np.where(inside, row[np.clip(place, 0, 2 * RADIUS)], 0) for row in table]
    ).astype(ml_dtypes.bfloat16)


def sinc(value):
    turn = jnp.pi * value
    return jnp.where(value == 0.0, 1.0, jnp.sin(turn) / jnp.where(value == 0.0, 1.0, turn))


def lanczos_taps(fraction):
    place = lax.broadcasted_iota(jnp.int32, (8, fraction.shape[1]), 0) - 2
    spread = place.astype(F32) - fraction
    return (sinc(spread) * sinc(spread / 3.0)).astype(BF16).astype(F32)


def in_hbm(value):
    return pltpu.with_memory_space_constraint(value, pltpu.HBM)


def lane_index(rows):
    return lax.broadcasted_iota(jnp.int32, (rows, LANES), 1)


def order_of(n):
    return (2, 3, 1, 0) if n == 4 else (*range(1, n), 0)


def in_order(values):
    return [values[g] for g in order_of(len(values))]


def from_order(values):
    order = order_of(len(values))
    return [values[order.index(g)] for g in range(len(values))]


def matches(code_ref, group, me, strips, capacity):
    found, count = [jnp.int32(0)] * capacity, jnp.int32(0)
    for q in range(strips):
        code = code_ref[group * strips + q] if group is not None else code_ref[q]
        hit = lax.div(code, jnp.int32(strips)) == me
        strip = lax.rem(code, jnp.int32(strips))
        found = [jnp.where(hit & (count == j), strip, f) for j, f in enumerate(found)]
        count = count + hit.astype(jnp.int32)
    return found, count


def slots_of(code_ref, me, strips, capacity, n, ring):
    owners = [lax.div(code_ref[0, q], jnp.int32(strips)) for q in range(strips)]
    slots = []
    for q in range(strips):
        rank = jnp.int32(0)
        for p in range(q):
            rank = rank + (owners[p] == owners[q]).astype(jnp.int32)
        group = lax.rem(owners[q] - me + n, jnp.int32(n)) if ring else owners[q]
        slots.append(group * capacity + rank)
    return slots


def pick_kernel(n, capacity, strips, ring, *refs):
    if ring:
        codes, template, outs = refs[:n], refs[n], refs[n + 1 :]
    else:
        codes, template, outs = [refs[0]] * n, refs[1], refs[2:]
    me = lax.axis_index("ccd")
    for g in range(n):
        found, _ = matches(codes[g], None if ring else g, me, strips, capacity)
        for j in range(capacity):
            if ring:
                outs[g][j] = template[strip_rows_at(found[j], template.shape[0] // strips), :]
            else:
                outs[0][g * capacity + j] = template[strip_rows_at(found[j], template.shape[0] // strips), :]


def two_of(value, owner, strips):
    lane = lax.broadcasted_iota(jnp.int32, value.shape, 1).astype(F32)
    low = (owner * strips).astype(F32)
    hit = (value >= low) & (value < low + strips)
    key = lane * strips + (value - low)
    first = jnp.min(jnp.where(hit, key, 1024.0)).astype(jnp.int32)
    last = jnp.max(jnp.where(hit, key, 0.0)).astype(jnp.int32)
    return lax.rem(first, jnp.int32(strips)), lax.rem(last, jnp.int32(strips))


def strip_rows_at(strip, strip_rows):
    return pl.ds(pl.multiple_of(strip * strip_rows, strip_rows), strip_rows)


def pick_two_kernel(strips, strip_rows, code, template, out):
    for j, strip in enumerate(two_of(code[...].astype(F32), lax.axis_index("ccd"), strips)):
        out[j] = template[strip_rows_at(strip, strip_rows), :]


def load_kernel(source, target, sem):
    copy = pltpu.make_async_copy(source, target, sem)
    copy.start()
    copy.wait()


def turned(base, first, rows):
    return pltpu.roll(jnp.broadcast_to(base, (rows, base.shape[1])), first, 1, stride=1, stride_axis=0)


def base_row(taps, q, start, sign, size):
    lane = lax.broadcasted_iota(jnp.int32, (1, size), 1)
    value = jnp.zeros((1, size), F32)
    for t in range(TAPS):
        at = lax.rem(start + sign * (t - 2) + size, jnp.int32(size))
        value = jnp.where(lane == at, jnp.broadcast_to(taps[t : t + 1, q : q + 1], (1, size)), value)
    return value


def prepare_kernel(n, capacity, strips, strip_rows, tiles, amp_count, ring, two, coefs_in, shifts_in, fractions_in,
                   bands_in, science_in, row_band_in, after, code, *refs):
    del after
    if two:
        own_code, template, own = refs[:3]
        refs = refs[3:]
    de, forward, backward, spread, gather, science, row_band, coefs, shifts, fractions, bands, sems = refs
    pairs = [(fractions_in, fractions), (shifts_in, shifts), (coefs_in, coefs),
             (bands_in, bands), (row_band_in, row_band), (science_in, science)]
    copies = [pltpu.make_async_copy(source, target, sems.at[i]) for i, (source, target) in enumerate(pairs)]
    for copy in copies:
        copy.start()
    for copy in copies[:2]:
        copy.wait()
    taps = [lanczos_taps(fractions[d : d + 1, :]) for d in range(2)]
    me = lax.axis_index("ccd")
    band, slots = strips * strip_rows, n * capacity
    size = slots * strip_rows
    if slots != strips:
        backward[...] = jnp.zeros(backward.shape, BF16)
    forward_lane = lax.broadcasted_iota(jnp.int32, (strip_rows, size), 1)
    backward_lane = lax.broadcasted_iota(jnp.int32, (strip_rows, band), 1)
    for q, slot in enumerate(slots_of(code, me, strips, capacity, n, ring)):
        low, high = slot * strip_rows, q * strip_rows
        value = turned(base_row(taps[0], q, low + shifts[0, q], 1, size), 0, strip_rows)
        value = jnp.where((forward_lane >= low) & (forward_lane < low + strip_rows), value, 0.0)
        forward[high : high + strip_rows, :] = value.astype(BF16)
        value = turned(base_row(taps[0], q, high - shifts[0, q], -1, band), 0, strip_rows)
        value = jnp.where((backward_lane >= high) & (backward_lane < high + strip_rows), value, 0.0)
        backward[strip_rows_at(slot, strip_rows), :] = value.astype(BF16)

    if two:
        for j, strip in enumerate(two_of(own_code[...].astype(F32), me, strips)):
            own[j] = template[strip_rows_at(strip, strip_rows), :]

    rows = 160
    away = lax.broadcasted_iota(jnp.int32, (rows, LANES), 0) - lane_index(rows)
    for out, low, centre, sign in ((spread, 48, HALF_TILE, -1), (gather, 112, LANES, 1)):
        within = (away >= centre - low - 8) & (away <= centre - low + 8)
        end = out.shape[1]
        for q in range(strips):
            start = (low - centre) + sign * shifts[1, q] + LANES
            value = turned(base_row(taps[1], q, start, sign, LANES), 0, rows)
            out[q, 0:low, :] = jnp.zeros((low, LANES), BF16)
            out[q, low : low + rows, :] = jnp.where(within, value, 0.0).astype(BF16)
            out[q, low + rows : end, :] = jnp.zeros((end - low - rows, LANES), BF16)
    for copy in copies[2:4]:
        copy.wait()
    amp = lax.axis_index("amp")
    width = tiles * LANES
    rows = 80
    for half in range(2):
        low = half * LANES + (0 if half else LANES - rows)
        for first in range(KINDS):
            at = (half * KINDS + first) * LANES
            band_rows = [bands[second, low : low + rows, :].astype(F32) for second in range(KINDS)]
            e = sum(band_rows[b] * coefs[2, 0, first * KINDS + b] for b in range(KINDS)).astype(BF16)
            empty = jnp.zeros((LANES - rows, 2 * LANES), BF16)
            begin = at + (0 if half else LANES - rows)
            for tile in range(tiles):
                column = lane_index(1) + (amp * width + tile * LANES)
                px = (column.astype(F32) + 0.5) / (width * amp_count) * 2.0 - 1.0
                weight = [coefs[0, 0, first * KINDS + b] + coefs[1, 0, first * KINDS + b] * px for b in range(KINDS)]
                d = sum(band_rows[b] * weight[b] for b in range(KINDS)).astype(BF16)
                de[tile, begin : begin + rows, 0:LANES] = d
                de[tile, begin : begin + rows, LANES : 2 * LANES] = e
                hollow = at + (rows if half else 0)
                de[tile, hollow : hollow + LANES - rows, :] = empty
    for copy in copies[4:]:
        copy.wait()


def collect_kernel(n, capacity, strips, strip_rows, ring, two, after, *refs):
    del after
    out = refs[-1]
    me = lax.axis_index("ccd")
    size = n * capacity * strip_rows
    lane = lax.broadcasted_iota(jnp.int32, (1, size), 1)
    named = jnp.full(lane.shape, -1, jnp.int32)
    for g in range(n):
        if two:
            found = two_of(refs[g][...].astype(F32), me, strips)
        else:
            found, total = matches(refs[g if ring else 0], None if ring else g, me, strips, capacity)
            found = [jnp.where(total > j, strip, -1) for j, strip in enumerate(found)]
        for j in range(capacity):
            low = (g * capacity + j) * strip_rows
            named = jnp.where((lane >= low) & (lane < low + strip_rows), found[j], named)
    lane = lax.broadcasted_iota(jnp.int32, (strip_rows, size), 1)
    row = lax.broadcasted_iota(jnp.int32, lane.shape, 0)
    same_row = lax.rem(lane, jnp.int32(strip_rows)) == row
    for p in range(strips):
        value = jnp.where(same_row & (named == p), 1.0, 0.0)
        out[p * strip_rows : (p + 1) * strip_rows, :] = value.astype(BF16)


def clear_ends(ref, tiles):
    zero = jnp.zeros((ref.shape[0], LANES), BF16)
    ref[:, 0:LANES] = zero
    ref[:, (tiles + 1) * LANES : (tiles + 2) * LANES] = zero


def stacked(refs):
    parts = [ref[...].reshape(-1, ref.shape[-1]) for ref in refs]
    return jnp.concatenate(parts, axis=0) if len(parts) > 1 else parts[0]


def warp_kernel(n, strips, strip_rows, tiles, ring, paired, *refs):
    forward, spread = refs[:2]
    count = n if ring else 1
    received, rest = from_order(refs[2 : 2 + count]), refs[2 + count :]
    if paired:
        image, send_row, send_amp, send_diag, rows_done = rest
    else:
        image, rows_done = rest
    width = tiles * LANES
    clear_ends(rows_done, tiles)
    rows_done[:, LANES : LANES + width] = jnp.dot(
        forward[...], stacked(received), preferred_element_type=F32
    ).astype(BF16)
    lane = lane_index(strip_rows)
    for q in range(strips):
        rows = slice(q * strip_rows, (q + 1) * strip_rows)
        windows = [rows_done[rows, b * LANES : (b + 2) * LANES] for b in range(tiles + 1)]
        result = jnp.dot(jnp.concatenate(windows, axis=0), spread[q], preferred_element_type=F32)
        for b in range(tiles + 1):
            value = result[b * strip_rows : (b + 1) * strip_rows]
            if b == 0:
                value = jnp.where(lane < HALF_TILE, 0.0, value)
            if b == tiles:
                value = jnp.where(lane < HALF_TILE, value, 0.0)
            image[rows, b * LANES : (b + 1) * LANES] = value.astype(BF16)
    if paired:
        band = strips * strip_rows
        row_first = lax.axis_index("row") == 0
        amp_first = lax.axis_index("amp") == 0
        edge_rows = jnp.where(row_first, image[band - MARGIN : band, :], image[0:MARGIN, :])
        send_row[...] = edge_rows
        send_amp[...] = jnp.where(amp_first, image[:, tiles * LANES :], image[:, 0:LANES])
        send_diag[...] = jnp.where(amp_first, edge_rows[:, tiles * LANES :], edge_rows[:, 0:LANES])


def joined(ref, rows, left, right, tiles, amp_count):
    amp = lax.axis_index("amp")
    zero = jnp.zeros((), BF16)
    first = ref[rows, 0:LANES] + jnp.where(amp > 0, left, zero)
    last = ref[rows, tiles * LANES :] + jnp.where(amp < amp_count - 1, right, zero)
    return [first] + [ref[rows, b * LANES : (b + 1) * LANES] for b in range(1, tiles)] + [last]


def row_convolved(bands, parts, across, at, count):
    for low in range(0, len(parts), 2):
        window = jnp.concatenate(parts[low : low + 2], axis=1)
        result = jnp.dot(bands, window, preferred_element_type=F32)
        for b in range(low, min(low + 2, len(parts))):
            for kind in range(KINDS):
                piece = result[kind * count : (kind + 1) * count, (b - low) * LANES : (b - low + 1) * LANES]
                across[at : at + count, (b * KINDS + kind) * LANES : (b * KINDS + kind + 1) * LANES] = piece.astype(BF16)


def columns_returned(lowered, columns, at, gather, strip_rows, tiles):
    rows = slice(at, at + strip_rows)
    windows = [lowered[rows, b * LANES : (b + 3) * LANES] for b in range(tiles)]
    result = jnp.dot(jnp.concatenate(windows, axis=0), gather, preferred_element_type=F32)
    for b in range(tiles):
        columns[rows, b * LANES : (b + 1) * LANES] = result[b * strip_rows : (b + 1) * strip_rows].astype(BF16)


def subtracted(science, across, de, store, count, tiles, place):
    for b in range(tiles):
        acc = jnp.dot(
            across[:, b * KINDS * LANES : (b + 2) * KINDS * LANES], de[b], preferred_element_type=F32
        )
        store(b, science(b) - (acc[:, 0:LANES] + place * acc[:, LANES:]))


def row_place(first, count, band, row_count):
    row = lax.broadcasted_iota(jnp.int32, (count, LANES), 0) + (lax.axis_index("row") * band + first)
    return (row.astype(F32) + 0.5) / (band * row_count) * 2.0 - 1.0


def mid_kernel(strips, strip_rows, tiles, row_count, amp_count, image, left, right, science, de, bands, gather,
               diff, columns, across, lowered):
    band = strips * strip_rows
    count = band - 2 * strip_rows
    rows = slice(strip_rows - MARGIN, band - strip_rows + MARGIN)
    parts = joined(image, rows, left[rows, :], right[rows, :], tiles, amp_count)
    row_convolved(bands[...], parts, across, 0, count)
    clear_ends(lowered, tiles)

    def store(b, value):
        diff[:, b * LANES : (b + 1) * LANES] = value
        lowered[:, (b + 1) * LANES : (b + 2) * LANES] = value.astype(BF16)

    subtracted(
        lambda b: science[strip_rows : strip_rows + count, b * LANES : (b + 1) * LANES],
        across, de, store, count, tiles, row_place(strip_rows, count, band, row_count),
    )
    for q in range(1, strips - 1):
        columns_returned(lowered, columns, (q - 1) * strip_rows, gather[q], strip_rows, tiles)


def edge_kernel(n, capacity, strips, strip_rows, tiles, row_count, amp_count, ring, image, left, right, top, bottom,
                top_left, top_right, bottom_left, bottom_right, science, de, bands, backward, gather,
                columns_mid, diff, *rest):
    outs = rest[: n if ring else 1]
    across, lowered, columns = rest[len(outs) :]
    band = strips * strip_rows
    inner = strip_rows + MARGIN
    row = lax.axis_index("row")
    zero = jnp.zeros((), BF16)
    everything = slice(0, MARGIN)
    above = [jnp.where(row > 0, part, zero)
             for part in joined(top, everything, top_left[...], top_right[...], tiles, amp_count)]
    below = [jnp.where(row < row_count - 1, part, zero)
             for part in joined(bottom, everything, bottom_left[...], bottom_right[...], tiles, amp_count)]
    first, last = slice(0, inner), slice(band - inner, band)
    upper = joined(image, first, left[first, :], right[first, :], tiles, amp_count)
    lower = joined(image, last, left[last, :], right[last, :], tiles, amp_count)
    row_convolved(bands[...], [jnp.concatenate(p, axis=0) for p in zip(above, upper)], across, 0, strip_rows)
    row_convolved(bands[...], [jnp.concatenate(p, axis=0) for p in zip(lower, below)], across, strip_rows, strip_rows)

    def store(b, value):
        at = slice(b * LANES, (b + 1) * LANES)
        diff[:, at] = value
        lowered[:, (b + 1) * LANES : (b + 2) * LANES] = value.astype(BF16)

    clear_ends(lowered, tiles)

    def edge_science(b):
        at = slice(b * LANES, (b + 1) * LANES)
        return jnp.concatenate([science[0:strip_rows, at], science[band - strip_rows : band, at]], axis=0)

    place = jnp.concatenate([row_place(0, strip_rows, band, row_count),
                             row_place(band - strip_rows, strip_rows, band, row_count)], axis=0)
    subtracted(edge_science, across, de, store, 2 * strip_rows, tiles, place)
    columns_returned(lowered, columns, 0, gather[0], strip_rows, tiles)
    columns_returned(lowered, columns, strip_rows, gather[strips - 1], strip_rows, tiles)
    whole = jnp.concatenate([columns[:strip_rows, :], columns_mid[...], columns[strip_rows:, :]], axis=0)
    result = jnp.dot(backward[...], whole, preferred_element_type=F32).astype(BF16)
    size = capacity * strip_rows * (1 if ring else n)
    for g, out in enumerate(outs):
        out[...] = result[g * size : (g + 1) * size].reshape(out.shape)


def sum_kernel(collect, *refs):
    *returned, stack, total, sems = refs
    values = stacked(from_order(returned))
    copies = []
    half = total.shape[0] // 2
    for i in range(2):
        rows = pl.ds(i * half, half)
        total[rows, :] = jnp.dot(collect[rows, :], values, preferred_element_type=F32)
        copy = pltpu.make_async_copy(total.at[rows], stack.at[rows], sems.at[i])
        copy.start()
        copies.append(copy)
    for copy in copies:
        copy.wait()


def body(science, template, owners, patch_strip, shifts, fractions, coefs):
    n = lax.axis_size("ccd")
    row_count = lax.axis_size("row")
    amp_count = lax.axis_size("amp")
    band, width = science.shape[1:]
    strips, strip_rows = template.shape[3:5]
    capacity = max(2, strips // n)
    tiles = width // LANES
    padded = width + LANES
    ring = n <= 4
    two = ring and capacity == 2 and strips == 2 * n
    paired = row_count == 2 and amp_count == 2
    swap = [(0, 1), (1, 0)]
    strip_shape = (capacity, strip_rows, width)

    def call(kernel, out_shape, operands, spaces, scratch=(), megabytes=8):
        shapes = [jax.ShapeDtypeStruct(*s) if isinstance(s, tuple) else s for s in out_shape]
        return pl.pallas_call(
            kernel,
            out_shape=shapes,
            in_specs=list(spaces),
            out_specs=[VMEM if isinstance(s, tuple) else HBM for s in out_shape],
            scratch_shapes=[pltpu.VMEM(*s) if isinstance(s, tuple) else s for s in scratch],
            compiler_params=pltpu.CompilerParams(vmem_limit_bytes=megabytes << 20),
            cost_estimate=pl.CostEstimate(flops=0, bytes_accessed=1 << 20, transcendentals=0),
        )(*operands)

    def turn(value, g):
        return lax.ppermute(value, "ccd", [(i, (i + g) % n) for i in range(n)])

    def exchange(parts, sign):
        if not ring:
            return [lax.all_to_all(parts[0], "ccd", split_axis=0, concat_axis=0, tiled=True)]
        return [parts[0]] + [turn(parts[g], sign * g) for g in range(1, n)]

    code = owners.reshape(1, strips) * strips + patch_strip.reshape(1, strips)
    (template_rows,) = call(
        load_kernel,
        [((band, width), BF16)],
        [in_hbm(template.reshape(band, width))],
        [HBM],
        [pltpu.SemaphoreType.DMA],
    )

    if two:
        codes = exchange([code] * n, 1)
        picked = [
            call(
                functools.partial(pick_two_kernel, strips, strip_rows),
                [(strip_shape, BF16)],
                [other, template_rows],
                [VMEM] * 2,
            )[0]
            for other in codes[1:]
        ]
    elif ring:
        codes = exchange([code.reshape(strips)] * n, 1)
        picked_shapes = [(strip_shape, BF16)] * n
    else:
        codes = [lax.all_gather(code.reshape(strips), "ccd", axis=0, tiled=True)]
        picked_shapes = [((n * capacity, strip_rows, width), BF16)]
    if not two:
        picked = call(
            functools.partial(pick_kernel, n, capacity, strips, ring),
            picked_shapes,
            [*codes, template_rows],
            [SMEM] * len(codes) + [VMEM],
        )
    mid_rows = band - 2 * strip_rows
    mid_bands = jnp.asarray(row_bands(mid_rows))
    slot_rows = n * capacity * strip_rows
    *own, de, forward, backward, spread, gather, science, mid_bands = call(
        functools.partial(prepare_kernel, n, capacity, strips, strip_rows, tiles, amp_count, ring, two),
        ([(strip_shape, BF16)] if two else []) + [
            ((tiles, 2 * KINDS * LANES, 2 * LANES), BF16),
            ((band, slot_rows), BF16),
            ((slot_rows, band), BF16),
            ((strips, 2 * LANES, LANES), BF16),
            ((strips, 3 * LANES, LANES), BF16),
            ((band, width), F32),
            (mid_bands.shape, BF16),
        ],
        [in_hbm(value) for value in (
            coefs.transpose(1, 0, 2), shifts.reshape(2, strips), fractions.reshape(2, strips),
            jnp.asarray(column_bands()), science.reshape(band, width), mid_bands)]
        + [picked[n // 2 - 1] if two else picked[-1], code] + ([code, template_rows] if two else []),
        [HBM] * 6 + [VMEM, SMEM] + [VMEM] * (2 if two else 0),
        [pltpu.SMEM((3, 1, 9), F32), pltpu.SMEM((2, strips), jnp.int32),
         ((2, strips), F32), ((KINDS, 2 * LANES, LANES), BF16), pltpu.SemaphoreType.DMA((6,))],
        megabytes=10,
    )
    if two:
        received = in_order(exchange([*own, *picked], -1))
    else:
        received = in_order(exchange(picked, -1))
    image_shape = ((band, padded), BF16)
    halo_shapes = [((MARGIN, padded), BF16), ((band, LANES), BF16), ((MARGIN, LANES), BF16)]
    warped = call(
        functools.partial(warp_kernel, n, strips, strip_rows, tiles, ring, paired),
        [image_shape] + (halo_shapes if paired else []),
        [forward, spread, *received],
        [VMEM] * (2 + len(received)),
        [((band, padded + LANES), BF16)],
    )
    image = warped[0]
    if paired:
        side = lax.ppermute(warped[2], "amp", swap)
        ends = lax.ppermute(warped[1], "row", swap)
        corner = lax.ppermute(warped[3], ("row", "amp"), [(0, 3), (3, 0), (1, 2), (2, 1)])
        left = right = side
        top = bottom = ends
        top_left = top_right = bottom_left = bottom_right = corner
    else:
        first, last = image[:MARGIN], image[band - MARGIN :]

        def moved(value, down, along):
            pairs = []
            for r in range(row_count):
                for a in range(amp_count):
                    if 0 <= r + down < row_count and 0 <= a + along < amp_count:
                        pairs.append((r * amp_count + a, (r + down) * amp_count + a + along))
            return lax.ppermute(value, ("row", "amp"), pairs)

        left = moved(image[:, padded - LANES :], 0, 1)
        right = moved(image[:, :LANES], 0, -1)
        top, bottom = moved(last, 1, 0), moved(first, -1, 0)
        top_left = moved(last[:, padded - LANES :], 1, 1)
        top_right = moved(last[:, :LANES], 1, -1)
        bottom_left = moved(first[:, padded - LANES :], -1, 1)
        bottom_right = moved(first[:, :LANES], -1, -1)

    diff_mid, columns_mid = call(
        functools.partial(mid_kernel, strips, strip_rows, tiles, row_count, amp_count),
        [((mid_rows, width), F32), ((mid_rows, width), BF16)],
        [image, left, right, science, de, mid_bands, gather],
        [VMEM] * 7,
        [((mid_rows, (tiles + 1) * KINDS * LANES), BF16), ((mid_rows, padded + LANES), BF16)],
    )
    outgoing_shapes = [(strip_shape, BF16)] * n if ring else [((n * capacity, strip_rows, width), BF16)]
    diff_edge, *outgoing = call(
        functools.partial(edge_kernel, n, capacity, strips, strip_rows, tiles, row_count, amp_count, ring),
        [((2 * strip_rows, width), F32)] + outgoing_shapes,
        [image, left, right, top, bottom, top_left, top_right, bottom_left, bottom_right, science, de,
         jnp.asarray(row_bands(strip_rows)), backward, gather, columns_mid],
        [VMEM] * 15,
        [((2 * strip_rows, (tiles + 1) * KINDS * LANES), BF16), ((2 * strip_rows, padded + LANES), BF16),
         ((2 * strip_rows, width), BF16)],
    )
    returned = in_order(exchange(outgoing, 1))
    (collect,) = call(
        functools.partial(collect_kernel, n, capacity, strips, strip_rows, ring, two),
        [((band, slot_rows), BF16)],
        [outgoing[0], *codes],
        [VMEM] + [VMEM if two else SMEM] * len(codes),
    )
    (stack,) = call(
        sum_kernel,
        [pltpu.HBM((band, width), F32)],
        [collect, *returned],
        [VMEM] * (1 + len(returned)),
        [((band, width), F32), pltpu.SemaphoreType.DMA((2,))],
    )
    difference = jnp.concatenate([diff_edge[:strip_rows], diff_mid, diff_edge[strip_rows:]])
    return difference[None], stack.reshape(template.shape)


def solution(mesh):
    return jax.shard_map(
        body,
        mesh=mesh,
        in_specs=(
            P(("grp", "ccd"), "row", "amp"),
            P(("grp", "ccd"), "row", "amp", None, None, None),
            P(("grp", "ccd"), "row", "amp", None, None),
            P(("grp", "ccd"), "row", "amp", None),
            P(("grp", "ccd"), "row", "amp", None, None),
            P(("grp", "ccd"), "row", "amp", None, None),
            P(("grp", "ccd"), None, None),
        ),
        out_specs=(
            P(("grp", "ccd"), "row", "amp"),
            P(("grp", "ccd"), "row", "amp", None, None, None),
        ),
        check_vma=False,
    )
```

```python
import functools

import jax
import jax.numpy as jnp
import ml_dtypes
import numpy as np
from jax import lax
from jax.experimental import pallas as pl
from jax.experimental.pallas import tpu as pltpu
from jax.sharding import PartitionSpec as P

RADIUS = 9
LANES = 128
HALF_TILE = 64
MARGIN = 16
TAPS = 6
KINDS = 3

F32 = jnp.float32
BF16 = jnp.bfloat16
SMEM = pl.BlockSpec(memory_space=pltpu.SMEM)
VMEM = pl.BlockSpec(memory_space=pltpu.VMEM)
HBM = pl.BlockSpec(memory_space=pltpu.HBM)


def kernel_table():
    support = np.arange(-RADIUS, RADIUS + 1).astype(np.float32)
    narrow = np.exp(-support * support / np.float32(4.5))
    slope = support * np.exp(-support * support / np.float32(12.5))
    broad = np.exp(-support * support / np.float32(40.5))
    table = np.stack([narrow / narrow.sum(), slope / np.abs(slope).sum(), broad / broad.sum()])
    return table.astype(ml_dtypes.bfloat16)


def column_bands():
    table = kernel_table()
    source = np.arange(2 * LANES)[:, None]
    target = np.arange(LANES)[None, :]
    place = source - HALF_TILE - target + RADIUS
    inside = (place >= 0) & (place <= 2 * RADIUS)
    return np.stack(
        [np.where(inside, row[np.clip(place, 0, 2 * RADIUS)], 0) for row in table]
    ).astype(ml_dtypes.bfloat16)


def row_bands(count):
    table = kernel_table()
    source = np.arange(count + 2 * MARGIN)[None, :]
    target = np.arange(count)[:, None]
    place = source - MARGIN - target + RADIUS
    inside = (place >= 0) & (place <= 2 * RADIUS)
    return np.concatenate(
        [np.where(inside, row[np.clip(place, 0, 2 * RADIUS)], 0) for row in table]
    ).astype(ml_dtypes.bfloat16)


def sinc(value):
    turn = jnp.pi * value
    return jnp.where(value == 0.0, 1.0, jnp.sin(turn) / jnp.where(value == 0.0, 1.0, turn))


def lanczos_taps(fraction):
    place = lax.broadcasted_iota(jnp.int32, (8, fraction.shape[1]), 0) - 2
    spread = place.astype(F32) - fraction
    return (sinc(spread) * sinc(spread / 3.0)).astype(BF16).astype(F32)


def in_hbm(value):
    return pltpu.with_memory_space_constraint(value, pltpu.HBM)


def lane_index(rows):
    return lax.broadcasted_iota(jnp.int32, (rows, LANES), 1)


def order_of(n):
    return (1, 3, 2, 0) if n == 4 else (*range(1, n), 0)


def in_order(values):
    return [values[g] for g in order_of(len(values))]


def from_order(values):
    order = order_of(len(values))
    return [values[order.index(g)] for g in range(len(values))]


def matches(code_ref, group, me, strips, capacity):
    found, count = [jnp.int32(0)] * capacity, jnp.int32(0)
    for q in range(strips):
        code = code_ref[group * strips + q] if group is not None else code_ref[q]
        hit = lax.div(code, jnp.int32(strips)) == me
        strip = lax.rem(code, jnp.int32(strips))
        found = [jnp.where(hit & (count == j), strip, f) for j, f in enumerate(found)]
        count = count + hit.astype(jnp.int32)
    return found, count


def slots_of(code_ref, me, strips, capacity, n, ring):
    owners = [lax.div(code_ref[0, q], jnp.int32(strips)) for q in range(strips)]
    slots = []
    for q in range(strips):
        rank = jnp.int32(0)
        for p in range(q):
            rank = rank + (owners[p] == owners[q]).astype(jnp.int32)
        group = lax.rem(owners[q] - me + n, jnp.int32(n)) if ring else owners[q]
        slots.append(group * capacity + rank)
    return slots


def pick_kernel(n, capacity, strips, ring, *refs):
    if ring:
        codes, template, outs = refs[:n], refs[n], refs[n + 1 :]
    else:
        codes, template, outs = [refs[0]] * n, refs[1], refs[2:]
    me = lax.axis_index("ccd")
    for g in range(n):
        found, _ = matches(codes[g], None if ring else g, me, strips, capacity)
        for j in range(capacity):
            if ring:
                outs[g][j] = template[strip_rows_at(found[j], template.shape[0] // strips), :]
            else:
                outs[0][g * capacity + j] = template[strip_rows_at(found[j], template.shape[0] // strips), :]


def two_of(value, owner, strips):
    lane = lax.broadcasted_iota(jnp.int32, value.shape, 1).astype(F32)
    low = (owner * strips).astype(F32)
    hit = (value >= low) & (value < low + strips)
    key = lane * strips + (value - low)
    first = jnp.min(jnp.where(hit, key, 1024.0)).astype(jnp.int32)
    last = jnp.max(jnp.where(hit, key, 0.0)).astype(jnp.int32)
    return lax.rem(first, jnp.int32(strips)), lax.rem(last, jnp.int32(strips))


def strip_rows_at(strip, strip_rows):
    return pl.ds(pl.multiple_of(strip * strip_rows, strip_rows), strip_rows)


def pick_two_kernel(strips, strip_rows, code, template, out):
    for j, strip in enumerate(two_of(code[...].astype(F32), lax.axis_index("ccd"), strips)):
        out[j] = template[strip_rows_at(strip, strip_rows), :]


def load_kernel(source, target, sem):
    copy = pltpu.make_async_copy(source, target, sem)
    copy.start()
    copy.wait()


def turned(base, first, rows):
    return pltpu.roll(jnp.broadcast_to(base, (rows, base.shape[1])), first, 1, stride=1, stride_axis=0)


def base_row(taps, q, start, sign, size):
    lane = lax.broadcasted_iota(jnp.int32, (1, size), 1)
    value = jnp.zeros((1, size), F32)
    for t in range(TAPS):
        at = lax.rem(start + sign * (t - 2) + size, jnp.int32(size))
        value = jnp.where(lane == at, jnp.broadcast_to(taps[t : t + 1, q : q + 1], (1, size)), value)
    return value


def prepare_kernel(n, capacity, strips, strip_rows, tiles, amp_count, ring, two, coefs_in, shifts_in, fractions_in,
                   bands_in, science_in, row_band_in, after, code, *refs):
    del after
    if two:
        own_code, template, own = refs[:3]
        refs = refs[3:]
    de, forward, backward, spread, gather, science, row_band, coefs, shifts, fractions, bands, sems = refs
    pairs = [(fractions_in, fractions), (shifts_in, shifts), (coefs_in, coefs),
             (bands_in, bands), (row_band_in, row_band), (science_in, science)]
    copies = [pltpu.make_async_copy(source, target, sems.at[i]) for i, (source, target) in enumerate(pairs)]
    for copy in copies:
        copy.start()
    for copy in copies[:2]:
        copy.wait()
    taps = [lanczos_taps(fractions[d : d + 1, :]) for d in range(2)]
    me = lax.axis_index("ccd")
    band, slots = strips * strip_rows, n * capacity
    size = slots * strip_rows
    if slots != strips:
        backward[...] = jnp.zeros(backward.shape, BF16)
    forward_lane = lax.broadcasted_iota(jnp.int32, (strip_rows, size), 1)
    backward_lane = lax.broadcasted_iota(jnp.int32, (strip_rows, band), 1)
    for q, slot in enumerate(slots_of(code, me, strips, capacity, n, ring)):
        low, high = slot * strip_rows, q * strip_rows
        value = turned(base_row(taps[0], q, low + shifts[0, q], 1, size), 0, strip_rows)
        value = jnp.where((forward_lane >= low) & (forward_lane < low + strip_rows), value, 0.0)
        forward[high : high + strip_rows, :] = value.astype(BF16)
        value = turned(base_row(taps[0], q, high - shifts[0, q], -1, band), 0, strip_rows)
        value = jnp.where((backward_lane >= high) & (backward_lane < high + strip_rows), value, 0.0)
        backward[strip_rows_at(slot, strip_rows), :] = value.astype(BF16)

    if two:
        for j, strip in enumerate(two_of(own_code[...].astype(F32), me, strips)):
            own[j] = template[strip_rows_at(strip, strip_rows), :]

    rows = 160
    away = lax.broadcasted_iota(jnp.int32, (rows, LANES), 0) - lane_index(rows)
    for out, low, centre, sign in ((spread, 48, HALF_TILE, -1), (gather, 112, LANES, 1)):
        within = (away >= centre - low - 8) & (away <= centre - low + 8)
        end = out.shape[1]
        for q in range(strips):
            start = (low - centre) + sign * shifts[1, q] + LANES
            value = turned(base_row(taps[1], q, start, sign, LANES), 0, rows)
            out[q, 0:low, :] = jnp.zeros((low, LANES), BF16)
            out[q, low : low + rows, :] = jnp.where(within, value, 0.0).astype(BF16)
            out[q, low + rows : end, :] = jnp.zeros((end - low - rows, LANES), BF16)
    for copy in copies[2:4]:
        copy.wait()
    amp = lax.axis_index("amp")
    width = tiles * LANES
    rows = 80
    for half in range(2):
        low = half * LANES + (0 if half else LANES - rows)
        for first in range(KINDS):
            at = (half * KINDS + first) * LANES
            band_rows = [bands[second, low : low + rows, :].astype(F32) for second in range(KINDS)]
            e = sum(band_rows[b] * coefs[2, 0, first * KINDS + b] for b in range(KINDS)).astype(BF16)
            empty = jnp.zeros((LANES - rows, 2 * LANES), BF16)
            begin = at + (0 if half else LANES - rows)
            for tile in range(tiles):
                column = lane_index(1) + (amp * width + tile * LANES)
                px = (column.astype(F32) + 0.5) / (width * amp_count) * 2.0 - 1.0
                weight = [coefs[0, 0, first * KINDS + b] + coefs[1, 0, first * KINDS + b] * px for b in range(KINDS)]
                d = sum(band_rows[b] * weight[b] for b in range(KINDS)).astype(BF16)
                de[tile, begin : begin + rows, 0:LANES] = d
                de[tile, begin : begin + rows, LANES : 2 * LANES] = e
                hollow = at + (rows if half else 0)
                de[tile, hollow : hollow + LANES - rows, :] = empty
    for copy in copies[4:]:
        copy.wait()


def collect_kernel(n, capacity, strips, strip_rows, ring, two, after, *refs):
    del after
    out = refs[-1]
    me = lax.axis_index("ccd")
    size = n * capacity * strip_rows
    lane = lax.broadcasted_iota(jnp.int32, (1, size), 1)
    named = jnp.full(lane.shape, -1, jnp.int32)
    for g in range(n):
        if two:
            found = two_of(refs[g][...].astype(F32), me, strips)
        else:
            found, total = matches(refs[g if ring else 0], None if ring else g, me, strips, capacity)
            found = [jnp.where(total > j, strip, -1) for j, strip in enumerate(found)]
        for j in range(capacity):
            low = (g * capacity + j) * strip_rows
            named = jnp.where((lane >= low) & (lane < low + strip_rows), found[j], named)
    lane = lax.broadcasted_iota(jnp.int32, (strip_rows, size), 1)
    row = lax.broadcasted_iota(jnp.int32, lane.shape, 0)
    same_row = lax.rem(lane, jnp.int32(strip_rows)) == row
    for p in range(strips):
        value = jnp.where(same_row & (named == p), 1.0, 0.0)
        out[p * strip_rows : (p + 1) * strip_rows, :] = value.astype(BF16)


def clear_ends(ref, tiles):
    zero = jnp.zeros((ref.shape[0], LANES), BF16)
    ref[:, 0:LANES] = zero
    ref[:, (tiles + 1) * LANES : (tiles + 2) * LANES] = zero


def stacked(refs):
    parts = [ref[...].reshape(-1, ref.shape[-1]) for ref in refs]
    return jnp.concatenate(parts, axis=0) if len(parts) > 1 else parts[0]


def warp_kernel(n, strips, strip_rows, tiles, ring, paired, *refs):
    forward, spread = refs[:2]
    count = n if ring else 1
    received, rest = from_order(refs[2 : 2 + count]), refs[2 + count :]
    if paired:
        image, send_amp, rows_done = rest
    else:
        image, rows_done = rest
    width = tiles * LANES
    clear_ends(rows_done, tiles)
    rows_done[:, LANES : LANES + width] = jnp.dot(
        forward[...], stacked(received), preferred_element_type=F32
    ).astype(BF16)
    lane = lane_index(strip_rows)
    for q in range(strips):
        rows = slice(q * strip_rows, (q + 1) * strip_rows)
        windows = [rows_done[rows, b * LANES : (b + 2) * LANES] for b in range(tiles + 1)]
        result = jnp.dot(jnp.concatenate(windows, axis=0), spread[q], preferred_element_type=F32)
        for b in range(tiles + 1):
            value = result[b * strip_rows : (b + 1) * strip_rows]
            if b == 0:
                value = jnp.where(lane < HALF_TILE, 0.0, value)
            if b == tiles:
                value = jnp.where(lane < HALF_TILE, value, 0.0)
            image[rows, b * LANES : (b + 1) * LANES] = value.astype(BF16)
    if paired:
        amp_first = lax.axis_index("amp") == 0
        send_amp[...] = jnp.where(amp_first, image[:, tiles * LANES :], image[:, 0:LANES])


def joined(ref, rows, left, right, tiles, amp_count):
    amp = lax.axis_index("amp")
    zero = jnp.zeros((), BF16)
    first = ref[rows, 0:LANES] + jnp.where(amp > 0, left, zero)
    last = ref[rows, tiles * LANES :] + jnp.where(amp < amp_count - 1, right, zero)
    return [first] + [ref[rows, b * LANES : (b + 1) * LANES] for b in range(1, tiles)] + [last]


def join_kernel(tiles, amp_count, paired, image, left, right, *outs):
    size = image.shape[0]
    edges = []
    for rows in (slice(0, MARGIN), slice(size - MARGIN, size)):
        parts = joined(image, rows, left[rows, :], right[rows, :], tiles, amp_count)
        edges.append(jnp.concatenate(parts, axis=1))
    if paired:
        edges = [jnp.where(lax.axis_index("row") == 0, edges[1], edges[0])]
    for edge, out in zip(edges, outs):
        out[...] = edge


def row_convolved(bands, parts, across, at, count):
    for low in range(0, len(parts), 2):
        window = jnp.concatenate(parts[low : low + 2], axis=1)
        result = jnp.dot(bands, window, preferred_element_type=F32)
        for b in range(low, min(low + 2, len(parts))):
            for kind in range(KINDS):
                piece = result[kind * count : (kind + 1) * count, (b - low) * LANES : (b - low + 1) * LANES]
                across[at : at + count, (b * KINDS + kind) * LANES : (b * KINDS + kind + 1) * LANES] = piece.astype(BF16)


def columns_returned(lowered, columns, at, gather, strip_rows, tiles):
    rows = slice(at, at + strip_rows)
    windows = [lowered[rows, b * LANES : (b + 3) * LANES] for b in range(tiles)]
    result = jnp.dot(jnp.concatenate(windows, axis=0), gather, preferred_element_type=F32)
    for b in range(tiles):
        columns[rows, b * LANES : (b + 1) * LANES] = result[b * strip_rows : (b + 1) * strip_rows].astype(BF16)


def subtracted(science, across, de, store, count, tiles, place):
    for b in range(tiles):
        acc = jnp.dot(
            across[:, b * KINDS * LANES : (b + 2) * KINDS * LANES], de[b], preferred_element_type=F32
        )
        store(b, science(b) - (acc[:, 0:LANES] + place * acc[:, LANES:]))


def row_place(first, count, band, row_count):
    row = lax.broadcasted_iota(jnp.int32, (count, LANES), 0) + (lax.axis_index("row") * band + first)
    return (row.astype(F32) + 0.5) / (band * row_count) * 2.0 - 1.0


def mid_kernel(strips, strip_rows, tiles, row_count, amp_count, image, left, right, science, de, bands, gather,
               diff, columns, across, lowered):
    band = strips * strip_rows
    count = band - 2 * strip_rows
    rows = slice(strip_rows - MARGIN, band - strip_rows + MARGIN)
    parts = joined(image, rows, left[rows, :], right[rows, :], tiles, amp_count)
    row_convolved(bands[...], parts, across, 0, count)
    clear_ends(lowered, tiles)

    def store(b, value):
        diff[:, b * LANES : (b + 1) * LANES] = value
        lowered[:, (b + 1) * LANES : (b + 2) * LANES] = value.astype(BF16)

    subtracted(
        lambda b: science[strip_rows : strip_rows + count, b * LANES : (b + 1) * LANES],
        across, de, store, count, tiles, row_place(strip_rows, count, band, row_count),
    )
    for q in range(1, strips - 1):
        columns_returned(lowered, columns, (q - 1) * strip_rows, gather[q], strip_rows, tiles)


def edge_kernel(n, capacity, strips, strip_rows, tiles, row_count, amp_count, ring, image, left, right, top, bottom,
                science, de, bands, backward, gather, columns_mid, diff, *rest):
    outs = rest[: n if ring else 1]
    across, lowered, columns = rest[len(outs) :]
    band = strips * strip_rows
    inner = strip_rows + MARGIN
    row = lax.axis_index("row")
    zero = jnp.zeros((), BF16)
    tile = [slice(b * LANES, (b + 1) * LANES) for b in range(tiles + 1)]
    above = [jnp.where(row > 0, top[:, t], zero) for t in tile]
    below = [jnp.where(row < row_count - 1, bottom[:, t], zero) for t in tile]
    first, last = slice(0, inner), slice(band - inner, band)
    upper = joined(image, first, left[first, :], right[first, :], tiles, amp_count)
    lower = joined(image, last, left[last, :], right[last, :], tiles, amp_count)
    row_convolved(bands[...], [jnp.concatenate(p, axis=0) for p in zip(above, upper)], across, 0, strip_rows)
    row_convolved(bands[...], [jnp.concatenate(p, axis=0) for p in zip(lower, below)], across, strip_rows, strip_rows)

    def store(b, value):
        at = slice(b * LANES, (b + 1) * LANES)
        diff[:, at] = value
        lowered[:, (b + 1) * LANES : (b + 2) * LANES] = value.astype(BF16)

    clear_ends(lowered, tiles)

    def edge_science(b):
        at = slice(b * LANES, (b + 1) * LANES)
        return jnp.concatenate([science[0:strip_rows, at], science[band - strip_rows : band, at]], axis=0)

    place = jnp.concatenate([row_place(0, strip_rows, band, row_count),
                             row_place(band - strip_rows, strip_rows, band, row_count)], axis=0)
    subtracted(edge_science, across, de, store, 2 * strip_rows, tiles, place)
    columns_returned(lowered, columns, 0, gather[0], strip_rows, tiles)
    columns_returned(lowered, columns, strip_rows, gather[strips - 1], strip_rows, tiles)
    whole = jnp.concatenate([columns[:strip_rows, :], columns_mid[...], columns[strip_rows:, :]], axis=0)
    result = jnp.dot(backward[...], whole, preferred_element_type=F32).astype(BF16)
    size = capacity * strip_rows * (1 if ring else n)
    for g, out in enumerate(outs):
        out[...] = result[g * size : (g + 1) * size].reshape(out.shape)


def sum_kernel(collect, *refs):
    *returned, stack, total, sems = refs
    values = stacked(returned[-1:] + returned[:-1])
    copies = []
    half = total.shape[0] // 2
    for i in range(2):
        rows = pl.ds(i * half, half)
        total[rows, :] = jnp.dot(collect[rows, :], values, preferred_element_type=F32)
        copy = pltpu.make_async_copy(total.at[rows], stack.at[rows], sems.at[i])
        copy.start()
        copies.append(copy)
    for copy in copies:
        copy.wait()


def body(science, template, owners, patch_strip, shifts, fractions, coefs):
    n = lax.axis_size("ccd")
    row_count = lax.axis_size("row")
    amp_count = lax.axis_size("amp")
    band, width = science.shape[1:]
    strips, strip_rows = template.shape[3:5]
    capacity = max(2, strips // n)
    tiles = width // LANES
    padded = width + LANES
    ring = n <= 4
    two = ring and capacity == 2 and strips == 2 * n
    paired = row_count == 2 and amp_count == 2
    swap = [(0, 1), (1, 0)]
    strip_shape = (capacity, strip_rows, width)

    def call(kernel, out_shape, operands, spaces, scratch=(), megabytes=8):
        shapes = [jax.ShapeDtypeStruct(*s) if isinstance(s, tuple) else s for s in out_shape]
        return pl.pallas_call(
            kernel,
            out_shape=shapes,
            in_specs=list(spaces),
            out_specs=[VMEM if isinstance(s, tuple) else HBM for s in out_shape],
            scratch_shapes=[pltpu.VMEM(*s) if isinstance(s, tuple) else s for s in scratch],
            compiler_params=pltpu.CompilerParams(vmem_limit_bytes=megabytes << 20),
            cost_estimate=pl.CostEstimate(flops=0, bytes_accessed=1 << 20, transcendentals=0),
        )(*operands)

    def turn(value, g):
        return lax.ppermute(value, "ccd", [(i, (i + g) % n) for i in range(n)])

    def exchange(parts, sign):
        if not ring:
            return [lax.all_to_all(parts[0], "ccd", split_axis=0, concat_axis=0, tiled=True)]
        return [parts[0]] + [turn(parts[g], sign * g) for g in range(1, n)]

    code = owners.reshape(1, strips) * strips + patch_strip.reshape(1, strips)
    (template_rows,) = call(
        load_kernel,
        [((band, width), BF16)],
        [in_hbm(template.reshape(band, width))],
        [HBM],
        [pltpu.SemaphoreType.DMA],
    )

    if two:
        codes = exchange([code] * n, 1)
        picked = [
            call(
                functools.partial(pick_two_kernel, strips, strip_rows),
                [(strip_shape, BF16)],
                [other, template_rows],
                [VMEM] * 2,
            )[0]
            for other in codes[1:]
        ]
    elif ring:
        codes = exchange([code.reshape(strips)] * n, 1)
        picked_shapes = [(strip_shape, BF16)] * n
    else:
        codes = [lax.all_gather(code.reshape(strips), "ccd", axis=0, tiled=True)]
        picked_shapes = [((n * capacity, strip_rows, width), BF16)]
    if not two:
        picked = call(
            functools.partial(pick_kernel, n, capacity, strips, ring),
            picked_shapes,
            [*codes, template_rows],
            [SMEM] * len(codes) + [VMEM],
        )
    mid_rows = band - 2 * strip_rows
    mid_bands = jnp.asarray(row_bands(mid_rows))
    slot_rows = n * capacity * strip_rows
    *own, de, forward, backward, spread, gather, science, mid_bands = call(
        functools.partial(prepare_kernel, n, capacity, strips, strip_rows, tiles, amp_count, ring, two),
        ([(strip_shape, BF16)] if two else []) + [
            ((tiles, 2 * KINDS * LANES, 2 * LANES), BF16),
            ((band, slot_rows), BF16),
            ((slot_rows, band), BF16),
            ((strips, 2 * LANES, LANES), BF16),
            ((strips, 3 * LANES, LANES), BF16),
            ((band, width), F32),
            (mid_bands.shape, BF16),
        ],
        [in_hbm(value) for value in (
            coefs.transpose(1, 0, 2), shifts.reshape(2, strips), fractions.reshape(2, strips),
            jnp.asarray(column_bands()), science.reshape(band, width), mid_bands)]
        + [picked[0], code] + ([code, template_rows] if two else []),
        [HBM] * 6 + [VMEM, SMEM] + [VMEM] * (2 if two else 0),
        [pltpu.SMEM((3, 1, 9), F32), pltpu.SMEM((2, strips), jnp.int32),
         ((2, strips), F32), ((KINDS, 2 * LANES, LANES), BF16), pltpu.SemaphoreType.DMA((6,))],
        megabytes=10,
    )
    if two:
        received = in_order(exchange([*own, *picked], -1))
    else:
        received = in_order(exchange(picked, -1))
    image_shape = ((band, padded), BF16)
    warped = call(
        functools.partial(warp_kernel, n, strips, strip_rows, tiles, ring, paired),
        [image_shape] + ([((band, LANES), BF16)] if paired else []),
        [forward, spread, *received],
        [VMEM] * (2 + len(received)),
        [((band, padded + LANES), BF16)],
    )
    image = warped[0]
    edge_shape = ((MARGIN, padded), BF16)
    join = functools.partial(join_kernel, tiles, amp_count, paired)
    if paired:
        left = right = lax.ppermute(warped[1], "amp", swap)
        (edge,) = call(join, [edge_shape], [image, left, right], [VMEM] * 3)
        top = bottom = lax.ppermute(edge, "row", swap)
    else:

        def moved(value, axis, step):
            count = lax.axis_size(axis)
            return lax.ppermute(value, axis, [(i, i + step) for i in range(count) if 0 <= i + step < count])

        left, right = moved(image[:, padded - LANES :], "amp", 1), moved(image[:, :LANES], "amp", -1)
        first, last = call(join, [edge_shape] * 2, [image, left, right], [VMEM] * 3)
        top, bottom = moved(last, "row", 1), moved(first, "row", -1)

    diff_mid, columns_mid = call(
        functools.partial(mid_kernel, strips, strip_rows, tiles, row_count, amp_count),
        [((mid_rows, width), F32), ((mid_rows, width), BF16)],
        [image, left, right, science, de, mid_bands, gather],
        [VMEM] * 7,
        [((mid_rows, (tiles + 1) * KINDS * LANES), BF16), ((mid_rows, padded + LANES), BF16)],
    )
    outgoing_shapes = [(strip_shape, BF16)] * n if ring else [((n * capacity, strip_rows, width), BF16)]
    diff_edge, *outgoing = call(
        functools.partial(edge_kernel, n, capacity, strips, strip_rows, tiles, row_count, amp_count, ring),
        [((2 * strip_rows, width), F32)] + outgoing_shapes,
        [image, left, right, top, bottom, science, de, jnp.asarray(row_bands(strip_rows)), backward, gather,
         columns_mid],
        [VMEM] * 11,
        [((2 * strip_rows, (tiles + 1) * KINDS * LANES), BF16), ((2 * strip_rows, padded + LANES), BF16),
         ((2 * strip_rows, width), BF16)],
    )
    returned = exchange(outgoing, 1)
    returned = returned[1:] + returned[:1]
    (collect,) = call(
        functools.partial(collect_kernel, n, capacity, strips, strip_rows, ring, two),
        [((band, slot_rows), BF16)],
        [outgoing[0], *codes],
        [VMEM] + [VMEM if two else SMEM] * len(codes),
    )
    (stack,) = call(
        sum_kernel,
        [pltpu.HBM((band, width), F32)],
        [collect, *returned],
        [VMEM] * (1 + len(returned)),
        [((band, width), F32), pltpu.SemaphoreType.DMA((2,))],
    )
    difference = jnp.concatenate([diff_edge[:strip_rows], diff_mid, diff_edge[strip_rows:]])
    return difference[None], stack.reshape(template.shape)


def solution(mesh):
    return jax.shard_map(
        body,
        mesh=mesh,
        in_specs=(
            P(("grp", "ccd"), "row", "amp"),
            P(("grp", "ccd"), "row", "amp", None, None, None),
            P(("grp", "ccd"), "row", "amp", None, None),
            P(("grp", "ccd"), "row", "amp", None),
            P(("grp", "ccd"), "row", "amp", None, None),
            P(("grp", "ccd"), "row", "amp", None, None),
            P(("grp", "ccd"), None, None),
        ),
        out_specs=(
            P(("grp", "ccd"), "row", "amp"),
            P(("grp", "ccd"), "row", "amp", None, None, None),
        ),
        check_vma=False,
    )
```

```python
import functools

import jax
import jax.numpy as jnp
import ml_dtypes
import numpy as np
from jax import lax
from jax.experimental import pallas as pl
from jax.experimental.pallas import tpu as pltpu
from jax.sharding import PartitionSpec as P

RADIUS = 9
LANES = 128
HALF_TILE = 64
MARGIN = 16
TAPS = 6
KINDS = 3

F32 = jnp.float32
BF16 = jnp.bfloat16
SMEM = pl.BlockSpec(memory_space=pltpu.SMEM)
VMEM = pl.BlockSpec(memory_space=pltpu.VMEM)
HBM = pl.BlockSpec(memory_space=pltpu.HBM)


def kernel_table():
    support = np.arange(-RADIUS, RADIUS + 1).astype(np.float32)
    narrow = np.exp(-support * support / np.float32(4.5))
    slope = support * np.exp(-support * support / np.float32(12.5))
    broad = np.exp(-support * support / np.float32(40.5))
    table = np.stack([narrow / narrow.sum(), slope / np.abs(slope).sum(), broad / broad.sum()])
    return table.astype(ml_dtypes.bfloat16)


def column_bands():
    table = kernel_table()
    source = np.arange(2 * LANES)[:, None]
    target = np.arange(LANES)[None, :]
    place = source - HALF_TILE - target + RADIUS
    inside = (place >= 0) & (place <= 2 * RADIUS)
    return np.stack(
        [np.where(inside, row[np.clip(place, 0, 2 * RADIUS)], 0) for row in table]
    ).astype(ml_dtypes.bfloat16)


def row_bands(count):
    table = kernel_table()
    source = np.arange(count + 2 * MARGIN)[None, :]
    target = np.arange(count)[:, None]
    place = source - MARGIN - target + RADIUS
    inside = (place >= 0) & (place <= 2 * RADIUS)
    return np.concatenate(
        [np.where(inside, row[np.clip(place, 0, 2 * RADIUS)], 0) for row in table]
    ).astype(ml_dtypes.bfloat16)


def sinc(value):
    turn = jnp.pi * value
    return jnp.where(value == 0.0, 1.0, jnp.sin(turn) / jnp.where(value == 0.0, 1.0, turn))


def lanczos_taps(fraction):
    place = lax.broadcasted_iota(jnp.int32, (8, fraction.shape[1]), 0) - 2
    spread = place.astype(F32) - fraction
    return (sinc(spread) * sinc(spread / 3.0)).astype(BF16).astype(F32)


def in_hbm(value):
    return pltpu.with_memory_space_constraint(value, pltpu.HBM)


def lane_index(rows):
    return lax.broadcasted_iota(jnp.int32, (rows, LANES), 1)


def order_of(n):
    return (1, 3, 2, 0) if n == 4 else (*range(1, n), 0)


def in_order(values):
    return [values[g] for g in order_of(len(values))]


def from_order(values):
    order = order_of(len(values))
    return [values[order.index(g)] for g in range(len(values))]


def matches(code_ref, group, me, strips, capacity):
    found, count = [jnp.int32(0)] * capacity, jnp.int32(0)
    for q in range(strips):
        code = code_ref[group * strips + q] if group is not None else code_ref[q]
        hit = lax.div(code, jnp.int32(strips)) == me
        strip = lax.rem(code, jnp.int32(strips))
        found = [jnp.where(hit & (count == j), strip, f) for j, f in enumerate(found)]
        count = count + hit.astype(jnp.int32)
    return found, count


def slots_of(code_ref, me, strips, capacity, n, ring):
    owners = [lax.div(code_ref[0, q], jnp.int32(strips)) for q in range(strips)]
    slots = []
    for q in range(strips):
        rank = jnp.int32(0)
        for p in range(q):
            rank = rank + (owners[p] == owners[q]).astype(jnp.int32)
        group = lax.rem(owners[q] - me + n, jnp.int32(n)) if ring else owners[q]
        slots.append(group * capacity + rank)
    return slots


def pick_kernel(n, capacity, strips, ring, *refs):
    if ring:
        codes, template, outs = refs[:n], refs[n], refs[n + 1 :]
    else:
        codes, template, outs = [refs[0]] * n, refs[1], refs[2:]
    me = lax.axis_index("ccd")
    for g in range(n):
        found, _ = matches(codes[g], None if ring else g, me, strips, capacity)
        for j in range(capacity):
            if ring:
                outs[g][j] = template[strip_rows_at(found[j], template.shape[0] // strips), :]
            else:
                outs[0][g * capacity + j] = template[strip_rows_at(found[j], template.shape[0] // strips), :]


def two_of(value, owner, strips):
    lane = lax.broadcasted_iota(jnp.int32, value.shape, 1).astype(F32)
    low = (owner * strips).astype(F32)
    hit = (value >= low) & (value < low + strips)
    key = lane * strips + (value - low)
    first = jnp.min(jnp.where(hit, key, 1024.0)).astype(jnp.int32)
    last = jnp.max(jnp.where(hit, key, 0.0)).astype(jnp.int32)
    return lax.rem(first, jnp.int32(strips)), lax.rem(last, jnp.int32(strips))


def strip_rows_at(strip, strip_rows):
    return pl.ds(pl.multiple_of(strip * strip_rows, strip_rows), strip_rows)


def pick_two_kernel(strips, strip_rows, code, template, out):
    for j, strip in enumerate(two_of(code[...].astype(F32), lax.axis_index("ccd"), strips)):
        out[j] = template[strip_rows_at(strip, strip_rows), :]


def load_kernel(source, target, sem):
    copy = pltpu.make_async_copy(source, target, sem)
    copy.start()
    copy.wait()


def turned(base, first, rows):
    return pltpu.roll(jnp.broadcast_to(base, (rows, base.shape[1])), first, 1, stride=1, stride_axis=0)


def base_row(taps, q, start, sign, size):
    lane = lax.broadcasted_iota(jnp.int32, (1, size), 1)
    value = jnp.zeros((1, size), F32)
    for t in range(TAPS):
        at = lax.rem(start + sign * (t - 2) + size, jnp.int32(size))
        value = jnp.where(lane == at, jnp.broadcast_to(taps[t : t + 1, q : q + 1], (1, size)), value)
    return value


def prepare_kernel(n, capacity, strips, strip_rows, tiles, amp_count, ring, two, coefs_in, shifts_in, fractions_in,
                   bands_in, science_in, row_band_in, after, code, *refs):
    del after
    if two:
        own_code, template, own = refs[:3]
        refs = refs[3:]
    de, forward, backward, spread, gather, science, row_band, coefs, shifts, fractions, bands, sems = refs
    pairs = [(fractions_in, fractions), (shifts_in, shifts), (coefs_in, coefs),
             (bands_in, bands), (row_band_in, row_band), (science_in, science)]
    copies = [pltpu.make_async_copy(source, target, sems.at[i]) for i, (source, target) in enumerate(pairs)]
    for copy in copies:
        copy.start()
    for copy in copies[:2]:
        copy.wait()
    taps = [lanczos_taps(fractions[d : d + 1, :]) for d in range(2)]
    me = lax.axis_index("ccd")
    band, slots = strips * strip_rows, n * capacity
    size = slots * strip_rows
    if slots != strips:
        backward[...] = jnp.zeros(backward.shape, BF16)
    forward_lane = lax.broadcasted_iota(jnp.int32, (strip_rows, size), 1)
    backward_lane = lax.broadcasted_iota(jnp.int32, (strip_rows, band), 1)
    for q, slot in enumerate(slots_of(code, me, strips, capacity, n, ring)):
        low, high = slot * strip_rows, q * strip_rows
        value = turned(base_row(taps[0], q, low + shifts[0, q], 1, size), 0, strip_rows)
        value = jnp.where((forward_lane >= low) & (forward_lane < low + strip_rows), value, 0.0)
        forward[high : high + strip_rows, :] = value.astype(BF16)
        value = turned(base_row(taps[0], q, high - shifts[0, q], -1, band), 0, strip_rows)
        value = jnp.where((backward_lane >= high) & (backward_lane < high + strip_rows), value, 0.0)
        backward[strip_rows_at(slot, strip_rows), :] = value.astype(BF16)

    if two:
        for j, strip in enumerate(two_of(own_code[...].astype(F32), me, strips)):
            own[j] = template[strip_rows_at(strip, strip_rows), :]

    rows = 160
    away = lax.broadcasted_iota(jnp.int32, (rows, LANES), 0) - lane_index(rows)
    for out, low, centre, sign in ((spread, 48, HALF_TILE, -1), (gather, 112, LANES, 1)):
        within = (away >= centre - low - 8) & (away <= centre - low + 8)
        end = out.shape[1]
        for q in range(strips):
            start = (low - centre) + sign * shifts[1, q] + LANES
            value = turned(base_row(taps[1], q, start, sign, LANES), 0, rows)
            out[q, 0:low, :] = jnp.zeros((low, LANES), BF16)
            out[q, low : low + rows, :] = jnp.where(within, value, 0.0).astype(BF16)
            out[q, low + rows : end, :] = jnp.zeros((end - low - rows, LANES), BF16)
    for copy in copies[2:4]:
        copy.wait()
    amp = lax.axis_index("amp")
    width = tiles * LANES
    rows = 80
    for half in range(2):
        low = half * LANES + (0 if half else LANES - rows)
        for first in range(KINDS):
            at = (half * KINDS + first) * LANES
            band_rows = [bands[second, low : low + rows, :].astype(F32) for second in range(KINDS)]
            e = sum(band_rows[b] * coefs[2, 0, first * KINDS + b] for b in range(KINDS)).astype(BF16)
            empty = jnp.zeros((LANES - rows, 2 * LANES), BF16)
            begin = at + (0 if half else LANES - rows)
            for tile in range(tiles):
                column = lane_index(1) + (amp * width + tile * LANES)
                px = (column.astype(F32) + 0.5) / (width * amp_count) * 2.0 - 1.0
                weight = [coefs[0, 0, first * KINDS + b] + coefs[1, 0, first * KINDS + b] * px for b in range(KINDS)]
                d = sum(band_rows[b] * weight[b] for b in range(KINDS)).astype(BF16)
                de[tile, begin : begin + rows, 0:LANES] = d
                de[tile, begin : begin + rows, LANES : 2 * LANES] = e
                hollow = at + (rows if half else 0)
                de[tile, hollow : hollow + LANES - rows, :] = empty
    for copy in copies[4:]:
        copy.wait()


def collect_kernel(n, capacity, strips, strip_rows, ring, two, after, *refs):
    del after
    out = refs[-1]
    me = lax.axis_index("ccd")
    size = n * capacity * strip_rows
    lane = lax.broadcasted_iota(jnp.int32, (1, size), 1)
    named = jnp.full(lane.shape, -1, jnp.int32)
    for g in range(n):
        if two:
            found = two_of(refs[g][...].astype(F32), me, strips)
        else:
            found, total = matches(refs[g if ring else 0], None if ring else g, me, strips, capacity)
            found = [jnp.where(total > j, strip, -1) for j, strip in enumerate(found)]
        for j in range(capacity):
            low = (g * capacity + j) * strip_rows
            named = jnp.where((lane >= low) & (lane < low + strip_rows), found[j], named)
    lane = lax.broadcasted_iota(jnp.int32, (strip_rows, size), 1)
    row = lax.broadcasted_iota(jnp.int32, lane.shape, 0)
    same_row = lax.rem(lane, jnp.int32(strip_rows)) == row
    for p in range(strips):
        value = jnp.where(same_row & (named == p), 1.0, 0.0)
        out[p * strip_rows : (p + 1) * strip_rows, :] = value.astype(BF16)


def clear_ends(ref, tiles):
    zero = jnp.zeros((ref.shape[0], LANES), BF16)
    ref[:, 0:LANES] = zero
    ref[:, (tiles + 1) * LANES : (tiles + 2) * LANES] = zero


def stacked(refs):
    parts = [ref[...].reshape(-1, ref.shape[-1]) for ref in refs]
    return jnp.concatenate(parts, axis=0) if len(parts) > 1 else parts[0]


def side_kernel(n, strips, strip_rows, tiles, forward, spread, *refs):
    out = refs[-1]
    pool = stacked(from_order(refs[:n]))
    first = lax.axis_index("amp") == 0
    source = jnp.where(first, pool[:, (tiles - 1) * LANES :], pool[:, 0:LANES])
    rows_done = jnp.dot(forward[...], source, preferred_element_type=F32).astype(BF16)
    lane = lane_index(strip_rows)
    inside = (lane < HALF_TILE) == first
    for q in range(strips):
        rows = slice(q * strip_rows, (q + 1) * strip_rows)
        taps = jnp.where(first, spread[q, 0:LANES, :], spread[q, LANES : 2 * LANES, :])
        value = jnp.dot(rows_done[rows], taps, preferred_element_type=F32)
        out[rows, :] = jnp.where(inside, value, 0.0).astype(BF16)


def warp_kernel(n, strips, strip_rows, tiles, ring, *refs):
    forward, spread = refs[:2]
    count = n if ring else 1
    received, rest = from_order(refs[2 : 2 + count]), refs[2 + count :]
    image, rows_done = rest
    width = tiles * LANES
    clear_ends(rows_done, tiles)
    rows_done[:, LANES : LANES + width] = jnp.dot(
        forward[...], stacked(received), preferred_element_type=F32
    ).astype(BF16)
    lane = lane_index(strip_rows)
    for q in range(strips):
        rows = slice(q * strip_rows, (q + 1) * strip_rows)
        windows = [rows_done[rows, b * LANES : (b + 2) * LANES] for b in range(tiles + 1)]
        result = jnp.dot(jnp.concatenate(windows, axis=0), spread[q], preferred_element_type=F32)
        for b in range(tiles + 1):
            value = result[b * strip_rows : (b + 1) * strip_rows]
            if b == 0:
                value = jnp.where(lane < HALF_TILE, 0.0, value)
            if b == tiles:
                value = jnp.where(lane < HALF_TILE, value, 0.0)
            image[rows, b * LANES : (b + 1) * LANES] = value.astype(BF16)


def joined(ref, rows, left, right, tiles, amp_count):
    amp = lax.axis_index("amp")
    zero = jnp.zeros((), BF16)
    first = ref[rows, 0:LANES] + jnp.where(amp > 0, left, zero)
    last = ref[rows, tiles * LANES :] + jnp.where(amp < amp_count - 1, right, zero)
    return [first] + [ref[rows, b * LANES : (b + 1) * LANES] for b in range(1, tiles)] + [last]


def join_kernel(tiles, amp_count, paired, image, left, right, *outs):
    size = image.shape[0]
    edges = []
    for rows in (slice(0, MARGIN), slice(size - MARGIN, size)):
        parts = joined(image, rows, left[rows, :], right[rows, :], tiles, amp_count)
        edges.append(jnp.concatenate(parts, axis=1))
    if paired:
        edges = [jnp.where(lax.axis_index("row") == 0, edges[1], edges[0])]
    for edge, out in zip(edges, outs):
        out[...] = edge


def row_convolved(bands, parts, across, at, count):
    for low in range(0, len(parts), 2):
        window = jnp.concatenate(parts[low : low + 2], axis=1)
        result = jnp.dot(bands, window, preferred_element_type=F32)
        for b in range(low, min(low + 2, len(parts))):
            for kind in range(KINDS):
                piece = result[kind * count : (kind + 1) * count, (b - low) * LANES : (b - low + 1) * LANES]
                across[at : at + count, (b * KINDS + kind) * LANES : (b * KINDS + kind + 1) * LANES] = piece.astype(BF16)


def columns_returned(lowered, columns, at, gather, strip_rows, tiles):
    rows = slice(at, at + strip_rows)
    windows = [lowered[rows, b * LANES : (b + 3) * LANES] for b in range(tiles)]
    result = jnp.dot(jnp.concatenate(windows, axis=0), gather, preferred_element_type=F32)
    for b in range(tiles):
        columns[rows, b * LANES : (b + 1) * LANES] = result[b * strip_rows : (b + 1) * strip_rows].astype(BF16)


def subtracted(science, across, de, store, count, tiles, place):
    for b in range(tiles):
        acc = jnp.dot(
            across[:, b * KINDS * LANES : (b + 2) * KINDS * LANES], de[b], preferred_element_type=F32
        )
        store(b, science(b) - (acc[:, 0:LANES] + place * acc[:, LANES:]))


def row_place(first, count, band, row_count):
    row = lax.broadcasted_iota(jnp.int32, (count, LANES), 0) + (lax.axis_index("row") * band + first)
    return (row.astype(F32) + 0.5) / (band * row_count) * 2.0 - 1.0


def mid_kernel(strips, strip_rows, tiles, row_count, amp_count, image, left, right, science, de, bands, gather,
               diff, columns, across, lowered):
    band = strips * strip_rows
    count = band - 2 * strip_rows
    rows = slice(strip_rows - MARGIN, band - strip_rows + MARGIN)
    parts = joined(image, rows, left[rows, :], right[rows, :], tiles, amp_count)
    row_convolved(bands[...], parts, across, 0, count)
    clear_ends(lowered, tiles)

    def store(b, value):
        diff[:, b * LANES : (b + 1) * LANES] = value
        lowered[:, (b + 1) * LANES : (b + 2) * LANES] = value.astype(BF16)

    subtracted(
        lambda b: science[strip_rows : strip_rows + count, b * LANES : (b + 1) * LANES],
        across, de, store, count, tiles, row_place(strip_rows, count, band, row_count),
    )
    for q in range(1, strips - 1):
        columns_returned(lowered, columns, (q - 1) * strip_rows, gather[q], strip_rows, tiles)


def edge_kernel(n, capacity, strips, strip_rows, tiles, row_count, amp_count, ring, image, left, right, top, bottom,
                science, de, bands, backward, gather, columns_mid, diff, *rest):
    outs = rest[: n if ring else 1]
    across, lowered, columns = rest[len(outs) :]
    band = strips * strip_rows
    inner = strip_rows + MARGIN
    row = lax.axis_index("row")
    zero = jnp.zeros((), BF16)
    tile = [slice(b * LANES, (b + 1) * LANES) for b in range(tiles + 1)]
    above = [jnp.where(row > 0, top[:, t], zero) for t in tile]
    below = [jnp.where(row < row_count - 1, bottom[:, t], zero) for t in tile]
    first, last = slice(0, inner), slice(band - inner, band)
    upper = joined(image, first, left[first, :], right[first, :], tiles, amp_count)
    lower = joined(image, last, left[last, :], right[last, :], tiles, amp_count)
    row_convolved(bands[...], [jnp.concatenate(p, axis=0) for p in zip(above, upper)], across, 0, strip_rows)
    row_convolved(bands[...], [jnp.concatenate(p, axis=0) for p in zip(lower, below)], across, strip_rows, strip_rows)

    def store(b, value):
        at = slice(b * LANES, (b + 1) * LANES)
        diff[:, at] = value
        lowered[:, (b + 1) * LANES : (b + 2) * LANES] = value.astype(BF16)

    clear_ends(lowered, tiles)

    def edge_science(b):
        at = slice(b * LANES, (b + 1) * LANES)
        return jnp.concatenate([science[0:strip_rows, at], science[band - strip_rows : band, at]], axis=0)

    place = jnp.concatenate([row_place(0, strip_rows, band, row_count),
                             row_place(band - strip_rows, strip_rows, band, row_count)], axis=0)
    subtracted(edge_science, across, de, store, 2 * strip_rows, tiles, place)
    columns_returned(lowered, columns, 0, gather[0], strip_rows, tiles)
    columns_returned(lowered, columns, strip_rows, gather[strips - 1], strip_rows, tiles)
    whole = jnp.concatenate([columns[:strip_rows, :], columns_mid[...], columns[strip_rows:, :]], axis=0)
    result = jnp.dot(backward[...], whole, preferred_element_type=F32).astype(BF16)
    size = capacity * strip_rows * (1 if ring else n)
    for g, out in enumerate(outs):
        out[...] = result[g * size : (g + 1) * size].reshape(out.shape)


def sum_kernel(collect, *refs):
    *returned, stack, total, sems = refs
    values = stacked(returned[-1:] + returned[:-1])
    copies = []
    half = total.shape[0] // 2
    for i in range(2):
        rows = pl.ds(i * half, half)
        total[rows, :] = jnp.dot(collect[rows, :], values, preferred_element_type=F32)
        copy = pltpu.make_async_copy(total.at[rows], stack.at[rows], sems.at[i])
        copy.start()
        copies.append(copy)
    for copy in copies:
        copy.wait()


def body(science, template, owners, patch_strip, shifts, fractions, coefs):
    n = lax.axis_size("ccd")
    row_count = lax.axis_size("row")
    amp_count = lax.axis_size("amp")
    band, width = science.shape[1:]
    strips, strip_rows = template.shape[3:5]
    capacity = max(2, strips // n)
    tiles = width // LANES
    padded = width + LANES
    ring = n <= 4
    two = ring and capacity == 2 and strips == 2 * n
    paired = row_count == 2 and amp_count == 2 and two
    swap = [(0, 1), (1, 0)]
    strip_shape = (capacity, strip_rows, width)

    def call(kernel, out_shape, operands, spaces, scratch=(), megabytes=8):
        shapes = [jax.ShapeDtypeStruct(*s) if isinstance(s, tuple) else s for s in out_shape]
        return pl.pallas_call(
            kernel,
            out_shape=shapes,
            in_specs=list(spaces),
            out_specs=[VMEM if isinstance(s, tuple) else HBM for s in out_shape],
            scratch_shapes=[pltpu.VMEM(*s) if isinstance(s, tuple) else s for s in scratch],
            compiler_params=pltpu.CompilerParams(vmem_limit_bytes=megabytes << 20),
            cost_estimate=pl.CostEstimate(flops=0, bytes_accessed=1 << 20, transcendentals=0),
        )(*operands)

    def turn(value, g):
        return lax.ppermute(value, "ccd", [(i, (i + g) % n) for i in range(n)])

    def exchange(parts, sign):
        if not ring:
            return [lax.all_to_all(parts[0], "ccd", split_axis=0, concat_axis=0, tiled=True)]
        return [parts[0]] + [turn(parts[g], sign * g) for g in range(1, n)]

    code = owners.reshape(1, strips) * strips + patch_strip.reshape(1, strips)
    (template_rows,) = call(
        load_kernel,
        [((band, width), BF16)],
        [in_hbm(template.reshape(band, width))],
        [HBM],
        [pltpu.SemaphoreType.DMA],
    )

    if two:
        codes = exchange([code] * n, 1)
        picked = [
            call(
                functools.partial(pick_two_kernel, strips, strip_rows),
                [(strip_shape, BF16)],
                [other, template_rows],
                [VMEM] * 2,
            )[0]
            for other in codes[1:]
        ]
    elif ring:
        codes = exchange([code.reshape(strips)] * n, 1)
        picked_shapes = [(strip_shape, BF16)] * n
    else:
        codes = [lax.all_gather(code.reshape(strips), "ccd", axis=0, tiled=True)]
        picked_shapes = [((n * capacity, strip_rows, width), BF16)]
    if not two:
        picked = call(
            functools.partial(pick_kernel, n, capacity, strips, ring),
            picked_shapes,
            [*codes, template_rows],
            [SMEM] * len(codes) + [VMEM],
        )
    mid_rows = band - 2 * strip_rows
    mid_bands = jnp.asarray(row_bands(mid_rows))
    slot_rows = n * capacity * strip_rows
    *own, de, forward, backward, spread, gather, science, mid_bands = call(
        functools.partial(prepare_kernel, n, capacity, strips, strip_rows, tiles, amp_count, ring, two),
        ([(strip_shape, BF16)] if two else []) + [
            ((tiles, 2 * KINDS * LANES, 2 * LANES), BF16),
            ((band, slot_rows), BF16),
            ((slot_rows, band), BF16),
            ((strips, 2 * LANES, LANES), BF16),
            ((strips, 3 * LANES, LANES), BF16),
            ((band, width), F32),
            (mid_bands.shape, BF16),
        ],
        [in_hbm(value) for value in (
            coefs.transpose(1, 0, 2), shifts.reshape(2, strips), fractions.reshape(2, strips),
            jnp.asarray(column_bands()), science.reshape(band, width), mid_bands)]
        + [picked[0], code] + ([code, template_rows] if two else []),
        [HBM] * 6 + [VMEM, SMEM] + [VMEM] * (2 if two else 0),
        [pltpu.SMEM((3, 1, 9), F32), pltpu.SMEM((2, strips), jnp.int32),
         ((2, strips), F32), ((KINDS, 2 * LANES, LANES), BF16), pltpu.SemaphoreType.DMA((6,))],
        megabytes=10,
    )
    if two:
        received = in_order(exchange([*own, *picked], -1))
    else:
        received = in_order(exchange(picked, -1))
    image_shape = ((band, padded), BF16)
    if paired:
        (beside,) = call(
            functools.partial(side_kernel, n, strips, strip_rows, tiles),
            [((band, LANES), BF16)],
            [forward, spread, *received],
            [VMEM] * (2 + n),
        )
        left = right = lax.ppermute(beside, "amp", swap)
    (image,) = call(
        functools.partial(warp_kernel, n, strips, strip_rows, tiles, ring),
        [image_shape],
        [forward, spread, *received],
        [VMEM] * (2 + len(received)),
        [((band, padded + LANES), BF16)],
    )
    edge_shape = ((MARGIN, padded), BF16)
    join = functools.partial(join_kernel, tiles, amp_count, paired)
    if paired:
        (edge,) = call(join, [edge_shape], [image, left, right], [VMEM] * 3)
        top = bottom = lax.ppermute(edge, "row", swap)
    else:

        def moved(value, axis, step):
            count = lax.axis_size(axis)
            return lax.ppermute(value, axis, [(i, i + step) for i in range(count) if 0 <= i + step < count])

        left, right = moved(image[:, padded - LANES :], "amp", 1), moved(image[:, :LANES], "amp", -1)
        first, last = call(join, [edge_shape] * 2, [image, left, right], [VMEM] * 3)
        top, bottom = moved(last, "row", 1), moved(first, "row", -1)

    diff_mid, columns_mid = call(
        functools.partial(mid_kernel, strips, strip_rows, tiles, row_count, amp_count),
        [((mid_rows, width), F32), ((mid_rows, width), BF16)],
        [image, left, right, science, de, mid_bands, gather],
        [VMEM] * 7,
        [((mid_rows, (tiles + 1) * KINDS * LANES), BF16), ((mid_rows, padded + LANES), BF16)],
    )
    outgoing_shapes = [(strip_shape, BF16)] * n if ring else [((n * capacity, strip_rows, width), BF16)]
    diff_edge, *outgoing = call(
        functools.partial(edge_kernel, n, capacity, strips, strip_rows, tiles, row_count, amp_count, ring),
        [((2 * strip_rows, width), F32)] + outgoing_shapes,
        [image, left, right, top, bottom, science, de, jnp.asarray(row_bands(strip_rows)), backward, gather,
         columns_mid],
        [VMEM] * 11,
        [((2 * strip_rows, (tiles + 1) * KINDS * LANES), BF16), ((2 * strip_rows, padded + LANES), BF16),
         ((2 * strip_rows, width), BF16)],
    )
    returned = exchange(outgoing, 1)
    returned = returned[1:] + returned[:1]
    (collect,) = call(
        functools.partial(collect_kernel, n, capacity, strips, strip_rows, ring, two),
        [((band, slot_rows), BF16)],
        [outgoing[0], *codes],
        [VMEM] + [VMEM if two else SMEM] * len(codes),
    )
    (stack,) = call(
        sum_kernel,
        [pltpu.HBM((band, width), F32)],
        [collect, *returned],
        [VMEM] * (1 + len(returned)),
        [((band, width), F32), pltpu.SemaphoreType.DMA((2,))],
    )
    difference = jnp.concatenate([diff_edge[:strip_rows], diff_mid, diff_edge[strip_rows:]])
    return difference[None], stack.reshape(template.shape)


def solution(mesh):
    return jax.shard_map(
        body,
        mesh=mesh,
        in_specs=(
            P(("grp", "ccd"), "row", "amp"),
            P(("grp", "ccd"), "row", "amp", None, None, None),
            P(("grp", "ccd"), "row", "amp", None, None),
            P(("grp", "ccd"), "row", "amp", None),
            P(("grp", "ccd"), "row", "amp", None, None),
            P(("grp", "ccd"), "row", "amp", None, None),
            P(("grp", "ccd"), None, None),
        ),
        out_specs=(
            P(("grp", "ccd"), "row", "amp"),
            P(("grp", "ccd"), "row", "amp", None, None, None),
        ),
        check_vma=False,
    )
```

```python
import functools

import jax
import jax.numpy as jnp
import ml_dtypes
import numpy as np
from jax import lax
from jax.experimental import pallas as pl
from jax.experimental.pallas import tpu as pltpu
from jax.sharding import PartitionSpec as P

RADIUS = 9
LANES = 128
HALF_TILE = 64
MARGIN = 16
TAPS = 6
KINDS = 3

F32 = jnp.float32
BF16 = jnp.bfloat16
SMEM = pl.BlockSpec(memory_space=pltpu.SMEM)
VMEM = pl.BlockSpec(memory_space=pltpu.VMEM)
HBM = pl.BlockSpec(memory_space=pltpu.HBM)


def kernel_table():
    support = np.arange(-RADIUS, RADIUS + 1).astype(np.float32)
    narrow = np.exp(-support * support / np.float32(4.5))
    slope = support * np.exp(-support * support / np.float32(12.5))
    broad = np.exp(-support * support / np.float32(40.5))
    table = np.stack([narrow / narrow.sum(), slope / np.abs(slope).sum(), broad / broad.sum()])
    return table.astype(ml_dtypes.bfloat16)


def column_bands():
    table = kernel_table()
    source = np.arange(2 * LANES)[:, None]
    target = np.arange(LANES)[None, :]
    place = source - HALF_TILE - target + RADIUS
    inside = (place >= 0) & (place <= 2 * RADIUS)
    return np.stack(
        [np.where(inside, row[np.clip(place, 0, 2 * RADIUS)], 0) for row in table]
    ).astype(ml_dtypes.bfloat16)


def row_bands(count):
    table = kernel_table()
    source = np.arange(count + 2 * MARGIN)[None, :]
    target = np.arange(count)[:, None]
    place = source - MARGIN - target + RADIUS
    inside = (place >= 0) & (place <= 2 * RADIUS)
    return np.concatenate(
        [np.where(inside, row[np.clip(place, 0, 2 * RADIUS)], 0) for row in table]
    ).astype(ml_dtypes.bfloat16)


def sinc(value):
    turn = jnp.pi * value
    return jnp.where(value == 0.0, 1.0, jnp.sin(turn) / jnp.where(value == 0.0, 1.0, turn))


def lanczos_taps(fraction):
    place = lax.broadcasted_iota(jnp.int32, (8, fraction.shape[1]), 0) - 2
    spread = place.astype(F32) - fraction
    return (sinc(spread) * sinc(spread / 3.0)).astype(BF16).astype(F32)


def in_hbm(value):
    return pltpu.with_memory_space_constraint(value, pltpu.HBM)


def lane_index(rows):
    return lax.broadcasted_iota(jnp.int32, (rows, LANES), 1)


def order_of(n):
    return (1, 3, 2, 0) if n == 4 else (*range(1, n), 0)


def in_order(values):
    return [values[g] for g in order_of(len(values))]


def from_order(values):
    order = order_of(len(values))
    return [values[order.index(g)] for g in range(len(values))]


def matches(code_ref, group, me, strips, capacity):
    found, count = [jnp.int32(0)] * capacity, jnp.int32(0)
    for q in range(strips):
        code = code_ref[group * strips + q] if group is not None else code_ref[q]
        hit = lax.div(code, jnp.int32(strips)) == me
        strip = lax.rem(code, jnp.int32(strips))
        found = [jnp.where(hit & (count == j), strip, f) for j, f in enumerate(found)]
        count = count + hit.astype(jnp.int32)
    return found, count


def slots_of(code_ref, me, strips, capacity, n, ring):
    owners = [lax.div(code_ref[0, q], jnp.int32(strips)) for q in range(strips)]
    slots = []
    for q in range(strips):
        rank = jnp.int32(0)
        for p in range(q):
            rank = rank + (owners[p] == owners[q]).astype(jnp.int32)
        group = lax.rem(owners[q] - me + n, jnp.int32(n)) if ring else owners[q]
        slots.append(group * capacity + rank)
    return slots


def pick_kernel(n, capacity, strips, ring, *refs):
    if ring:
        codes, template, outs = refs[:n], refs[n], refs[n + 1 :]
    else:
        codes, template, outs = [refs[0]] * n, refs[1], refs[2:]
    me = lax.axis_index("ccd")
    for g in range(n):
        found, _ = matches(codes[g], None if ring else g, me, strips, capacity)
        for j in range(capacity):
            if ring:
                outs[g][j] = template[strip_rows_at(found[j], template.shape[0] // strips), :]
            else:
                outs[0][g * capacity + j] = template[strip_rows_at(found[j], template.shape[0] // strips), :]


def two_of(value, owner, strips):
    lane = lax.broadcasted_iota(jnp.int32, value.shape, 1).astype(F32)
    low = (owner * strips).astype(F32)
    hit = (value >= low) & (value < low + strips)
    key = lane * strips + (value - low)
    first = jnp.min(jnp.where(hit, key, 1024.0)).astype(jnp.int32)
    last = jnp.max(jnp.where(hit, key, 0.0)).astype(jnp.int32)
    return lax.rem(first, jnp.int32(strips)), lax.rem(last, jnp.int32(strips))


def strip_rows_at(strip, strip_rows):
    return pl.ds(pl.multiple_of(strip * strip_rows, strip_rows), strip_rows)


def pick_two_kernel(strips, strip_rows, code, template, out):
    for j, strip in enumerate(two_of(code[...].astype(F32), lax.axis_index("ccd"), strips)):
        out[j] = template[strip_rows_at(strip, strip_rows), :]


def load_kernel(source, target, sem):
    copy = pltpu.make_async_copy(source, target, sem)
    copy.start()
    copy.wait()


def turned(base, first, rows):
    return pltpu.roll(jnp.broadcast_to(base, (rows, base.shape[1])), first, 1, stride=1, stride_axis=0)


def base_row(taps, q, start, sign, size):
    lane = lax.broadcasted_iota(jnp.int32, (1, size), 1)
    value = jnp.zeros((1, size), F32)
    for t in range(TAPS):
        at = lax.rem(start + sign * (t - 2) + size, jnp.int32(size))
        value = jnp.where(lane == at, jnp.broadcast_to(taps[t : t + 1, q : q + 1], (1, size)), value)
    return value


def prepare_kernel(n, capacity, strips, strip_rows, tiles, amp_count, ring, two, coefs_in, shifts_in, fractions_in,
                   bands_in, science_in, row_band_in, after, code, *refs):
    del after
    if two:
        own_code, template, own = refs[:3]
        refs = refs[3:]
    de, forward, backward, spread, gather, science, row_band, coefs, shifts, fractions, bands, sems = refs
    pairs = [(fractions_in, fractions), (shifts_in, shifts), (coefs_in, coefs),
             (bands_in, bands), (row_band_in, row_band), (science_in, science)]
    copies = [pltpu.make_async_copy(source, target, sems.at[i]) for i, (source, target) in enumerate(pairs)]
    for copy in copies:
        copy.start()
    for copy in copies[:2]:
        copy.wait()
    taps = [lanczos_taps(fractions[d : d + 1, :]) for d in range(2)]
    me = lax.axis_index("ccd")
    band, slots = strips * strip_rows, n * capacity
    size = slots * strip_rows
    if slots != strips:
        backward[...] = jnp.zeros(backward.shape, BF16)
    forward_lane = lax.broadcasted_iota(jnp.int32, (strip_rows, size), 1)
    backward_lane = lax.broadcasted_iota(jnp.int32, (strip_rows, band), 1)
    for q, slot in enumerate(slots_of(code, me, strips, capacity, n, ring)):
        low, high = slot * strip_rows, q * strip_rows
        value = turned(base_row(taps[0], q, low + shifts[0, q], 1, size), 0, strip_rows)
        value = jnp.where((forward_lane >= low) & (forward_lane < low + strip_rows), value, 0.0)
        forward[high : high + strip_rows, :] = value.astype(BF16)
        value = turned(base_row(taps[0], q, high - shifts[0, q], -1, band), 0, strip_rows)
        value = jnp.where((backward_lane >= high) & (backward_lane < high + strip_rows), value, 0.0)
        backward[strip_rows_at(slot, strip_rows), :] = value.astype(BF16)

    if two:
        for j, strip in enumerate(two_of(own_code[...].astype(F32), me, strips)):
            own[j] = template[strip_rows_at(strip, strip_rows), :]

    rows = 160
    away = lax.broadcasted_iota(jnp.int32, (rows, LANES), 0) - lane_index(rows)
    for out, low, centre, sign in ((spread, 48, HALF_TILE, -1), (gather, 112, LANES, 1)):
        within = (away >= centre - low - 8) & (away <= centre - low + 8)
        end = out.shape[1]
        for q in range(strips):
            start = (low - centre) + sign * shifts[1, q] + LANES
            value = turned(base_row(taps[1], q, start, sign, LANES), 0, rows)
            out[q, 0:low, :] = jnp.zeros((low, LANES), BF16)
            out[q, low : low + rows, :] = jnp.where(within, value, 0.0).astype(BF16)
            out[q, low + rows : end, :] = jnp.zeros((end - low - rows, LANES), BF16)
    for copy in copies[2:4]:
        copy.wait()
    amp = lax.axis_index("amp")
    width = tiles * LANES
    rows = 80
    for half in range(2):
        low = half * LANES + (0 if half else LANES - rows)
        for first in range(KINDS):
            at = (half * KINDS + first) * LANES
            band_rows = [bands[second, low : low + rows, :].astype(F32) for second in range(KINDS)]
            e = sum(band_rows[b] * coefs[2, 0, first * KINDS + b] for b in range(KINDS)).astype(BF16)
            empty = jnp.zeros((LANES - rows, 2 * LANES), BF16)
            begin = at + (0 if half else LANES - rows)
            for tile in range(tiles):
                column = lane_index(1) + (amp * width + tile * LANES)
                px = (column.astype(F32) + 0.5) / (width * amp_count) * 2.0 - 1.0
                weight = [coefs[0, 0, first * KINDS + b] + coefs[1, 0, first * KINDS + b] * px for b in range(KINDS)]
                d = sum(band_rows[b] * weight[b] for b in range(KINDS)).astype(BF16)
                de[tile, begin : begin + rows, 0:LANES] = d
                de[tile, begin : begin + rows, LANES : 2 * LANES] = e
                hollow = at + (rows if half else 0)
                de[tile, hollow : hollow + LANES - rows, :] = empty
    for copy in copies[4:]:
        copy.wait()


def collect_kernel(n, capacity, strips, strip_rows, ring, two, after, *refs):
    del after
    out = refs[-1]
    me = lax.axis_index("ccd")
    size = n * capacity * strip_rows
    lane = lax.broadcasted_iota(jnp.int32, (1, size), 1)
    named = jnp.full(lane.shape, -1, jnp.int32)
    for g in range(n):
        if two:
            found = two_of(refs[g][...].astype(F32), me, strips)
        else:
            found, total = matches(refs[g if ring else 0], None if ring else g, me, strips, capacity)
            found = [jnp.where(total > j, strip, -1) for j, strip in enumerate(found)]
        for j in range(capacity):
            low = (g * capacity + j) * strip_rows
            named = jnp.where((lane >= low) & (lane < low + strip_rows), found[j], named)
    lane = lax.broadcasted_iota(jnp.int32, (strip_rows, size), 1)
    row = lax.broadcasted_iota(jnp.int32, lane.shape, 0)
    same_row = lax.rem(lane, jnp.int32(strip_rows)) == row
    for p in range(strips):
        value = jnp.where(same_row & (named == p), 1.0, 0.0)
        out[p * strip_rows : (p + 1) * strip_rows, :] = value.astype(BF16)


def clear_ends(ref, tiles):
    zero = jnp.zeros((ref.shape[0], LANES), BF16)
    ref[:, 0:LANES] = zero
    ref[:, (tiles + 1) * LANES : (tiles + 2) * LANES] = zero


def stacked(refs):
    parts = [ref[...].reshape(-1, ref.shape[-1]) for ref in refs]
    return jnp.concatenate(parts, axis=0) if len(parts) > 1 else parts[0]


def side_kernel(n, strips, strip_rows, tiles, forward, spread, *refs):
    out = refs[-1]
    pool = stacked(from_order(refs[:n]))
    first = lax.axis_index("amp") == 0
    source = jnp.where(first, pool[:, (tiles - 1) * LANES :], pool[:, 0:LANES])
    rows_done = jnp.dot(forward[...], source, preferred_element_type=F32).astype(BF16)
    lane = lane_index(strip_rows)
    inside = (lane < HALF_TILE) == first
    for q in range(strips):
        rows = slice(q * strip_rows, (q + 1) * strip_rows)
        taps = jnp.where(first, spread[q, 0:LANES, :], spread[q, LANES : 2 * LANES, :])
        value = jnp.dot(rows_done[rows], taps, preferred_element_type=F32)
        out[rows, :] = jnp.where(inside, value, 0.0).astype(BF16)


def warp_kernel(n, strips, strip_rows, tiles, ring, *refs):
    forward, spread = refs[:2]
    count = n if ring else 1
    received, rest = from_order(refs[2 : 2 + count]), refs[2 + count :]
    image, rows_done = rest
    width = tiles * LANES
    clear_ends(rows_done, tiles)
    rows_done[:, LANES : LANES + width] = jnp.dot(
        forward[...], stacked(received), preferred_element_type=F32
    ).astype(BF16)
    lane = lane_index(strip_rows)
    for q in range(strips):
        rows = slice(q * strip_rows, (q + 1) * strip_rows)
        windows = [rows_done[rows, b * LANES : (b + 2) * LANES] for b in range(tiles + 1)]
        result = jnp.dot(jnp.concatenate(windows, axis=0), spread[q], preferred_element_type=F32)
        for b in range(tiles + 1):
            value = result[b * strip_rows : (b + 1) * strip_rows]
            if b == 0:
                value = jnp.where(lane < HALF_TILE, 0.0, value)
            if b == tiles:
                value = jnp.where(lane < HALF_TILE, value, 0.0)
            image[rows, b * LANES : (b + 1) * LANES] = value.astype(BF16)


def joined(ref, rows, left, right, tiles, amp_count):
    amp = lax.axis_index("amp")
    zero = jnp.zeros((), BF16)
    first = ref[rows, 0:LANES] + jnp.where(amp > 0, left, zero)
    last = ref[rows, tiles * LANES :] + jnp.where(amp < amp_count - 1, right, zero)
    return [first] + [ref[rows, b * LANES : (b + 1) * LANES] for b in range(1, tiles)] + [last]


def join_kernel(tiles, amp_count, paired, image, left, right, *outs):
    size = image.shape[0]
    edges = []
    for rows in (slice(0, MARGIN), slice(size - MARGIN, size)):
        parts = joined(image, rows, left[rows, :], right[rows, :], tiles, amp_count)
        edges.append(jnp.concatenate(parts, axis=1))
    if paired:
        edges = [jnp.where(lax.axis_index("row") == 0, edges[1], edges[0])]
    for edge, out in zip(edges, outs):
        out[...] = edge


def row_convolved(bands, parts, across, at, count):
    for low in range(0, len(parts), 2):
        window = jnp.concatenate(parts[low : low + 2], axis=1)
        result = jnp.dot(bands, window, preferred_element_type=F32)
        for b in range(low, min(low + 2, len(parts))):
            for kind in range(KINDS):
                piece = result[kind * count : (kind + 1) * count, (b - low) * LANES : (b - low + 1) * LANES]
                across[at : at + count, (b * KINDS + kind) * LANES : (b * KINDS + kind + 1) * LANES] = piece.astype(BF16)


def columns_returned(lowered, columns, at, gather, strip_rows, tiles):
    rows = slice(at, at + strip_rows)
    windows = [lowered[rows, b * LANES : (b + 3) * LANES] for b in range(tiles)]
    result = jnp.dot(jnp.concatenate(windows, axis=0), gather, preferred_element_type=F32)
    for b in range(tiles):
        columns[rows, b * LANES : (b + 1) * LANES] = result[b * strip_rows : (b + 1) * strip_rows].astype(BF16)


def subtracted(science, across, de, store, count, tiles, place):
    for b in range(tiles):
        acc = jnp.dot(
            across[:, b * KINDS * LANES : (b + 2) * KINDS * LANES], de[b], preferred_element_type=F32
        )
        store(b, science(b) - (acc[:, 0:LANES] + place * acc[:, LANES:]))


def row_place(first, count, band, row_count):
    row = lax.broadcasted_iota(jnp.int32, (count, LANES), 0) + (lax.axis_index("row") * band + first)
    return (row.astype(F32) + 0.5) / (band * row_count) * 2.0 - 1.0


def mid_kernel(strips, strip_rows, tiles, row_count, amp_count, image, left, right, science, de, bands, gather,
               diff, columns, across, lowered):
    band = strips * strip_rows
    count = band - 2 * strip_rows
    rows = slice(strip_rows - MARGIN, band - strip_rows + MARGIN)
    parts = joined(image, rows, left[rows, :], right[rows, :], tiles, amp_count)
    row_convolved(bands[...], parts, across, 0, count)
    clear_ends(lowered, tiles)

    def store(b, value):
        diff[:, b * LANES : (b + 1) * LANES] = value
        lowered[:, (b + 1) * LANES : (b + 2) * LANES] = value.astype(BF16)

    subtracted(
        lambda b: science[strip_rows : strip_rows + count, b * LANES : (b + 1) * LANES],
        across, de, store, count, tiles, row_place(strip_rows, count, band, row_count),
    )
    for q in range(1, strips - 1):
        columns_returned(lowered, columns, (q - 1) * strip_rows, gather[q], strip_rows, tiles)


def edge_kernel(n, capacity, strips, strip_rows, tiles, row_count, amp_count, ring, image, left, right, top, bottom,
                science, de, bands, backward, gather, columns_mid, diff, *rest):
    outs = rest[: n if ring else 1]
    across, lowered, columns = rest[len(outs) :]
    band = strips * strip_rows
    inner = strip_rows + MARGIN
    row = lax.axis_index("row")
    zero = jnp.zeros((), BF16)
    tile = [slice(b * LANES, (b + 1) * LANES) for b in range(tiles + 1)]
    above = [jnp.where(row > 0, top[:, t], zero) for t in tile]
    below = [jnp.where(row < row_count - 1, bottom[:, t], zero) for t in tile]
    first, last = slice(0, inner), slice(band - inner, band)
    upper = joined(image, first, left[first, :], right[first, :], tiles, amp_count)
    lower = joined(image, last, left[last, :], right[last, :], tiles, amp_count)
    row_convolved(bands[...], [jnp.concatenate(p, axis=0) for p in zip(above, upper)], across, 0, strip_rows)
    row_convolved(bands[...], [jnp.concatenate(p, axis=0) for p in zip(lower, below)], across, strip_rows, strip_rows)

    def store(b, value):
        at = slice(b * LANES, (b + 1) * LANES)
        diff[:, at] = value
        lowered[:, (b + 1) * LANES : (b + 2) * LANES] = value.astype(BF16)

    clear_ends(lowered, tiles)

    def edge_science(b):
        at = slice(b * LANES, (b + 1) * LANES)
        return jnp.concatenate([science[0:strip_rows, at], science[band - strip_rows : band, at]], axis=0)

    place = jnp.concatenate([row_place(0, strip_rows, band, row_count),
                             row_place(band - strip_rows, strip_rows, band, row_count)], axis=0)
    subtracted(edge_science, across, de, store, 2 * strip_rows, tiles, place)
    columns_returned(lowered, columns, 0, gather[0], strip_rows, tiles)
    columns_returned(lowered, columns, strip_rows, gather[strips - 1], strip_rows, tiles)
    whole = jnp.concatenate([columns[:strip_rows, :], columns_mid[...], columns[strip_rows:, :]], axis=0)
    result = jnp.dot(backward[...], whole, preferred_element_type=F32).astype(BF16)
    size = capacity * strip_rows * (1 if ring else n)
    for g, out in enumerate(outs):
        out[...] = result[g * size : (g + 1) * size].reshape(out.shape)


def begin_kernel(collect, own, first, out):
    values = stacked([own, first])
    out[...] = jnp.dot(collect[:, 0 : values.shape[0]], values, preferred_element_type=F32)


def end_kernel(begun, collect, *refs):
    *returned, stack, total, sems = refs
    values = stacked(returned)
    copies = []
    half = total.shape[0] // 2
    for i in range(2):
        rows = pl.ds(i * half, half)
        more = jnp.dot(collect[rows, collect.shape[1] - values.shape[0] :], values, preferred_element_type=F32)
        total[rows, :] = begun[rows, :] + more
        copy = pltpu.make_async_copy(total.at[rows], stack.at[rows], sems.at[i])
        copy.start()
        copies.append(copy)
    for copy in copies:
        copy.wait()


def sum_kernel(collect, *refs):
    *returned, stack, total, sems = refs
    values = stacked(returned[-1:] + returned[:-1])
    copies = []
    half = total.shape[0] // 2
    for i in range(2):
        rows = pl.ds(i * half, half)
        total[rows, :] = jnp.dot(collect[rows, :], values, preferred_element_type=F32)
        copy = pltpu.make_async_copy(total.at[rows], stack.at[rows], sems.at[i])
        copy.start()
        copies.append(copy)
    for copy in copies:
        copy.wait()


def body(science, template, owners, patch_strip, shifts, fractions, coefs):
    n = lax.axis_size("ccd")
    row_count = lax.axis_size("row")
    amp_count = lax.axis_size("amp")
    band, width = science.shape[1:]
    strips, strip_rows = template.shape[3:5]
    capacity = max(2, strips // n)
    tiles = width // LANES
    padded = width + LANES
    ring = n <= 4
    two = ring and capacity == 2 and strips == 2 * n
    paired = row_count == 2 and amp_count == 2 and two
    swap = [(0, 1), (1, 0)]
    strip_shape = (capacity, strip_rows, width)

    def call(kernel, out_shape, operands, spaces, scratch=(), megabytes=8):
        shapes = [jax.ShapeDtypeStruct(*s) if isinstance(s, tuple) else s for s in out_shape]
        return pl.pallas_call(
            kernel,
            out_shape=shapes,
            in_specs=list(spaces),
            out_specs=[VMEM if isinstance(s, tuple) else HBM for s in out_shape],
            scratch_shapes=[pltpu.VMEM(*s) if isinstance(s, tuple) else s for s in scratch],
            compiler_params=pltpu.CompilerParams(vmem_limit_bytes=megabytes << 20),
            cost_estimate=pl.CostEstimate(flops=0, bytes_accessed=1 << 20, transcendentals=0),
        )(*operands)

    def turn(value, g):
        return lax.ppermute(value, "ccd", [(i, (i + g) % n) for i in range(n)])

    def exchange(parts, sign):
        if not ring:
            return [lax.all_to_all(parts[0], "ccd", split_axis=0, concat_axis=0, tiled=True)]
        return [parts[0]] + [turn(parts[g], sign * g) for g in range(1, n)]

    code = owners.reshape(1, strips) * strips + patch_strip.reshape(1, strips)
    (template_rows,) = call(
        load_kernel,
        [((band, width), BF16)],
        [in_hbm(template.reshape(band, width))],
        [HBM],
        [pltpu.SemaphoreType.DMA],
    )

    if two:
        codes = exchange([code] * n, 1)
        picked = [
            call(
                functools.partial(pick_two_kernel, strips, strip_rows),
                [(strip_shape, BF16)],
                [other, template_rows],
                [VMEM] * 2,
            )[0]
            for other in codes[1:]
        ]
    elif ring:
        codes = exchange([code.reshape(strips)] * n, 1)
        picked_shapes = [(strip_shape, BF16)] * n
    else:
        codes = [lax.all_gather(code.reshape(strips), "ccd", axis=0, tiled=True)]
        picked_shapes = [((n * capacity, strip_rows, width), BF16)]
    if not two:
        picked = call(
            functools.partial(pick_kernel, n, capacity, strips, ring),
            picked_shapes,
            [*codes, template_rows],
            [SMEM] * len(codes) + [VMEM],
        )
    mid_rows = band - 2 * strip_rows
    mid_bands = jnp.asarray(row_bands(mid_rows))
    slot_rows = n * capacity * strip_rows
    *own, de, forward, backward, spread, gather, science, mid_bands = call(
        functools.partial(prepare_kernel, n, capacity, strips, strip_rows, tiles, amp_count, ring, two),
        ([(strip_shape, BF16)] if two else []) + [
            ((tiles, 2 * KINDS * LANES, 2 * LANES), BF16),
            ((band, slot_rows), BF16),
            ((slot_rows, band), BF16),
            ((strips, 2 * LANES, LANES), BF16),
            ((strips, 3 * LANES, LANES), BF16),
            ((band, width), F32),
            (mid_bands.shape, BF16),
        ],
        [in_hbm(value) for value in (
            coefs.transpose(1, 0, 2), shifts.reshape(2, strips), fractions.reshape(2, strips),
            jnp.asarray(column_bands()), science.reshape(band, width), mid_bands)]
        + [picked[0], code] + ([code, template_rows] if two else []),
        [HBM] * 6 + [VMEM, SMEM] + [VMEM] * (2 if two else 0),
        [pltpu.SMEM((3, 1, 9), F32), pltpu.SMEM((2, strips), jnp.int32),
         ((2, strips), F32), ((KINDS, 2 * LANES, LANES), BF16), pltpu.SemaphoreType.DMA((6,))],
        megabytes=10,
    )
    if two:
        received = in_order(exchange([*own, *picked], -1))
    else:
        received = in_order(exchange(picked, -1))
    image_shape = ((band, padded), BF16)
    if paired:
        (beside,) = call(
            functools.partial(side_kernel, n, strips, strip_rows, tiles),
            [((band, LANES), BF16)],
            [forward, spread, *received],
            [VMEM] * (2 + n),
        )
        left = right = lax.ppermute(beside, "amp", swap)
    (image,) = call(
        functools.partial(warp_kernel, n, strips, strip_rows, tiles, ring),
        [image_shape],
        [forward, spread, *received],
        [VMEM] * (2 + len(received)),
        [((band, padded + LANES), BF16)],
    )
    edge_shape = ((MARGIN, padded), BF16)
    join = functools.partial(join_kernel, tiles, amp_count, paired)
    if paired:
        (edge,) = call(join, [edge_shape], [image, left, right], [VMEM] * 3)
        top = bottom = lax.ppermute(edge, "row", swap)
    else:

        def moved(value, axis, step):
            count = lax.axis_size(axis)
            return lax.ppermute(value, axis, [(i, i + step) for i in range(count) if 0 <= i + step < count])

        left, right = moved(image[:, padded - LANES :], "amp", 1), moved(image[:, :LANES], "amp", -1)
        first, last = call(join, [edge_shape] * 2, [image, left, right], [VMEM] * 3)
        top, bottom = moved(last, "row", 1), moved(first, "row", -1)

    diff_mid, columns_mid = call(
        functools.partial(mid_kernel, strips, strip_rows, tiles, row_count, amp_count),
        [((mid_rows, width), F32), ((mid_rows, width), BF16)],
        [image, left, right, science, de, mid_bands, gather],
        [VMEM] * 7,
        [((mid_rows, (tiles + 1) * KINDS * LANES), BF16), ((mid_rows, padded + LANES), BF16)],
    )
    outgoing_shapes = [(strip_shape, BF16)] * n if ring else [((n * capacity, strip_rows, width), BF16)]
    diff_edge, *outgoing = call(
        functools.partial(edge_kernel, n, capacity, strips, strip_rows, tiles, row_count, amp_count, ring),
        [((2 * strip_rows, width), F32)] + outgoing_shapes,
        [image, left, right, top, bottom, science, de, jnp.asarray(row_bands(strip_rows)), backward, gather,
         columns_mid],
        [VMEM] * 11,
        [((2 * strip_rows, (tiles + 1) * KINDS * LANES), BF16), ((2 * strip_rows, padded + LANES), BF16),
         ((2 * strip_rows, width), BF16)],
    )
    returned = exchange(outgoing, 1)
    returned = returned[1:] + returned[:1]
    (collect,) = call(
        functools.partial(collect_kernel, n, capacity, strips, strip_rows, ring, two),
        [((band, slot_rows), BF16)],
        [outgoing[0], *codes],
        [VMEM] + [VMEM if two else SMEM] * len(codes),
    )
    if two:
        (begun,) = call(begin_kernel, [((band, width), F32)], [collect, returned[-1], returned[0]], [VMEM] * 3)
        (stack,) = call(
            end_kernel,
            [pltpu.HBM((band, width), F32)],
            [begun, collect, *returned[1:-1]],
            [VMEM] * n,
            [((band, width), F32), pltpu.SemaphoreType.DMA((2,))],
        )
    else:
        (stack,) = call(
            sum_kernel,
            [pltpu.HBM((band, width), F32)],
            [collect, *returned],
            [VMEM] * (1 + len(returned)),
            [((band, width), F32), pltpu.SemaphoreType.DMA((2,))],
        )
    difference = jnp.concatenate([diff_edge[:strip_rows], diff_mid, diff_edge[strip_rows:]])
    return difference[None], stack.reshape(template.shape)


def solution(mesh):
    return jax.shard_map(
        body,
        mesh=mesh,
        in_specs=(
            P(("grp", "ccd"), "row", "amp"),
            P(("grp", "ccd"), "row", "amp", None, None, None),
            P(("grp", "ccd"), "row", "amp", None, None),
            P(("grp", "ccd"), "row", "amp", None),
            P(("grp", "ccd"), "row", "amp", None, None),
            P(("grp", "ccd"), "row", "amp", None, None),
            P(("grp", "ccd"), None, None),
        ),
        out_specs=(
            P(("grp", "ccd"), "row", "amp"),
            P(("grp", "ccd"), "row", "amp", None, None, None),
        ),
        check_vma=False,
    )
```
